32 devices in a mesh: seq: 8 (over z, x), tp: 4 (over y, core).
Axes of the slice: x: 2, y: 2, z: 4, core: 2. Of those that a mesh axis runs over, the one named last changes fastest.
Arguments:
- token_inputs: bfloat16 [4, 64, 5120], P(None, 'seq'), may hold values from -6 to 6
- attn_gain: float32 [5120], replicated, may hold values from 0.1 to 1.9
- w_query: bfloat16 [5120, 4096], P(None, 'tp'), may hold values from -0.078125 to 0.078125
- key_projection: bfloat16 [5120, 1024], P(None, 'tp'), may hold values from -0.078125 to 0.078125
- value_projection: bfloat16 [5120, 1024], P(None, 'tp'), may hold values from -0.078125 to 0.078125
- w_output: bfloat16 [4096, 5120], P('tp'), may hold values from -0.09375 to 0.09375
- mlp_gain: float32 [5120], replicated, may hold values from 0.1 to 1.9
- w_gate: bfloat16 [5120, 32768], P(None, ('seq', 'tp')), may hold values from -0.078125 to 0.078125
- w_up: bfloat16 [5120, 32768], P(None, ('seq', 'tp')), may hold values from -0.078125 to 0.078125
- w_down: bfloat16 [32768, 5120], P(('seq', 'tp')), may hold values from -0.03125 to 0.03125
- key_cache: bfloat16 [288, 8, 256, 128], P('seq', 'tp'), may hold values from -300 to 300
- paged_value_cache: bfloat16 [288, 8, 256, 128], P('seq', 'tp'), may hold values from -6 to 6
- cache_lengths: int32 [64], replicated, may hold values from 1 to 32768, as said below
- page_request: int32 [288], P('seq'), may hold values from -1 to 63, as said below
- page_number: int32 [288], P('seq'), may hold values from 0 to 127, as said below
- request_slot: int32 [64], replicated, may hold values from 0 to 63, each once
Outputs:
- attended: bfloat16 [4, 64, 5120], P(None, 'seq')
- layer_out: bfloat16 [4, 64, 5120], P(None, 'seq')
The draws below stay inside these ranges and needn't reach their ends.
Inputs may be any that keep to these rules, and one draw needn't show every extreme that they name: `cache_lengths`: one request holds exactly 32768 positions. `page_request`: the pages of request r that hold its positions are numbered 0 to ceil(cache_lengths[r] / 256) - 1, and each of them is held by exactly one pool page; every other pool page is free (-1), and some page is free. `page_number`: 0 on free pages.
All inputs are finite; a program needn't handle non-finite values.
Results may differ from the reference program's by a relative error of at most 0.012.
Values may be sent and summed in bfloat16 or wider, within the bound.
No kernel may reach another device: no remote copies, remote signals or barrier semaphores. Data moves between devices by JAX's collectives and lax.ppermute only.
A program may use at most 128 MiB of HBM per device.

```python
import jax
import jax.numpy as jnp
from jax import lax

MODEL_WIDTH = 5120
QUERY_HEADS = 32
KEY_VALUE_HEADS = 8
HEAD_SIZE = 128
FF = 32768
STEPS = 4
PAGE_POSITIONS = 256
MAXPAGES = 128
REQUEST_COUNT = 64
POOL_PAGES = 288


def page_layout(key):
    layout_key = jax.random.fold_in(key, 23)
    key_big, key_pages, key_tails, key_order = jax.random.split(layout_key, 4)
    request_ids = jnp.arange(REQUEST_COUNT, dtype=jnp.int32)
    biggest = jax.random.randint(key_big, (), 0, REQUEST_COUNT)
    other_most = (POOL_PAGES - MAXPAGES - 1) // (REQUEST_COUNT - 1)
    page_counts = jax.random.randint(key_pages, (REQUEST_COUNT,), 1, other_most + 1)
    page_counts = jnp.where(request_ids == biggest, MAXPAGES, page_counts).astype(jnp.int32)
    tail_tokens = jax.random.randint(key_tails, (REQUEST_COUNT,), 1, PAGE_POSITIONS + 1)
    tail_tokens = jnp.where(request_ids == biggest, PAGE_POSITIONS, tail_tokens).astype(jnp.int32)
    lengths = (page_counts - 1) * PAGE_POSITIONS + tail_tokens
    pool_order = jax.random.permutation(key_order, REQUEST_COUNT)
    ordered_counts = page_counts[pool_order]
    ordered_starts = (jnp.cumsum(ordered_counts) - ordered_counts).astype(jnp.int32)
    starts = jnp.zeros((REQUEST_COUNT,), jnp.int32).at[pool_order].set(ordered_starts)
    pool_slots = jnp.arange(POOL_PAGES, dtype=jnp.int32)
    inside = (pool_slots[:, None] >= starts[None, :]) & (pool_slots[:, None] < (starts + page_counts)[None, :])
    page_owner = jnp.where(jnp.any(inside, axis=1), jnp.sum(jnp.where(inside, request_ids[None, :], 0), axis=1), -1)
    number = jnp.where(page_owner >= 0, pool_slots - starts[jnp.maximum(page_owner, 0)], 0)
    return (lengths.astype(jnp.int32), page_owner.astype(jnp.int32), number.astype(jnp.int32))


def draw_cache_lengths(key, part):
    return page_layout(key)[0]


def draw_page_request(key, part):
    return page_layout(key)[1]


def draw_page_number(key, part):
    return page_layout(key)[2]


def draw_key_cache(key, part):
    noise_key = jax.random.fold_in(jax.random.fold_in(key, 5), 0)
    array_shape = (POOL_PAGES, KEY_VALUE_HEADS, PAGE_POSITIONS, HEAD_SIZE)
    result = jax.random.truncated_normal(noise_key, -6.0, 6.0, array_shape, jnp.float32)
    return result.astype(jnp.bfloat16)


def shard_levels(own_key, dims, pieces, low, top_value):
    def one(axis_at, shards_of):
        steps = jax.random.uniform(jax.random.fold_in(jax.random.fold_in(own_key, 6), axis_at), (shards_of,), jnp.float32, low / len(pieces), top_value / len(pieces))
        return jnp.repeat(jnp.exp(steps), dims[axis_at] // shards_of).reshape((-1,) + (1,) * (len(dims) - axis_at - 1))

    factor_of = one(*pieces[0])
    for cut in pieces[1:]:
        factor_of = factor_of * one(*cut)
    return factor_of


def gaussian(key, shape, width, reach, shards=(), held_as=jnp.bfloat16):
    array = width * jax.random.normal(key, shape, jnp.float32)
    if shards:
        array = array * shard_levels(key, shape, shards, -0.22, 0.18)
    return jnp.clip(array, -reach, reach).astype(held_as)


def setup_inputs(seed: int = 0) -> dict:
    arg_keys = jax.random.split(jax.random.key(seed), 17)
    token_inputs = gaussian(arg_keys[0], (STEPS, REQUEST_COUNT, MODEL_WIDTH), 1.0, 6.0, ((1, 8),))
    attn_gain = jnp.clip(1.0 + 0.18 * jax.random.normal(arg_keys[1], (MODEL_WIDTH,), jnp.float32), 0.1, 1.9)
    w_query = gaussian(arg_keys[2], (MODEL_WIDTH, QUERY_HEADS * HEAD_SIZE), MODEL_WIDTH ** -0.5, 0.078125, ((1, 4),))
    key_projection = gaussian(arg_keys[3], (MODEL_WIDTH, KEY_VALUE_HEADS * HEAD_SIZE), MODEL_WIDTH ** -0.5, 0.078125, ((1, 4),))
    value_projection = gaussian(arg_keys[4], (MODEL_WIDTH, KEY_VALUE_HEADS * HEAD_SIZE), MODEL_WIDTH ** -0.5, 0.078125, ((1, 4),))
    w_output = gaussian(arg_keys[5], (QUERY_HEADS * HEAD_SIZE, MODEL_WIDTH), (QUERY_HEADS * HEAD_SIZE) ** -0.5, 0.09375, ((0, 4),))
    mlp_gain = jnp.clip(1.0 + 0.18 * jax.random.normal(arg_keys[6], (MODEL_WIDTH,), jnp.float32), 0.1, 1.9)
    w_gate = gaussian(arg_keys[7], (MODEL_WIDTH, FF), MODEL_WIDTH ** -0.5, 0.078125, ((1, 32),))
    w_up = gaussian(arg_keys[8], (MODEL_WIDTH, FF), MODEL_WIDTH ** -0.5, 0.078125, ((1, 32),))
    w_down = gaussian(arg_keys[9], (FF, MODEL_WIDTH), FF ** -0.5, 0.03125, ((0, 32),))
    key_cache = draw_key_cache(jax.random.fold_in(arg_keys[16], 71), 0)
    paged_value_cache = gaussian(arg_keys[11], (POOL_PAGES, KEY_VALUE_HEADS, PAGE_POSITIONS, HEAD_SIZE), 1.0, 6.0, ((0, 8), (1, 4)))
    cache_lengths = draw_cache_lengths(jax.random.fold_in(arg_keys[16], 71), 0)
    page_request = draw_page_request(jax.random.fold_in(arg_keys[16], 71), 0)
    page_number = draw_page_number(jax.random.fold_in(arg_keys[16], 71), 0)
    request_slot = jax.random.permutation(arg_keys[15], REQUEST_COUNT).astype(jnp.int32)
    return {"token_inputs": token_inputs, "attn_gain": attn_gain, "w_query": w_query, "key_projection": key_projection, "value_projection": value_projection, "w_output": w_output, "mlp_gain": mlp_gain, "w_gate": w_gate, "w_up": w_up, "w_down": w_down, "key_cache": key_cache, "paged_value_cache": paged_value_cache, "cache_lengths": cache_lengths, "page_request": page_request, "page_number": page_number, "request_slot": request_slot}


rope_theta = 100000000.0
norm_eps = 1e-05
masked_low = -1e+30

def rms_norm(values, gain):
    floats = values.astype(jnp.float32)
    square_mean = lax.optimization_barrier(jnp.mean(floats * floats, axis=-1, keepdims=True))
    return floats * lax.rsqrt(square_mean + norm_eps) * gain

def apply_rotary(values, token_position):
    half_dim = values.shape[-1] // 2
    exponent = jnp.arange(half_dim, dtype=jnp.float32) * (2.0 / values.shape[-1])
    inverse_freq = rope_theta ** (-exponent)
    angles = token_position.astype(jnp.float32)[:, None] * inverse_freq[None, :]
    angles = angles[:, None, :]
    cosine = jnp.cos(angles)
    sine_part = jnp.sin(angles)
    first_half = values[..., :half_dim]
    second_half = values[..., half_dim:]
    return jnp.concatenate([first_half * cosine - second_half * sine_part, second_half * cosine + first_half * sine_part], axis=-1)

def cache_part(query_head_rows, key_cache, paged_value_cache, page_req, token_mask, page_live):
    request_ids = jnp.arange(REQUEST_COUNT, dtype=jnp.int32)

    def per_head(operands):
        keys_head, values_head, query_head = operands
        page_query = query_head[page_req].astype(jnp.float32)
        scores = jnp.einsum('pgd,ptd->pgt', page_query, keys_head.astype(jnp.float32)) * HEAD_SIZE ** (-0.5)
        scores = jnp.where(token_mask[:, None, :], scores, masked_low)
        page_max = lax.optimization_barrier(jnp.max(scores, axis=-1))
        weights = jnp.where(token_mask[:, None, :], jnp.exp(scores - page_max[..., None]), 0.0)
        page_sum = lax.optimization_barrier(jnp.sum(weights, axis=-1))
        rounded = lax.optimization_barrier(weights.astype(jnp.bfloat16))
        page_acc = jnp.einsum('pgt,ptd->pgd', rounded.astype(jnp.float32), values_head.astype(jnp.float32))
        page_owner = (page_req[None, :] == request_ids[:, None]) & page_live[None, :]
        req_max = lax.optimization_barrier(jnp.max(jnp.where(page_owner[:, :, None], page_max[None], masked_low), axis=1))
        factor = jnp.exp(page_max - req_max[page_req])
        onehot = page_owner.astype(jnp.float32)
        req_sum = jnp.einsum('rp,pg->rg', onehot, page_sum * factor, precision=lax.Precision.HIGHEST)
        req_acc = jnp.einsum('rp,pgd->rgd', onehot, page_acc * factor[..., None], precision=lax.Precision.HIGHEST)
        return (req_max, req_sum, req_acc)
    head_max, head_sum, head_acc = lax.map(per_head, (jnp.swapaxes(key_cache, 0, 1), jnp.swapaxes(paged_value_cache, 0, 1), jnp.swapaxes(query_head_rows, 0, 1)))
    return (jnp.swapaxes(head_max, 0, 1), jnp.swapaxes(head_sum, 0, 1), jnp.swapaxes(head_acc, 0, 1))

def reference(token_inputs, attn_gain, w_query, key_projection, value_projection, w_output, mlp_gain, w_gate, w_up, w_down, key_cache, paged_value_cache, cache_lengths, page_request, page_number, request_slot):
    heads_per_group = QUERY_HEADS // KEY_VALUE_HEADS
    inverse_slot = jnp.zeros((REQUEST_COUNT,), jnp.int32).at[request_slot].set(jnp.arange(REQUEST_COUNT, dtype=jnp.int32))
    page_live = page_request >= 0
    page_req = jnp.where(page_live, page_request, 0).astype(jnp.int32)
    token_pos = page_number[:, None] * PAGE_POSITIONS + jnp.arange(PAGE_POSITIONS, dtype=jnp.int32)[None, :]
    token_mask = page_live[:, None] & (token_pos < cache_lengths[page_req][:, None])
    recent_keys = []
    recent_values = []
    attended_list = []
    output_list = []
    for step_index in range(STEPS):
        hidden_in = token_inputs[step_index][request_slot]
        token_position = cache_lengths + step_index
        normalized_input = rms_norm(hidden_in, attn_gain).astype(jnp.bfloat16)
        query_head_rows = apply_rotary(jnp.dot(normalized_input, w_query, preferred_element_type=jnp.float32).reshape(REQUEST_COUNT, QUERY_HEADS, HEAD_SIZE), token_position)
        query_head_rows = query_head_rows.astype(jnp.bfloat16).reshape(REQUEST_COUNT, KEY_VALUE_HEADS, heads_per_group, HEAD_SIZE)
        fresh_key = apply_rotary(jnp.dot(normalized_input, key_projection, preferred_element_type=jnp.float32).reshape(REQUEST_COUNT, KEY_VALUE_HEADS, HEAD_SIZE), token_position).astype(jnp.bfloat16)
        fresh_value = jnp.dot(normalized_input, value_projection, preferred_element_type=jnp.float32).astype(jnp.bfloat16).reshape(REQUEST_COUNT, KEY_VALUE_HEADS, HEAD_SIZE)
        recent_keys.append(fresh_key)
        recent_values.append(fresh_value)
        cache_max, cache_sum, cache_acc = cache_part(query_head_rows, key_cache, paged_value_cache, page_req, token_mask, page_live)
        stacked_keys = jnp.stack(recent_keys).astype(jnp.float32)
        stacked_values = jnp.stack(recent_values).astype(jnp.float32)
        recent_scores = jnp.einsum('rkgd,jrkd->rkgj', query_head_rows.astype(jnp.float32), stacked_keys) * HEAD_SIZE ** (-0.5)
        recent_max = lax.optimization_barrier(jnp.max(recent_scores, axis=-1))
        recent_weights = jnp.exp(recent_scores - recent_max[..., None])
        recent_sum = lax.optimization_barrier(jnp.sum(recent_weights, axis=-1))
        rounded = lax.optimization_barrier(recent_weights.astype(jnp.bfloat16))
        recent_acc = jnp.einsum('rkgj,jrkd->rkgd', rounded.astype(jnp.float32), stacked_values)
        total_max = jnp.maximum(cache_max, recent_max)
        cache_factor = jnp.exp(cache_max - total_max)
        recent_factor = jnp.exp(recent_max - total_max)
        total_sum = cache_sum * cache_factor + recent_sum * recent_factor
        total_acc = cache_acc * cache_factor[..., None] + recent_acc * recent_factor[..., None]
        attention = (total_acc / total_sum[..., None]).astype(jnp.bfloat16).reshape(REQUEST_COUNT, QUERY_HEADS * HEAD_SIZE)
        attended = (hidden_in.astype(jnp.float32) + jnp.dot(attention, w_output, preferred_element_type=jnp.float32)).astype(jnp.bfloat16)
        normed_mlp = rms_norm(attended, mlp_gain).astype(jnp.bfloat16)
        gate_proj = jnp.dot(normed_mlp, w_gate, preferred_element_type=jnp.float32)
        up_proj = jnp.dot(normed_mlp, w_up, preferred_element_type=jnp.float32)
        activation = (jax.nn.silu(gate_proj) * up_proj).astype(jnp.bfloat16)
        layer_out = (attended.astype(jnp.float32) + jnp.dot(activation, w_down, preferred_element_type=jnp.float32)).astype(jnp.bfloat16)
        attended_list.append(attended[inverse_slot])
        output_list.append(layer_out[inverse_slot])
    return (jnp.stack(attended_list), jnp.stack(output_list))
```

```python
import functools

import jax
import jax.numpy as jnp
from jax import lax
from jax.experimental import pallas as pl
from jax.experimental.pallas import tpu as pltpu
from jax.sharding import PartitionSpec as P

STEPS = 4
CORES = 2

rope_theta = 100000000.0
norm_eps = 1e-05
masked_low = -1e30
f32 = jnp.float32
bf16 = jnp.bfloat16


def split_axis(size):
    fast = 1
    while fast * fast * 4 <= size:
        fast *= 2
    return size // fast, fast


def swap(value, axis, mask):
    size = lax.axis_size(axis)
    return lax.ppermute(value, axis, [(i, i ^ mask) for i in range(size)])


def rms_norm(values, gain):
    floats = values.astype(f32)
    square_mean = jnp.mean(floats * floats, axis=-1, keepdims=True)
    return floats * lax.rsqrt(square_mean + norm_eps) * gain


def rotary_tables(token_position, head_dim):
    half_dim = head_dim // 2
    exponent = jnp.arange(half_dim, dtype=f32) * (2.0 / head_dim)
    inverse_freq = rope_theta ** (-exponent)
    angles = token_position.astype(f32)[:, None] * inverse_freq[None, :]
    return jnp.cos(angles)[:, None, :], jnp.sin(angles)[:, None, :]


def apply_rotary(values, cosine, sine):
    half_dim = values.shape[-1] // 2
    first_half = values[..., :half_dim]
    second_half = values[..., half_dim:]
    return jnp.concatenate(
        [first_half * cosine - second_half * sine, second_half * cosine + first_half * sine],
        axis=-1,
    )


def dot_t(a, b):
    return lax.dot_general(a, b, (((1,), (1,)), ((), ())), preferred_element_type=f32)


def round_trip(value):
    return value.astype(bf16).astype(f32)


def encode_stats(top, total, pairs):
    pieces = []
    rest = top
    for _ in range(3):
        piece = round_trip(rest)
        pieces.append(piece)
        rest = rest - piece
    rest = total
    for _ in range(2):
        piece = round_trip(rest)
        pieces.append(piece)
        rest = rest - piece
    tile = pieces[0]
    for i in range(1, 5):
        tile = tile + pltpu.roll(pieces[i], i * pairs, 1)
    return tile.astype(bf16)


def decode_stats(tile, pairs):
    values = tile.astype(f32)
    lanes = values.shape[1]
    shifted = [values] + [pltpu.roll(values, lanes - i * pairs, 1) for i in range(1, 5)]
    top = shifted[0] + shifted[1] + shifted[2]
    total = shifted[3] + shifted[4]
    return top, total


def pages_kernel(
    block_pages, slot_ref, valid_ref, query_ref, fresh_key_ref, fresh_value_ref, key_hbm, value_hbm,
    out_ref, key_buf, value_buf, top_ref, total_ref, acc_ref, sems,
):
    page_count, kv_local, page_size, head_dim = key_buf.shape
    blocks = page_count // block_pages
    groups, tiles = out_ref.shape[:2]
    pairs = tiles - 1
    rows = query_ref.shape[1]
    per_step = rows // STEPS
    scale = head_dim ** (-0.5)

    def copies(block):
        at = pl.ds(block * block_pages, block_pages)
        return (
            pltpu.make_async_copy(key_hbm.at[at], key_buf.at[at], sems.at[0, block]),
            pltpu.make_async_copy(value_hbm.at[at], value_buf.at[at], sems.at[1, block]),
        )

    for block in range(blocks):
        for copy in copies(block):
            copy.start()

    top_ref[...] = jnp.full(top_ref.shape, masked_low, f32)
    total_ref[...] = jnp.zeros(total_ref.shape, f32)
    acc_ref[...] = jnp.zeros(acc_ref.shape, f32)

    fresh = fresh_key_ref.shape[1]
    row_step = lax.broadcasted_iota(jnp.int32, (rows, fresh), 0) // per_step
    column = lax.broadcasted_iota(jnp.int32, (rows, fresh), 1)
    earlier = column <= row_step
    for i in range(pairs):
        scores = dot_t(query_ref[i], fresh_key_ref[i]) * scale
        scores = jnp.where(earlier, scores, masked_low)
        top = jnp.max(scores, axis=1, keepdims=True)
        weights = jnp.where(earlier, jnp.exp(scores - top), 0.0)
        top_ref[i] = jnp.broadcast_to(top, (rows, head_dim))
        total_ref[i] = jnp.broadcast_to(jnp.sum(weights, axis=1, keepdims=True), (rows, head_dim))
        acc_ref[i] = jnp.dot(weights.astype(bf16), fresh_value_ref[i], preferred_element_type=f32)

    lane = lax.broadcasted_iota(jnp.int32, (rows, page_size), 1)

    @pl.loop(0, blocks)
    def _(block):
        for copy in copies(block):
            copy.wait()
        found = []
        for i in range(block_pages):
            page = block * block_pages + i
            slot = slot_ref[page]
            live = lane < valid_ref[page]
            for head in range(kv_local):
                at = slot * kv_local + head
                scores = dot_t(query_ref[at], key_buf[page, head]) * scale
                scores = jnp.where(live, scores, masked_low)
                top = jnp.max(scores, axis=1, keepdims=True)
                weights = jnp.where(live, jnp.exp(scores - top), 0.0)
                total = jnp.sum(weights, axis=1, keepdims=True)
                acc = jnp.dot(weights.astype(bf16), value_buf[page, head], preferred_element_type=f32)
                found.append((at, top, total, acc))
        for at, top, total, acc in found:
            old_top = top_ref[at]
            new_top = jnp.maximum(old_top, top)
            old_factor = jnp.exp(old_top - new_top)
            factor = jnp.exp(top - new_top)
            top_ref[at] = new_top
            total_ref[at] = total_ref[at] * old_factor + total * factor
            acc_ref[at] = acc_ref[at] * old_factor + acc * factor

    out_lane = lax.broadcasted_iota(jnp.int32, (rows, head_dim), 1)

    @pl.loop(0, groups)
    def _(group):
        tops = jnp.zeros((rows, head_dim), f32)
        totals = jnp.zeros((rows, head_dim), f32)
        for i in range(pairs):
            at = group * pairs + i
            out_ref[group, i] = acc_ref[at].astype(bf16)
            tops = jnp.where(out_lane == i, top_ref[at], tops)
            totals = jnp.where(out_lane == i, total_ref[at], totals)
        out_ref[group, pairs] = encode_stats(tops, totals, pairs)


def attend_pages(queries, fresh_keys, fresh_values, key_cache, value_cache, slots, valid, groups):
    pairs = fresh_keys.shape[0]
    rows, head_dim = queries.shape[1:]
    page_count, kv_local, page_size, _ = key_cache.shape
    block_pages = 4
    while page_count % block_pages:
        block_pages -= 1
    blocks = page_count // block_pages
    count = queries.shape[0]
    vmem = pl.BlockSpec(memory_space=pltpu.VMEM)
    smem = pl.BlockSpec(memory_space=pltpu.SMEM)
    hbm = pl.BlockSpec(memory_space=pl.ANY)
    return pl.pallas_call(
        functools.partial(pages_kernel, block_pages),
        out_shape=jax.ShapeDtypeStruct((groups, pairs + 1, rows, head_dim), bf16),
        in_specs=[smem, smem, vmem, vmem, vmem, hbm, hbm],
        out_specs=vmem,
        scratch_shapes=[
            pltpu.VMEM(key_cache.shape, bf16),
            pltpu.VMEM(value_cache.shape, bf16),
            pltpu.VMEM((count, rows, head_dim), f32),
            pltpu.VMEM((count, rows, head_dim), f32),
            pltpu.VMEM((count, rows, head_dim), f32),
            pltpu.SemaphoreType.DMA((2, blocks)),
        ],
        compiler_params=pltpu.CompilerParams(vmem_limit_bytes=32 << 20),
        cost_estimate=pl.CostEstimate(
            flops=4 * rows * page_count * kv_local * page_size * head_dim,
            bytes_accessed=4 * page_count * kv_local * page_size * head_dim,
            transcendentals=0,
        ),
        name="attend_pages",
    )(slots, valid, queries, fresh_keys, fresh_values, key_cache, value_cache)


def merge_kernel(final, count, *refs):
    parts, out_ref = refs[:count], refs[count]
    groups, tiles, rows, head_dim = parts[0].shape
    pairs = tiles - 1
    scratch = refs[count + 1] if final else None
    for group in range(groups):
        stats = [decode_stats(part[group, pairs], pairs) for part in parts]
        top = functools.reduce(jnp.maximum, [s[0] for s in stats])
        factors = [jnp.exp(s[0] - top) for s in stats]
        total = functools.reduce(jnp.add, [s[1] * f for s, f in zip(stats, factors)])
        if final:
            inverse = 1.0 / total
            factors = [f * inverse for f in factors]
        for i in range(pairs):
            acc = functools.reduce(
                jnp.add,
                [part[group, i].astype(f32) * f[:, i : i + 1] for part, f in zip(parts, factors)],
            )
            if not final:
                out_ref[group, i] = acc.astype(bf16)
                continue
            kv_local = scratch.shape[1] // (rows // STEPS * head_dim)
            request, head = i // kv_local, i % kv_local
            per_step = rows // STEPS
            local_rows = pairs // kv_local
            for row in range(rows):
                step, member = row // per_step, row % per_step
                column = (head * per_step + member) * head_dim
                scratch[step * local_rows + request, column : column + head_dim] = acc[row]
        if not final:
            lane = lax.broadcasted_iota(jnp.int32, (rows, head_dim), 1)
            used = lane < pairs
            out_ref[group, pairs] = encode_stats(
                jnp.where(used, top, 0.0), jnp.where(used, total, 0.0), pairs
            )
    if final:
        out_ref[...] = scratch[...].astype(bf16)


def merge_parts(parts, out_shape=None):
    final = out_shape is not None
    vmem = pl.BlockSpec(memory_space=pltpu.VMEM)
    return pl.pallas_call(
        functools.partial(merge_kernel, final, len(parts)),
        out_shape=jax.ShapeDtypeStruct(out_shape if final else parts[0].shape, bf16),
        in_specs=[vmem] * len(parts),
        out_specs=vmem,
        scratch_shapes=[pltpu.VMEM(out_shape, f32)] if final else [],
        name="merge_parts",
    )(*parts)


def local(
    token_inputs,
    attn_gain,
    w_query,
    key_projection,
    value_projection,
    w_output,
    mlp_gain,
    w_gate,
    w_up,
    w_down,
    key_cache,
    paged_value_cache,
    cache_lengths,
    page_request,
    page_number,
    request_slot,
):
    steps, row_count, width = token_inputs.shape
    seq, tp = lax.axis_size("seq"), lax.axis_size("tp")
    deep, across = split_axis(seq)
    ways, cores = tp // CORES, CORES
    page_count, kv_local, page_size, head_dim = key_cache.shape
    heads_per_group = w_query.shape[1] // (kv_local * head_dim)
    rows = steps * row_count
    pairs = row_count * kv_local
    me, part = lax.axis_index("seq"), lax.axis_index("tp")
    quarter = width // tp

    own_rows = me * row_count + jnp.arange(row_count, dtype=jnp.int32)
    row_lengths = jnp.sum(
        jnp.where(request_slot[None, :] == own_rows[:, None], cache_lengths[None, :], 0), axis=1
    )
    page_live = page_request >= 0
    request_ids = jnp.arange(request_slot.shape[0], dtype=jnp.int32)
    is_request = request_ids[None, :] == page_request[:, None]
    page_row = jnp.sum(jnp.where(is_request, request_slot[None, :], 0), axis=1)
    page_length = jnp.sum(jnp.where(is_request, cache_lengths[None, :], 0), axis=1)
    valid = jnp.where(page_live, jnp.clip(page_length - page_number * page_size, 0, page_size), 0)
    mask = (page_row // row_count) ^ me
    slots = ((mask % across) * deep + mask // across) * row_count + page_row % row_count

    positions = (row_lengths[None, :] + jnp.arange(steps, dtype=jnp.int32)[:, None]).reshape(rows)
    cosine, sine = rotary_tables(positions, head_dim)
    normalized = rms_norm(token_inputs, attn_gain).astype(bf16).reshape(rows, width)
    query = apply_rotary(
        jnp.dot(normalized, w_query, preferred_element_type=f32).reshape(rows, -1, head_dim), cosine, sine
    ).astype(bf16)
    query = query.reshape(steps, row_count, kv_local, heads_per_group, head_dim)
    query = query.transpose(1, 2, 0, 3, 4).reshape(pairs, steps * heads_per_group, head_dim)

    shared = [query] + [swap(query, "seq", across * k) for k in range(1, deep)]
    shared = jnp.concatenate(shared, axis=0)
    queries = [shared] + [swap(shared, "seq", k) for k in range(1, across)]
    queries = jnp.concatenate(queries, axis=0)

    fresh_key = apply_rotary(
        jnp.dot(normalized, key_projection, preferred_element_type=f32).reshape(rows, -1, head_dim),
        cosine,
        sine,
    ).astype(bf16)
    fresh_value = jnp.dot(normalized, value_projection, preferred_element_type=f32).astype(bf16)

    def fresh_tiles(value):
        value = value.reshape(steps, row_count, kv_local, head_dim).transpose(1, 2, 0, 3)
        value = value.reshape(pairs, steps, head_dim)
        return jnp.pad(value, ((0, 0), (0, 16 - steps), (0, 0)))

    packed = attend_pages(
        queries,
        fresh_tiles(fresh_key),
        fresh_tiles(fresh_value),
        key_cache,
        paged_value_cache,
        slots,
        valid,
        seq,
    )
    sides = [packed[:deep]] + [swap(packed[k * deep : (k + 1) * deep], "seq", k) for k in range(1, across)]
    merged = merge_parts(sides)
    layers = [merged[:1]] + [swap(merged[k : k + 1], "seq", across * k) for k in range(1, deep)]
    attention = merge_parts(layers, (rows, kv_local * heads_per_group * head_dim))

    head_part = jnp.dot(attention, w_output, preferred_element_type=f32)

    def columns(value, slot):
        return lax.dynamic_slice_in_dim(value, (part ^ slot) * quarter, quarter, value.ndim - 1)

    own_input = columns(token_inputs.reshape(rows, width), 0)
    terms = [columns(head_part, slot) for slot in range(tp)]
    received = [swap(terms[slot].astype(bf16), "tp", slot) for slot in range(1, tp)]
    total = own_input.astype(f32) + terms[0]
    for term in received:
        total = total + term.astype(f32)
    own_attended = total.astype(bf16)

    layered = [own_attended] + [swap(own_attended, "seq", across * k) for k in range(1, deep)]
    near = jnp.concatenate(layered[: deep // 2], axis=0)
    far = jnp.concatenate(layered[deep // 2 :], axis=0)
    near = jnp.concatenate([near] + [swap(near, "seq", k) for k in range(1, across)], axis=0)
    far = jnp.stack([far] + [swap(far, "tp", CORES * k) for k in range(1, ways)])
    near = jnp.stack([near] + [swap(near, "tp", CORES * k) for k in range(1, ways)])
    far = jnp.concatenate([far] + [swap(far, "seq", k) for k in range(1, across)], axis=1)
    both = jnp.concatenate([near, far], axis=1)
    other = swap(both, "tp", 1)
    all_rows = both.shape[1]

    def assemble(pieces, other_pieces, height):
        whole = jnp.zeros((height, width), bf16)
        for k in range(ways):
            for core, source in ((0, pieces), (1, other_pieces)):
                at = (part ^ (k * CORES + core)) * quarter
                whole = lax.dynamic_update_slice_in_dim(whole, source[k], at, 1)
        return whole

    gathered = assemble(both, other, all_rows)
    attended = gathered[:rows].reshape(steps, row_count, width)

    normed_mlp = rms_norm(gathered, mlp_gain).astype(bf16)
    gate_proj = jnp.dot(normed_mlp, w_gate, preferred_element_type=f32)
    up_proj = jnp.dot(normed_mlp, w_up, preferred_element_type=f32)
    activation = (jax.nn.silu(gate_proj) * up_proj).astype(bf16)
    partial_terms = jnp.dot(activation, w_down, preferred_element_type=f32).astype(bf16)

    pieces = jnp.stack([columns(partial_terms, slot) for slot in range(tp)]).reshape(
        ways, cores, all_rows, quarter
    )
    summed = pieces[:, 0].astype(f32) + swap(pieces[:, 1], "tp", 1).astype(f32)
    summed = summed.astype(bf16)
    half = all_rows // 2
    near, far = summed[:, :half], summed[:, half:]

    def add(first, others):
        value = first.astype(f32)
        for other in others:
            value = value + other.astype(f32)
        return value

    near = add(near[0], [swap(near[k], "tp", CORES * k) for k in range(1, ways)]).astype(bf16)
    far = far.reshape(ways, across, half // across, quarter)
    far = add(far[:, 0], [swap(far[:, k], "seq", k) for k in range(1, across)]).astype(bf16)
    near = near.reshape(across, half // across, quarter)
    near = add(near[0], [swap(near[k], "seq", k) for k in range(1, across)]).astype(bf16)
    far = add(far[0], [swap(far[k], "tp", CORES * k) for k in range(1, ways)]).astype(bf16)
    layered = jnp.concatenate([near, far], axis=0).reshape(deep, rows, quarter)
    mlp_result = add(layered[0], [swap(layered[k], "seq", across * k) for k in range(1, deep)])
    own_out = (own_attended.astype(f32) + mlp_result).astype(bf16)

    spread = jnp.stack([own_out] + [swap(own_out, "tp", CORES * k) for k in range(1, ways)])
    layer_out = assemble(spread, swap(spread, "tp", 1), rows).reshape(steps, row_count, width)
    return attended, layer_out


def solution(mesh):
    in_specs = (
        P(None, "seq", None),
        P(),
        P(None, "tp"),
        P(None, "tp"),
        P(None, "tp"),
        P("tp", None),
        P(),
        P(None, ("seq", "tp")),
        P(None, ("seq", "tp")),
        P(("seq", "tp"), None),
        P("seq", "tp", None, None),
        P("seq", "tp", None, None),
        P(),
        P("seq"),
        P("seq"),
        P(),
    )
    out_specs = (P(None, "seq", None), P(None, "seq", None))
    return jax.shard_map(local, mesh=mesh, in_specs=in_specs, out_specs=out_specs, check_vma=False)
```

```python
import functools

import jax
import jax.numpy as jnp
from jax import lax
from jax.experimental import pallas as pl
from jax.experimental.pallas import tpu as pltpu
from jax.sharding import PartitionSpec as P

STEPS = 4
CORES = 2

rope_theta = 100000000.0
norm_eps = 1e-05
masked_low = -1e30
f32 = jnp.float32
bf16 = jnp.bfloat16


def split_axis(size):
    fast = 1
    while fast * fast * 4 <= size:
        fast *= 2
    return size // fast, fast


def swap(value, axis, mask):
    size = lax.axis_size(axis)
    return lax.ppermute(value, axis, [(i, i ^ mask) for i in range(size)])


def dot_t(a, b):
    return lax.dot_general(a, b, (((1,), (1,)), ((), ())), preferred_element_type=f32)


def round_trip(value):
    return value.astype(bf16).astype(f32)


def encode_stats(top, total, pairs):
    pieces = []
    rest = top
    for _ in range(3):
        piece = round_trip(rest)
        pieces.append(piece)
        rest = rest - piece
    rest = total
    for _ in range(2):
        piece = round_trip(rest)
        pieces.append(piece)
        rest = rest - piece
    tile = pieces[0]
    for i in range(1, 5):
        tile = tile + pltpu.roll(pieces[i], i * pairs, 1)
    return tile.astype(bf16)


def decode_stats(tile, pairs):
    values = tile.astype(f32)
    lanes = values.shape[1]
    shifted = [values] + [pltpu.roll(values, lanes - i * pairs, 1) for i in range(1, 5)]
    top = shifted[0] + shifted[1] + shifted[2]
    total = shifted[3] + shifted[4]
    return top, total


def pages_kernel(
    block_pages, slot_ref, valid_ref, query_ref, fresh_key_ref, fresh_value_ref, key_hbm, value_hbm,
    out_ref, key_buf, value_buf, top_ref, total_ref, acc_ref, sems,
):
    page_count, kv_local, page_size, head_dim = key_buf.shape
    blocks = page_count // block_pages
    groups, tiles = out_ref.shape[:2]
    pairs = tiles - 1
    rows = query_ref.shape[1]
    per_step = rows // STEPS
    scale = head_dim ** (-0.5)

    def copies(block):
        at = pl.ds(block * block_pages, block_pages)
        return (
            pltpu.make_async_copy(key_hbm.at[at], key_buf.at[at], sems.at[0, block]),
            pltpu.make_async_copy(value_hbm.at[at], value_buf.at[at], sems.at[1, block]),
        )

    for block in range(blocks):
        for copy in copies(block):
            copy.start()

    top_ref[...] = jnp.full(top_ref.shape, masked_low, f32)
    total_ref[...] = jnp.zeros(total_ref.shape, f32)
    acc_ref[...] = jnp.zeros(acc_ref.shape, f32)

    def weigh(scores, live):
        scores = [jnp.where(keep, score * scale, masked_low) for score, keep in zip(scores, live)]
        tops = [jnp.max(score, axis=1, keepdims=True) for score in scores]
        weights = [
            jnp.where(keep, jnp.exp(score - top), 0.0) for score, top, keep in zip(scores, tops, live)
        ]
        totals = [jnp.sum(weight, axis=1, keepdims=True) for weight in weights]
        return tops, totals, [weight.astype(bf16) for weight in weights]

    fresh = fresh_key_ref.shape[1]
    row_step = lax.broadcasted_iota(jnp.int32, (rows, fresh), 0) // per_step
    column = lax.broadcasted_iota(jnp.int32, (rows, fresh), 1)
    scores = [dot_t(query_ref[i], fresh_key_ref[i]) for i in range(pairs)]
    tops, totals, weights = weigh(scores, [column <= row_step] * pairs)
    accs = [jnp.dot(weights[i], fresh_value_ref[i], preferred_element_type=f32) for i in range(pairs)]
    for i in range(pairs):
        top_ref[i] = jnp.broadcast_to(tops[i], (rows, head_dim))
        total_ref[i] = jnp.broadcast_to(totals[i], (rows, head_dim))
        acc_ref[i] = accs[i]

    lane = lax.broadcasted_iota(jnp.int32, (rows, page_size), 1)

    @pl.loop(0, blocks)
    def _(block):
        for copy in copies(block):
            copy.wait()
        pages = [block * block_pages + i for i in range(block_pages)]
        places = [(page, head) for page in pages for head in range(kv_local)]
        at = [slot_ref[page] * kv_local + head for page, head in places]
        live = [lane < valid_ref[page] for page, _ in places]
        scores = [dot_t(query_ref[i], key_buf[page, head]) for i, (page, head) in zip(at, places)]
        tops, totals, weights = weigh(scores, live)
        accs = [
            jnp.dot(weight, value_buf[page, head], preferred_element_type=f32)
            for weight, (page, head) in zip(weights, places)
        ]
        for i, top, total, acc in zip(at, tops, totals, accs):
            old_top = top_ref[i]
            new_top = jnp.maximum(old_top, top)
            old_factor = jnp.exp(old_top - new_top)
            factor = jnp.exp(top - new_top)
            top_ref[i] = new_top
            total_ref[i] = total_ref[i] * old_factor + total * factor
            acc_ref[i] = acc_ref[i] * old_factor + acc * factor

    out_lane = lax.broadcasted_iota(jnp.int32, (rows, head_dim), 1)

    @pl.loop(0, groups)
    def _(group):
        tops = jnp.zeros((rows, head_dim), f32)
        totals = jnp.zeros((rows, head_dim), f32)
        for i in range(pairs):
            at = group * pairs + i
            out_ref[group, i] = acc_ref[at].astype(bf16)
            tops = jnp.where(out_lane == i, top_ref[at], tops)
            totals = jnp.where(out_lane == i, total_ref[at], totals)
        out_ref[group, pairs] = encode_stats(tops, totals, pairs)


def attend_pages(queries, fresh_keys, fresh_values, key_cache, value_cache, slots, valid, groups):
    pairs = fresh_keys.shape[0]
    rows, head_dim = queries.shape[1:]
    page_count, kv_local, page_size, _ = key_cache.shape
    block_pages = 6
    while page_count % block_pages:
        block_pages -= 1
    blocks = page_count // block_pages
    count = queries.shape[0]
    vmem = pl.BlockSpec(memory_space=pltpu.VMEM)
    smem = pl.BlockSpec(memory_space=pltpu.SMEM)
    hbm = pl.BlockSpec(memory_space=pl.ANY)
    return pl.pallas_call(
        functools.partial(pages_kernel, block_pages),
        out_shape=jax.ShapeDtypeStruct((groups, pairs + 1, rows, head_dim), bf16),
        in_specs=[smem, smem, vmem, vmem, vmem, hbm, hbm],
        out_specs=vmem,
        scratch_shapes=[
            pltpu.VMEM(key_cache.shape, bf16),
            pltpu.VMEM(value_cache.shape, bf16),
            pltpu.VMEM((count, rows, head_dim), f32),
            pltpu.VMEM((count, rows, head_dim), f32),
            pltpu.VMEM((count, rows, head_dim), f32),
            pltpu.SemaphoreType.DMA((2, blocks)),
        ],
        compiler_params=pltpu.CompilerParams(vmem_limit_bytes=60 << 20),
        cost_estimate=pl.CostEstimate(
            flops=4 * rows * page_count * kv_local * page_size * head_dim,
            bytes_accessed=4 * page_count * kv_local * page_size * head_dim,
            transcendentals=0,
        ),
        name="attend_pages",
    )(slots, valid, queries, fresh_keys, fresh_values, key_cache, value_cache)


def merge_tile(parts, group, pairs):
    stats = [decode_stats(part[group, pairs], pairs) for part in parts]
    top = functools.reduce(jnp.maximum, [s[0] for s in stats])
    factors = [jnp.exp(s[0] - top) for s in stats]
    total = functools.reduce(jnp.add, [s[1] * f for s, f in zip(stats, factors)])
    return top, total, factors


def merge_pair(parts, factors, group, i):
    return functools.reduce(
        jnp.add, [part[group, i].astype(f32) * f[:, i : i + 1] for part, f in zip(parts, factors)]
    )


def merge_kernel(count, *refs):
    parts, out_ref = refs[:count], refs[count]
    groups, tiles, rows, head_dim = parts[0].shape
    pairs = tiles - 1
    used = lax.broadcasted_iota(jnp.int32, (rows, head_dim), 1) < pairs
    for group in range(groups):
        top, total, factors = merge_tile(parts, group, pairs)
        for i in range(pairs):
            out_ref[group, i] = merge_pair(parts, factors, group, i).astype(bf16)
        out_ref[group, pairs] = encode_stats(
            jnp.where(used, top, 0.0), jnp.where(used, total, 0.0), pairs
        )


vmem = pl.BlockSpec(memory_space=pltpu.VMEM)
smem = pl.BlockSpec(memory_space=pltpu.SMEM)
hbm = pl.BlockSpec(memory_space=pl.ANY)


def merge_parts(parts):
    return pl.pallas_call(
        functools.partial(merge_kernel, len(parts)),
        out_shape=jax.ShapeDtypeStruct(parts[0].shape, bf16),
        in_specs=[vmem] * len(parts),
        out_specs=vmem,
        compiler_params=pltpu.CompilerParams(vmem_limit_bytes=8 << 20),
        name="merge_parts",
    )(*parts)


def start_all(copies):
    for copy in copies:
        copy.start()


def query_kernel(
    kv_local, me_ref, slots_ref, lengths_ref, input_ref, gain_ref, weight_hbm,
    query_ref, normalized_ref, cosine_ref, sine_ref, weight_buf, total_ref, tile_ref, sems,
):
    steps, row_count, width = input_ref.shape
    head_dim = cosine_ref.shape[1]
    heads = weight_buf.shape[1] // head_dim
    group = heads // kv_local
    chunks = sems.shape[0]
    depth = width // chunks
    copies = []
    for chunk in range(chunks):
        at = pl.ds(chunk * depth, depth)
        copies.append(pltpu.make_async_copy(weight_hbm.at[at], weight_buf.at[at], sems.at[chunk]))
    start_all(copies)

    gain = gain_ref[...]
    for step in range(0, steps, 2):
        pair = []
        for at in (step, step + 1):
            floats = input_ref[at].astype(f32)
            mean = jnp.mean(floats * floats, axis=1, keepdims=True)
            pair.append(floats * lax.rsqrt(mean + norm_eps) * gain)
        normalized_ref[step * row_count : (step + 2) * row_count] = jnp.concatenate(pair, axis=0).astype(bf16)

    requests = slots_ref.shape[1]
    own = me_ref[0] * row_count + lax.broadcasted_iota(jnp.int32, (row_count, requests), 0)
    length = jnp.sum(jnp.where(slots_ref[...] == own, lengths_ref[...], 0), axis=1, keepdims=True)
    half = head_dim // 2
    lane = lax.broadcasted_iota(jnp.int32, (row_count, head_dim), 1)
    exponent = jnp.where(lane < half, lane, lane - half).astype(f32) * (2.0 / head_dim)
    inverse_freq = rope_theta ** (-exponent)
    for step in range(steps):
        angles = (length + step).astype(f32) * inverse_freq
        sine = jnp.sin(angles)
        cosine_ref[step * row_count : (step + 1) * row_count] = jnp.cos(angles)
        sine_ref[step * row_count : (step + 1) * row_count] = jnp.where(lane < half, -sine, sine)

    for chunk, copy in enumerate(copies):
        copy.wait()
        at = slice(chunk * depth, (chunk + 1) * depth)
        product = jnp.dot(normalized_ref[:, at], weight_buf[at], preferred_element_type=f32)
        total_ref[...] = product if chunk == 0 else total_ref[...] + product

    cosine, sine = cosine_ref[...], sine_ref[...]
    tile_rows = steps * group
    for head in range(heads):
        value = total_ref[:, head * head_dim : (head + 1) * head_dim]
        value = value * cosine + pltpu.roll(value, half, 1) * sine
        for step in range(steps):
            first = head // group * tile_rows + step * group + head % group
            tile_ref[pl.ds(first, row_count, stride=kv_local * tile_rows), :] = value[
                step * row_count : (step + 1) * row_count
            ]
    query_ref[...] = tile_ref[...].reshape(query_ref.shape).astype(bf16)


def project_queries(me, request_slot, cache_lengths, token_inputs, gain, weight, kv_local, head_dim):
    steps, row_count, width = token_inputs.shape
    rows = steps * row_count
    columns = weight.shape[1]
    tile_rows = columns // (kv_local * head_dim) * steps
    pairs = row_count * kv_local
    chunks = 4
    return pl.pallas_call(
        functools.partial(query_kernel, kv_local),
        out_shape=(
            jax.ShapeDtypeStruct((pairs, tile_rows, head_dim), bf16),
            jax.ShapeDtypeStruct((rows, width), bf16),
            jax.ShapeDtypeStruct((rows, head_dim), f32),
            jax.ShapeDtypeStruct((rows, head_dim), f32),
        ),
        in_specs=[smem, vmem, vmem, vmem, vmem, hbm],
        out_specs=(vmem, vmem, vmem, vmem),
        scratch_shapes=[
            pltpu.VMEM((width, columns), bf16),
            pltpu.VMEM((rows, columns), f32),
            pltpu.VMEM((pairs * tile_rows, head_dim), f32),
            pltpu.SemaphoreType.DMA((chunks,)),
        ],
        compiler_params=pltpu.CompilerParams(vmem_limit_bytes=58 << 20),
        cost_estimate=pl.CostEstimate(
            flops=2 * rows * width * columns, bytes_accessed=2 * width * columns, transcendentals=0
        ),
        name="project_queries",
    )(
        me.reshape(1),
        request_slot.reshape(1, -1),
        cache_lengths.reshape(1, -1),
        token_inputs,
        gain.reshape(1, width),
        weight,
    )


def fresh_kernel(
    kv_local, normalized_ref, cosine_ref, sine_ref, key_hbm, value_hbm,
    key_ref, value_ref, key_buf, value_buf, key_tile, value_tile, sems,
):
    rows, width = normalized_ref.shape
    head_dim = cosine_ref.shape[1]
    row_count = rows // STEPS
    pads = key_ref.shape[1]
    copies = [
        pltpu.make_async_copy(key_hbm, key_buf, sems.at[0]),
        pltpu.make_async_copy(value_hbm, value_buf, sems.at[1]),
    ]
    start_all(copies)
    key_tile[...] = jnp.zeros(key_tile.shape, f32)
    value_tile[...] = jnp.zeros(value_tile.shape, f32)
    cosine, sine = cosine_ref[...], sine_ref[...]
    for copy, buf, tile in ((copies[0], key_buf, key_tile), (copies[1], value_buf, value_tile)):
        copy.wait()
        product = jnp.dot(normalized_ref[...], buf[...], preferred_element_type=f32)
        for head in range(kv_local):
            value = product[:, head * head_dim : (head + 1) * head_dim]
            if buf is key_buf:
                value = value * cosine + pltpu.roll(value, head_dim // 2, 1) * sine
            for step in range(STEPS):
                tile[pl.ds(head * pads + step, row_count, stride=kv_local * pads), :] = value[
                    step * row_count : (step + 1) * row_count
                ]
    key_ref[...] = key_tile[...].reshape(key_ref.shape).astype(bf16)
    value_ref[...] = value_tile[...].reshape(value_ref.shape).astype(bf16)


def project_fresh(normalized, cosine, sine, key_projection, value_projection, kv_local, head_dim):
    rows, width = normalized.shape
    pairs = rows // STEPS * kv_local
    pads = 16
    columns = key_projection.shape[1]
    return pl.pallas_call(
        functools.partial(fresh_kernel, kv_local),
        out_shape=(jax.ShapeDtypeStruct((pairs, pads, head_dim), bf16),) * 2,
        in_specs=[vmem, vmem, vmem, hbm, hbm],
        out_specs=(vmem, vmem),
        scratch_shapes=[
            pltpu.VMEM((width, columns), bf16),
            pltpu.VMEM((width, columns), bf16),
            pltpu.VMEM((pairs * pads, head_dim), f32),
            pltpu.VMEM((pairs * pads, head_dim), f32),
            pltpu.SemaphoreType.DMA((2,)),
        ],
        compiler_params=pltpu.CompilerParams(vmem_limit_bytes=58 << 20),
        cost_estimate=pl.CostEstimate(
            flops=4 * rows * width * columns, bytes_accessed=4 * width * columns, transcendentals=0
        ),
        name="project_fresh",
    )(normalized, cosine, sine, key_projection, value_projection)


def out_kernel(
    count, kv_local, part_ref, input_ref, weight_hbm, *refs
):
    parts = refs[:count]
    own_ref, term_ref, weight_buf, tile_ref, attention_ref, sems = refs[count:]
    tp = sems.shape[0]
    quarter = own_ref.shape[1]
    part = part_ref[0]
    copies = []
    for slot in range(tp):
        at = pl.multiple_of((part ^ slot) * quarter, quarter)
        copies.append(
            pltpu.make_async_copy(
                weight_hbm.at[:, pl.ds(at, quarter)], weight_buf.at[slot], sems.at[slot]
            )
        )
    order = list(range(1, tp)) + [0]
    start_all([copies[slot] for slot in order])

    _, tiles, tile_rows, head_dim = parts[0].shape
    pairs = tiles - 1
    row_count = pairs // kv_local
    group = tile_rows // STEPS
    _, total, factors = merge_tile(parts, 0, pairs)
    inverse = 1.0 / total
    factors = [f * inverse for f in factors]
    for i in range(pairs):
        acc = merge_pair(parts, factors, 0, i)
        request, head = i // kv_local, i % kv_local
        for row in range(tile_rows):
            step, member = row // group, row % group
            column = (head * group + member) * head_dim
            at = step * row_count + request
            tile_ref[at : at + 1, column : column + head_dim] = acc[row : row + 1]
    attention_ref[...] = tile_ref[...].astype(bf16)
    for slot in order:
        copies[slot].wait()
        product = jnp.dot(attention_ref[...], weight_buf[slot], preferred_element_type=f32)
        if slot == 0:
            own_ref[...] = input_ref[...].astype(f32) + product
        else:
            term_ref[slot - 1] = product.astype(bf16)


def project_out(part, parts, own_input, weight, tp, kv_local):
    rows, quarter = own_input.shape
    depth = weight.shape[0]
    return pl.pallas_call(
        functools.partial(out_kernel, len(parts), kv_local),
        out_shape=(
            jax.ShapeDtypeStruct((rows, quarter), f32),
            jax.ShapeDtypeStruct((tp - 1, rows, quarter), bf16),
        ),
        in_specs=[smem, vmem, hbm] + [vmem] * len(parts),
        out_specs=(vmem, vmem),
        scratch_shapes=[
            pltpu.VMEM((tp, depth, quarter), bf16),
            pltpu.VMEM((rows, depth), f32),
            pltpu.VMEM((rows, depth), bf16),
            pltpu.SemaphoreType.DMA((tp,)),
        ],
        compiler_params=pltpu.CompilerParams(vmem_limit_bytes=58 << 20),
        cost_estimate=pl.CostEstimate(
            flops=2 * rows * weight.size, bytes_accessed=2 * weight.size, transcendentals=0
        ),
        name="project_out",
    )(part.reshape(1), own_input, weight, *parts)


def gate_up_copies(part, core, ways, quarter, gate_hbm, up_hbm, gate_buf, up_buf, sems):
    copies = []
    for way in range(ways):
        at = pl.multiple_of((part ^ (way * CORES + core)) * quarter, quarter)
        copies.append(
            pltpu.make_async_copy(gate_hbm.at[pl.ds(at, quarter)], gate_buf.at[way], sems.at[0, way])
        )
        copies.append(pltpu.make_async_copy(up_hbm.at[pl.ds(at, quarter)], up_buf.at[way], sems.at[1, way]))
    return copies


def scaled_rows(part, core, way, rows_ref, gain_ref):
    floats = rows_ref[way].astype(f32)
    squares = jnp.sum(floats * floats, axis=1, keepdims=True)
    return (floats * gain_ref[part ^ (way * CORES + core)]).astype(bf16), squares


def gate_up_kernel(
    core, part_ref, rows_ref, gain_ref, gate_hbm, up_hbm, gate_ref, up_ref, square_ref,
    gate_buf, up_buf, scaled_ref, sems,
):
    ways, _, quarter = rows_ref.shape
    part = part_ref[0]
    copies = gate_up_copies(part, core, ways, quarter, gate_hbm, up_hbm, gate_buf, up_buf, sems)
    start_all(copies)
    square = 0.0
    for way in range(ways):
        scaled, squares = scaled_rows(part, core, way, rows_ref, gain_ref)
        scaled_ref[way] = scaled
        square = square + squares
    square_ref[...] = jnp.broadcast_to(square, square_ref.shape)
    for way in range(ways):
        for copy, buf, out in (
            (copies[2 * way], gate_buf, gate_ref),
            (copies[2 * way + 1], up_buf, up_ref),
        ):
            copy.wait()
            product = jnp.dot(scaled_ref[way], buf[way], preferred_element_type=f32)
            out[...] = product if way == 0 else out[...] + product


def gate_up_half(part, core, rows, gains, w_gate, w_up):
    ways, all_rows, quarter = rows.shape
    hidden = w_gate.shape[1]
    return pl.pallas_call(
        functools.partial(gate_up_kernel, core),
        out_shape=(
            jax.ShapeDtypeStruct((all_rows, hidden), f32),
            jax.ShapeDtypeStruct((all_rows, hidden), f32),
            jax.ShapeDtypeStruct((all_rows, 128), f32),
        ),
        in_specs=[smem, vmem, vmem, hbm, hbm],
        out_specs=(vmem, vmem, vmem),
        scratch_shapes=[
            pltpu.VMEM((ways, quarter, hidden), bf16),
            pltpu.VMEM((ways, quarter, hidden), bf16),
            pltpu.VMEM(rows.shape, bf16),
            pltpu.SemaphoreType.DMA((2, ways)),
        ],
        compiler_params=pltpu.CompilerParams(vmem_limit_bytes=48 << 20),
        cost_estimate=pl.CostEstimate(
            flops=4 * rows.size * hidden,
            bytes_accessed=4 * ways * quarter * hidden + 8 * all_rows * hidden,
            transcendentals=0,
        ),
        name="gate_up_half",
    )(part.reshape(1), rows, gains, w_gate, w_up)


def down_copies(part, core, ways, quarter, down_hbm, down_buf, sems):
    copies = []
    for way in range(ways):
        at = pl.multiple_of((part ^ (way * CORES + core)) * quarter, quarter)
        copies.append(
            pltpu.make_async_copy(down_hbm.at[:, pl.ds(at, quarter)], down_buf.at[way], sems.at[way])
        )
    return copies


def rest_kernel(
    width, part_ref, rows_ref, gain_ref, old_gate_ref, old_up_ref, square_ref, gate_hbm, up_hbm, down_hbm,
    activation_ref, term_ref, gate_buf, up_buf, down_buf, scaled_ref, gate_ref, up_ref, sems, down_sems,
):
    ways, _, quarter = rows_ref.shape
    part = part_ref[0]
    copies = gate_up_copies(part, 1, ways, quarter, gate_hbm, up_hbm, gate_buf, up_buf, sems)
    later = down_copies(part, 1, ways, quarter, down_hbm, down_buf, down_sems)
    start_all(copies + later)
    square = square_ref[:, :1]
    for way in range(ways):
        scaled, squares = scaled_rows(part, 1, way, rows_ref, gain_ref)
        scaled_ref[way] = scaled
        square = square + squares
    factor = lax.rsqrt(square * (1.0 / width) + norm_eps)
    for way in range(ways):
        for copy, buf, old, out in (
            (copies[2 * way], gate_buf, old_gate_ref, gate_ref),
            (copies[2 * way + 1], up_buf, old_up_ref, up_ref),
        ):
            copy.wait()
            product = jnp.dot(scaled_ref[way], buf[way], preferred_element_type=f32)
            out[...] = (old if way == 0 else out)[...] + product
    gate = gate_ref[...] * factor
    up = up_ref[...] * factor
    activation_ref[...] = (gate / (1.0 + jnp.exp(-gate)) * up).astype(bf16)
    for way in range(ways):
        later[way].wait()
        product = jnp.dot(activation_ref[...], down_buf[way], preferred_element_type=f32)
        term_ref[way] = product.astype(bf16)


def gate_up_rest(part, rows, gains, w_gate, w_up, w_down, sums, width):
    ways, all_rows, quarter = rows.shape
    hidden = w_gate.shape[1]
    return pl.pallas_call(
        functools.partial(rest_kernel, width),
        out_shape=(
            jax.ShapeDtypeStruct((all_rows, hidden), bf16),
            jax.ShapeDtypeStruct((ways, all_rows, quarter), bf16),
        ),
        in_specs=[smem, vmem, vmem, vmem, vmem, vmem, hbm, hbm, hbm],
        out_specs=(vmem, vmem),
        scratch_shapes=[
            pltpu.VMEM((ways, quarter, hidden), bf16),
            pltpu.VMEM((ways, quarter, hidden), bf16),
            pltpu.VMEM((ways, hidden, quarter), bf16),
            pltpu.VMEM(rows.shape, bf16),
            pltpu.VMEM((all_rows, hidden), f32),
            pltpu.VMEM((all_rows, hidden), f32),
            pltpu.SemaphoreType.DMA((2, ways)),
            pltpu.SemaphoreType.DMA((ways,)),
        ],
        compiler_params=pltpu.CompilerParams(vmem_limit_bytes=48 << 20),
        cost_estimate=pl.CostEstimate(
            flops=6 * rows.size * hidden, bytes_accessed=6 * ways * quarter * hidden, transcendentals=0
        ),
        name="gate_up_rest",
    )(part.reshape(1), rows, gains, *sums, w_gate, w_up, w_down)


def down_kernel(part_ref, activation_ref, down_hbm, term_ref, down_buf, sems):
    ways, _, quarter = term_ref.shape
    copies = down_copies(part_ref[0], 0, ways, quarter, down_hbm, down_buf, sems)
    start_all(copies)
    for way in range(ways):
        copies[way].wait()
        product = jnp.dot(activation_ref[...], down_buf[way], preferred_element_type=f32)
        term_ref[way] = product.astype(bf16)


def down_half(part, activation, w_down, ways):
    all_rows, hidden = activation.shape
    quarter = w_down.shape[1] // (ways * CORES)
    return pl.pallas_call(
        down_kernel,
        out_shape=jax.ShapeDtypeStruct((ways, all_rows, quarter), bf16),
        in_specs=[smem, vmem, hbm],
        out_specs=vmem,
        scratch_shapes=[
            pltpu.VMEM((ways, hidden, quarter), bf16),
            pltpu.SemaphoreType.DMA((ways,)),
        ],
        compiler_params=pltpu.CompilerParams(vmem_limit_bytes=48 << 20),
        cost_estimate=pl.CostEstimate(
            flops=w_down.size * all_rows, bytes_accessed=w_down.size, transcendentals=0
        ),
        name="down_half",
    )(part.reshape(1), activation, w_down)


def local(
    token_inputs,
    attn_gain,
    w_query,
    key_projection,
    value_projection,
    w_output,
    mlp_gain,
    w_gate,
    w_up,
    w_down,
    key_cache,
    paged_value_cache,
    cache_lengths,
    page_request,
    page_number,
    request_slot,
):
    steps, row_count, width = token_inputs.shape
    seq, tp = lax.axis_size("seq"), lax.axis_size("tp")
    deep, across = split_axis(seq)
    ways, cores = tp // CORES, CORES
    page_count, kv_local, page_size, head_dim = key_cache.shape
    heads_per_group = w_query.shape[1] // (kv_local * head_dim)
    rows = steps * row_count
    pairs = row_count * kv_local
    me, part = lax.axis_index("seq"), lax.axis_index("tp")
    quarter = width // tp

    page_live = page_request >= 0
    request_ids = jnp.arange(request_slot.shape[0], dtype=jnp.int32)
    is_request = request_ids[None, :] == page_request[:, None]
    page_row = jnp.sum(jnp.where(is_request, request_slot[None, :], 0), axis=1)
    page_length = jnp.sum(jnp.where(is_request, cache_lengths[None, :], 0), axis=1)
    valid = jnp.where(page_live, jnp.clip(page_length - page_number * page_size, 0, page_size), 0)
    mask = (page_row // row_count) ^ me
    slots = ((mask % across) * deep + mask // across) * row_count + page_row % row_count

    query, normalized, cosine, sine = project_queries(
        me, request_slot, cache_lengths, token_inputs, attn_gain, w_query, kv_local, head_dim
    )
    shared = [query] + [swap(query, "seq", across * k) for k in range(1, deep)]
    shared = jnp.concatenate(shared, axis=0)
    queries = [shared] + [swap(shared, "seq", k) for k in range(1, across)]
    queries = jnp.concatenate(queries, axis=0)

    fresh_keys, fresh_values = project_fresh(
        normalized, cosine, sine, key_projection, value_projection, kv_local, head_dim
    )

    packed = attend_pages(
        queries,
        fresh_keys,
        fresh_values,
        key_cache,
        paged_value_cache,
        slots,
        valid,
        seq,
    )
    sides = [packed[:deep]] + [swap(packed[k * deep : (k + 1) * deep], "seq", k) for k in range(1, across)]
    merged = merge_parts(sides)
    layers = [merged[:1]] + [swap(merged[k : k + 1], "seq", across * k) for k in range(1, deep)]
    own_input = lax.dynamic_slice_in_dim(token_inputs.reshape(rows, width), part * quarter, quarter, 1)
    own_term, terms = project_out(part, layers, own_input, w_output, tp, kv_local)
    total = own_term
    for slot in range(1, tp):
        total = total + swap(terms[slot - 1], "tp", slot).astype(f32)
    own_attended = total.astype(bf16)

    layered = [own_attended] + [swap(own_attended, "seq", across * k) for k in range(1, deep)]
    near = jnp.concatenate(layered[: deep // 2], axis=0)
    far = jnp.concatenate(layered[deep // 2 :], axis=0)
    near = jnp.concatenate([near] + [swap(near, "seq", k) for k in range(1, across)], axis=0)
    far = jnp.stack([far] + [swap(far, "tp", CORES * k) for k in range(1, ways)])
    near = jnp.stack([near] + [swap(near, "tp", CORES * k) for k in range(1, ways)])
    far = jnp.concatenate([far] + [swap(far, "seq", k) for k in range(1, across)], axis=1)
    both = jnp.concatenate([near, far], axis=1)
    other = swap(both, "tp", 1)
    all_rows = both.shape[1]

    def assemble(pieces, other_pieces, height):
        whole = jnp.zeros((height, width), bf16)
        for k in range(ways):
            for core, source in ((0, pieces), (1, other_pieces)):
                at = (part ^ (k * CORES + core)) * quarter
                whole = lax.dynamic_update_slice_in_dim(whole, source[k], at, 1)
        return whole

    gains = mlp_gain.reshape(tp, 1, quarter)
    sums = gate_up_half(part, 0, both, gains, w_gate, w_up)
    activation, other_terms = gate_up_rest(part, other, gains, w_gate, w_up, w_down, sums, width)
    received = swap(other_terms, "tp", 1)
    own_terms = down_half(part, activation, w_down, ways)
    summed = (own_terms.astype(f32) + received.astype(f32)).astype(bf16)
    attended = assemble(both[:, :rows], other[:, :rows], rows).reshape(steps, row_count, width)
    half = all_rows // 2
    near, far = summed[:, :half], summed[:, half:]

    def add(first, others):
        value = first.astype(f32)
        for other in others:
            value = value + other.astype(f32)
        return value

    near = add(near[0], [swap(near[k], "tp", CORES * k) for k in range(1, ways)]).astype(bf16)
    far = far.reshape(ways, across, half // across, quarter)
    far = add(far[:, 0], [swap(far[:, k], "seq", k) for k in range(1, across)]).astype(bf16)
    near = near.reshape(across, half // across, quarter)
    near = add(near[0], [swap(near[k], "seq", k) for k in range(1, across)]).astype(bf16)
    far = add(far[0], [swap(far[k], "tp", CORES * k) for k in range(1, ways)]).astype(bf16)
    layered = jnp.concatenate([near, far], axis=0).reshape(deep, rows, quarter)
    mlp_result = add(layered[0], [swap(layered[k], "seq", across * k) for k in range(1, deep)])
    own_out = (own_attended.astype(f32) + mlp_result).astype(bf16)

    spread = jnp.stack([own_out] + [swap(own_out, "tp", CORES * k) for k in range(1, ways)])
    layer_out = assemble(spread, swap(spread, "tp", 1), rows).reshape(steps, row_count, width)
    return attended, layer_out


def solution(mesh):
    in_specs = (
        P(None, "seq", None),
        P(),
        P(None, "tp"),
        P(None, "tp"),
        P(None, "tp"),
        P("tp", None),
        P(),
        P(None, ("seq", "tp")),
        P(None, ("seq", "tp")),
        P(("seq", "tp"), None),
        P("seq", "tp", None, None),
        P("seq", "tp", None, None),
        P(),
        P("seq"),
        P("seq"),
        P(),
    )
    out_specs = (P(None, "seq", None), P(None, "seq", None))
    return jax.shard_map(local, mesh=mesh, in_specs=in_specs, out_specs=out_specs, check_vma=False)
```

```python
import functools

import jax
import jax.numpy as jnp
from jax import lax
from jax.experimental import pallas as pl
from jax.experimental.pallas import tpu as pltpu
from jax.sharding import PartitionSpec as P

STEPS = 4
CORES = 2

rope_theta = 100000000.0
norm_eps = 1e-05
masked_low = -1e30
f32 = jnp.float32
bf16 = jnp.bfloat16


def split_axis(size):
    fast = 1
    while fast * fast * 4 <= size:
        fast *= 2
    return size // fast, fast


def swap(value, axis, mask):
    size = lax.axis_size(axis)
    return lax.ppermute(value, axis, [(i, i ^ mask) for i in range(size)])


def dot_t(a, b):
    return lax.dot_general(a, b, (((1,), (1,)), ((), ())), preferred_element_type=f32)


def round_trip(value):
    return value.astype(bf16).astype(f32)


def encode_stats(top, total, pairs):
    pieces = []
    rest = top
    for _ in range(3):
        piece = round_trip(rest)
        pieces.append(piece)
        rest = rest - piece
    rest = total
    for _ in range(2):
        piece = round_trip(rest)
        pieces.append(piece)
        rest = rest - piece
    tile = pieces[0]
    for i in range(1, 5):
        tile = tile + pltpu.roll(pieces[i], i * pairs, 1)
    return tile.astype(bf16)


def decode_stats(tile, pairs):
    values = tile.astype(f32)
    lanes = values.shape[1]
    shifted = [values] + [pltpu.roll(values, lanes - i * pairs, 1) for i in range(1, 5)]
    top = shifted[0] + shifted[1] + shifted[2]
    total = shifted[3] + shifted[4]
    return top, total


def pages_kernel(
    block_pages, slot_ref, valid_ref, query_ref, fresh_key_ref, fresh_value_ref, key_buf, value_buf,
    out_ref, top_ref, total_ref, acc_ref,
):
    page_count, kv_local, page_size, head_dim = key_buf.shape
    blocks = page_count // block_pages
    groups, tiles = out_ref.shape[:2]
    pairs = tiles - 1
    rows = query_ref.shape[1]
    per_step = rows // STEPS
    scale = head_dim ** (-0.5)

    top_ref[...] = jnp.full(top_ref.shape, masked_low, f32)
    total_ref[...] = jnp.zeros(total_ref.shape, f32)
    acc_ref[...] = jnp.zeros(acc_ref.shape, f32)

    def weigh(scores, live):
        scores = [jnp.where(keep, score * scale, masked_low) for score, keep in zip(scores, live)]
        tops = [jnp.max(score, axis=1, keepdims=True) for score in scores]
        weights = [
            jnp.where(keep, jnp.exp(score - top), 0.0) for score, top, keep in zip(scores, tops, live)
        ]
        totals = [jnp.sum(weight, axis=1, keepdims=True) for weight in weights]
        return tops, totals, [weight.astype(bf16) for weight in weights]

    fresh = fresh_key_ref.shape[1]
    row_step = lax.broadcasted_iota(jnp.int32, (rows, fresh), 0) // per_step
    column = lax.broadcasted_iota(jnp.int32, (rows, fresh), 1)
    scores = [dot_t(query_ref[i], fresh_key_ref[i]) for i in range(pairs)]
    tops, totals, weights = weigh(scores, [column <= row_step] * pairs)
    accs = [jnp.dot(weights[i], fresh_value_ref[i], preferred_element_type=f32) for i in range(pairs)]
    for i in range(pairs):
        top_ref[i] = jnp.broadcast_to(tops[i], (rows, head_dim))
        total_ref[i] = jnp.broadcast_to(totals[i], (rows, head_dim))
        acc_ref[i] = accs[i]

    lane = lax.broadcasted_iota(jnp.int32, (rows, page_size), 1)

    @pl.loop(0, blocks)
    def _(block):
        pages = [block * block_pages + i for i in range(block_pages)]
        places = [(page, head) for page in pages for head in range(kv_local)]
        at = [slot_ref[page] * kv_local + head for page, head in places]
        live = [lane < valid_ref[page] for page, _ in places]
        scores = [dot_t(query_ref[i], key_buf[page, head]) for i, (page, head) in zip(at, places)]
        tops, totals, weights = weigh(scores, live)
        accs = [
            jnp.dot(weight, value_buf[page, head], preferred_element_type=f32)
            for weight, (page, head) in zip(weights, places)
        ]
        for i, top, total, acc in zip(at, tops, totals, accs):
            old_top = top_ref[i]
            new_top = jnp.maximum(old_top, top)
            old_factor = jnp.exp(old_top - new_top)
            factor = jnp.exp(top - new_top)
            top_ref[i] = new_top
            total_ref[i] = total_ref[i] * old_factor + total * factor
            acc_ref[i] = acc_ref[i] * old_factor + acc * factor

    out_lane = lax.broadcasted_iota(jnp.int32, (rows, head_dim), 1)

    @pl.loop(0, groups)
    def _(group):
        tops = jnp.zeros((rows, head_dim), f32)
        totals = jnp.zeros((rows, head_dim), f32)
        for i in range(pairs):
            at = group * pairs + i
            out_ref[group, i] = acc_ref[at].astype(bf16)
            tops = jnp.where(out_lane == i, top_ref[at], tops)
            totals = jnp.where(out_lane == i, total_ref[at], totals)
        out_ref[group, pairs] = encode_stats(tops, totals, pairs)


def attend_pages(queries, fresh_keys, fresh_values, key_cache, value_cache, slots, valid, groups):
    pairs = fresh_keys.shape[0]
    rows, head_dim = queries.shape[1:]
    page_count, kv_local, page_size, _ = key_cache.shape
    block_pages = 6
    while page_count % block_pages:
        block_pages -= 1
    count = queries.shape[0]
    return pl.pallas_call(
        functools.partial(pages_kernel, block_pages),
        out_shape=jax.ShapeDtypeStruct((groups, pairs + 1, rows, head_dim), bf16),
        in_specs=[smem, smem] + [vmem] * 5,
        out_specs=vmem,
        scratch_shapes=[
            pltpu.VMEM((count, rows, head_dim), f32),
            pltpu.VMEM((count, rows, head_dim), f32),
            pltpu.VMEM((count, rows, head_dim), f32),
        ],
        compiler_params=pltpu.CompilerParams(vmem_limit_bytes=14 << 20),
        cost_estimate=pl.CostEstimate(
            flops=4 * rows * page_count * kv_local * page_size * head_dim,
            bytes_accessed=4 * page_count * kv_local * page_size * head_dim,
            transcendentals=0,
        ),
        name="attend_pages",
    )(slots, valid, queries, fresh_keys, fresh_values, key_cache, value_cache)


def merge_tile(parts, group, pairs):
    stats = [decode_stats(part[group, pairs], pairs) for part in parts]
    top = functools.reduce(jnp.maximum, [s[0] for s in stats])
    factors = [jnp.exp(s[0] - top) for s in stats]
    total = functools.reduce(jnp.add, [s[1] * f for s, f in zip(stats, factors)])
    return top, total, factors


def merge_pair(parts, factors, group, i):
    return functools.reduce(
        jnp.add, [part[group, i].astype(f32) * f[:, i : i + 1] for part, f in zip(parts, factors)]
    )


def merge_kernel(count, *refs):
    parts, out_ref = refs[:count], refs[count]
    groups, tiles, rows, head_dim = parts[0].shape
    pairs = tiles - 1
    used = lax.broadcasted_iota(jnp.int32, (rows, head_dim), 1) < pairs
    for group in range(groups):
        top, total, factors = merge_tile(parts, group, pairs)
        for i in range(pairs):
            out_ref[group, i] = merge_pair(parts, factors, group, i).astype(bf16)
        out_ref[group, pairs] = encode_stats(
            jnp.where(used, top, 0.0), jnp.where(used, total, 0.0), pairs
        )


vmem = pl.BlockSpec(memory_space=pltpu.VMEM)
smem = pl.BlockSpec(memory_space=pltpu.SMEM)
hbm = pl.BlockSpec(memory_space=pl.ANY)


def merge_parts(parts):
    return pl.pallas_call(
        functools.partial(merge_kernel, len(parts)),
        out_shape=jax.ShapeDtypeStruct(parts[0].shape, bf16),
        in_specs=[vmem] * len(parts),
        out_specs=vmem,
        compiler_params=pltpu.CompilerParams(vmem_limit_bytes=8 << 20),
        name="merge_parts",
    )(*parts)


def columns_of(ref, index, size):
    return ref[:, pl.ds(pl.multiple_of(index * size, size), size)]


def rows_of(ref, index, size):
    return ref[pl.ds(pl.multiple_of(index * size, size), size), :]


def start_all(copies):
    for copy in copies:
        copy.start()


def query_kernel(
    kv_local, me_ref, slots_ref, lengths_ref, input_ref, gain_ref, weight_hbm,
    query_ref, normalized_ref, cosine_ref, sine_ref, weight_buf, total_ref, tile_ref, sems,
):
    steps, row_count, width = input_ref.shape
    head_dim = cosine_ref.shape[1]
    heads = weight_buf.shape[1] // head_dim
    group = heads // kv_local
    chunks = sems.shape[0]
    depth = width // chunks
    copies = []
    for chunk in range(chunks):
        at = pl.ds(chunk * depth, depth)
        copies.append(pltpu.make_async_copy(weight_hbm.at[at], weight_buf.at[at], sems.at[chunk]))
    start_all(copies)

    gain = gain_ref[...]
    for step in range(0, steps, 2):
        pair = []
        for at in (step, step + 1):
            floats = input_ref[at].astype(f32)
            mean = jnp.mean(floats * floats, axis=1, keepdims=True)
            pair.append(floats * lax.rsqrt(mean + norm_eps) * gain)
        normalized_ref[step * row_count : (step + 2) * row_count] = jnp.concatenate(pair, axis=0).astype(bf16)

    requests = slots_ref.shape[1]
    own = me_ref[0] * row_count + lax.broadcasted_iota(jnp.int32, (row_count, requests), 0)
    length = jnp.sum(jnp.where(slots_ref[...] == own, lengths_ref[...], 0), axis=1, keepdims=True)
    half = head_dim // 2
    lane = lax.broadcasted_iota(jnp.int32, (row_count, head_dim), 1)
    exponent = jnp.where(lane < half, lane, lane - half).astype(f32) * (2.0 / head_dim)
    inverse_freq = rope_theta ** (-exponent)
    for step in range(steps):
        angles = (length + step).astype(f32) * inverse_freq
        sine = jnp.sin(angles)
        cosine_ref[step * row_count : (step + 1) * row_count] = jnp.cos(angles)
        sine_ref[step * row_count : (step + 1) * row_count] = jnp.where(lane < half, -sine, sine)

    for chunk, copy in enumerate(copies):
        copy.wait()
        at = slice(chunk * depth, (chunk + 1) * depth)
        product = jnp.dot(normalized_ref[:, at], weight_buf[at], preferred_element_type=f32)
        total_ref[...] = product if chunk == 0 else total_ref[...] + product

    cosine, sine = cosine_ref[...], sine_ref[...]
    tile_rows = steps * group
    for head in range(heads):
        value = total_ref[:, head * head_dim : (head + 1) * head_dim]
        value = value * cosine + pltpu.roll(value, half, 1) * sine
        for step in range(steps):
            first = head // group * tile_rows + step * group + head % group
            tile_ref[pl.ds(first, row_count, stride=kv_local * tile_rows), :] = value[
                step * row_count : (step + 1) * row_count
            ]
    query_ref[...] = tile_ref[...].reshape(query_ref.shape).astype(bf16)


def project_queries(me, request_slot, cache_lengths, token_inputs, gain, weight, kv_local, head_dim):
    steps, row_count, width = token_inputs.shape
    rows = steps * row_count
    columns = weight.shape[1]
    tile_rows = columns // (kv_local * head_dim) * steps
    pairs = row_count * kv_local
    chunks = 4
    return pl.pallas_call(
        functools.partial(query_kernel, kv_local),
        out_shape=(
            jax.ShapeDtypeStruct((pairs, tile_rows, head_dim), bf16),
            jax.ShapeDtypeStruct((rows, width), bf16),
            jax.ShapeDtypeStruct((rows, head_dim), f32),
            jax.ShapeDtypeStruct((rows, head_dim), f32),
        ),
        in_specs=[smem, vmem, vmem, vmem, vmem, hbm],
        out_specs=(vmem, vmem, vmem, vmem),
        scratch_shapes=[
            pltpu.VMEM((width, columns), bf16),
            pltpu.VMEM((rows, columns), f32),
            pltpu.VMEM((pairs * tile_rows, head_dim), f32),
            pltpu.SemaphoreType.DMA((chunks,)),
        ],
        compiler_params=pltpu.CompilerParams(vmem_limit_bytes=58 << 20),
        cost_estimate=pl.CostEstimate(
            flops=2 * rows * width * columns, bytes_accessed=2 * width * columns, transcendentals=0
        ),
        name="project_queries",
    )(
        me.reshape(1),
        request_slot.reshape(1, -1),
        cache_lengths.reshape(1, -1),
        token_inputs,
        gain.reshape(1, width),
        weight,
    )


def fresh_kernel(
    kv_local, normalized_ref, cosine_ref, sine_ref, key_hbm, value_hbm,
    key_ref, value_ref, key_buf, value_buf, key_tile, value_tile, sems,
):
    rows, width = normalized_ref.shape
    head_dim = cosine_ref.shape[1]
    row_count = rows // STEPS
    pads = key_ref.shape[1]
    copies = [
        pltpu.make_async_copy(key_hbm, key_buf, sems.at[0]),
        pltpu.make_async_copy(value_hbm, value_buf, sems.at[1]),
    ]
    start_all(copies)
    key_tile[...] = jnp.zeros(key_tile.shape, f32)
    value_tile[...] = jnp.zeros(value_tile.shape, f32)
    cosine, sine = cosine_ref[...], sine_ref[...]
    for copy, buf, tile in ((copies[0], key_buf, key_tile), (copies[1], value_buf, value_tile)):
        copy.wait()
        product = jnp.dot(normalized_ref[...], buf[...], preferred_element_type=f32)
        for head in range(kv_local):
            value = product[:, head * head_dim : (head + 1) * head_dim]
            if buf is key_buf:
                value = value * cosine + pltpu.roll(value, head_dim // 2, 1) * sine
            for step in range(STEPS):
                tile[pl.ds(head * pads + step, row_count, stride=kv_local * pads), :] = value[
                    step * row_count : (step + 1) * row_count
                ]
    key_ref[...] = key_tile[...].reshape(key_ref.shape).astype(bf16)
    value_ref[...] = value_tile[...].reshape(value_ref.shape).astype(bf16)


def project_fresh(normalized, cosine, sine, key_projection, value_projection, kv_local, head_dim):
    rows, width = normalized.shape
    pairs = rows // STEPS * kv_local
    pads = 16
    columns = key_projection.shape[1]
    return pl.pallas_call(
        functools.partial(fresh_kernel, kv_local),
        out_shape=(jax.ShapeDtypeStruct((pairs, pads, head_dim), bf16),) * 2,
        in_specs=[vmem, vmem, vmem, hbm, hbm],
        out_specs=(vmem, vmem),
        scratch_shapes=[
            pltpu.VMEM((width, columns), bf16),
            pltpu.VMEM((width, columns), bf16),
            pltpu.VMEM((pairs * pads, head_dim), f32),
            pltpu.VMEM((pairs * pads, head_dim), f32),
            pltpu.SemaphoreType.DMA((2,)),
        ],
        compiler_params=pltpu.CompilerParams(vmem_limit_bytes=50 << 20),
        cost_estimate=pl.CostEstimate(
            flops=4 * rows * width * columns, bytes_accessed=4 * width * columns, transcendentals=0
        ),
        name="project_fresh",
    )(normalized, cosine, sine, key_projection, value_projection)


def out_kernel(
    count, kv_local, part_ref, input_ref, weight_hbm, *refs
):
    parts = refs[:count]
    own_ref, term_ref, weight_buf, tile_ref, attention_ref, sems = refs[count:]
    tp = sems.shape[0]
    quarter = own_ref.shape[1]
    part = part_ref[0]
    copies = []
    for slot in range(tp):
        at = pl.multiple_of((part ^ slot) * quarter, quarter)
        copies.append(
            pltpu.make_async_copy(
                weight_hbm.at[:, pl.ds(at, quarter)], weight_buf.at[slot], sems.at[slot]
            )
        )
    order = list(range(1, tp)) + [0]
    start_all([copies[slot] for slot in order])

    _, tiles, tile_rows, head_dim = parts[0].shape
    pairs = tiles - 1
    row_count = pairs // kv_local
    group = tile_rows // STEPS
    _, total, factors = merge_tile(parts, 0, pairs)
    inverse = 1.0 / total
    factors = [f * inverse for f in factors]
    for i in range(pairs):
        acc = merge_pair(parts, factors, 0, i)
        request, head = i // kv_local, i % kv_local
        for row in range(tile_rows):
            step, member = row // group, row % group
            column = (head * group + member) * head_dim
            at = step * row_count + request
            tile_ref[at : at + 1, column : column + head_dim] = acc[row : row + 1]
    attention_ref[...] = tile_ref[...].astype(bf16)
    for slot in order:
        copies[slot].wait()
        product = jnp.dot(attention_ref[...], weight_buf[slot], preferred_element_type=f32)
        if slot == 0:
            own_ref[...] = input_ref[...].astype(f32) + product
        else:
            term_ref[slot - 1] = product.astype(bf16)


def project_out(part, parts, own_input, weight, tp, kv_local):
    rows, quarter = own_input.shape
    depth = weight.shape[0]
    return pl.pallas_call(
        functools.partial(out_kernel, len(parts), kv_local),
        out_shape=(
            jax.ShapeDtypeStruct((rows, quarter), f32),
            jax.ShapeDtypeStruct((tp - 1, rows, quarter), bf16),
        ),
        in_specs=[smem, vmem, hbm] + [vmem] * len(parts),
        out_specs=(vmem, vmem),
        scratch_shapes=[
            pltpu.VMEM((tp, depth, quarter), bf16),
            pltpu.VMEM((rows, depth), f32),
            pltpu.VMEM((rows, depth), bf16),
            pltpu.SemaphoreType.DMA((tp,)),
        ],
        compiler_params=pltpu.CompilerParams(vmem_limit_bytes=50 << 20),
        cost_estimate=pl.CostEstimate(
            flops=2 * rows * weight.size, bytes_accessed=2 * weight.size, transcendentals=0
        ),
        name="project_out",
    )(part.reshape(1), own_input, weight, *parts)


def join_kernel(ways, near_count, *refs):
    out_ref = refs[-1]
    half = refs[0].shape[1]
    row = 0
    for group in range(2):
        pieces = refs[group * near_count : (group + 1) * near_count]
        height = pieces[0].shape[0]
        for way in range(ways):
            out_ref[way, row : row + height, :half] = pieces[way][...]
        at = row
        for piece in pieces[ways:]:
            out_ref[:, at : at + piece.shape[1], half:] = piece[...]
            at += piece.shape[1]
        row += height


def join_groups(near, far, ways):
    pieces = near + far
    columns = pieces[0].shape[1] + pieces[ways].shape[2]
    all_rows = near[0].shape[0] + far[0].shape[0]
    return pl.pallas_call(
        functools.partial(join_kernel, ways, len(near)),
        out_shape=jax.ShapeDtypeStruct((ways, all_rows, columns), bf16),
        in_specs=[vmem] * len(pieces),
        out_specs=vmem,
        compiler_params=pltpu.CompilerParams(vmem_limit_bytes=8 << 20),
        cost_estimate=pl.CostEstimate(
            flops=0, bytes_accessed=4 * ways * all_rows * columns, transcendentals=0
        ),
        name="join_groups",
    )(*pieces)


def gate_up_copies(part, core, ways, quarter, gate_hbm, up_hbm, gate_buf, up_buf, sems):
    copies = []
    for way in range(ways):
        at = pl.multiple_of((part ^ (way * CORES + core)) * quarter, quarter)
        copies.append(
            pltpu.make_async_copy(gate_hbm.at[pl.ds(at, quarter)], gate_buf.at[way], sems.at[0, way])
        )
        copies.append(pltpu.make_async_copy(up_hbm.at[pl.ds(at, quarter)], up_buf.at[way], sems.at[1, way]))
    return copies


def scaled_rows(part, core, way, rows_ref, gain_ref):
    floats = rows_ref[way].astype(f32)
    squares = jnp.sum(floats * floats, axis=1, keepdims=True)
    return (floats * gain_ref[part ^ (way * CORES + core)]).astype(bf16), squares


def gate_up_kernel(
    core, part_ref, rows_ref, gain_ref, gate_hbm, up_hbm, gate_ref, up_ref, square_ref,
    gate_buf, up_buf, scaled_ref, sems,
):
    ways, _, quarter = rows_ref.shape
    part = part_ref[0]
    copies = gate_up_copies(part, core, ways, quarter, gate_hbm, up_hbm, gate_buf, up_buf, sems)
    start_all(copies)
    square = 0.0
    for way in range(ways):
        scaled, squares = scaled_rows(part, core, way, rows_ref, gain_ref)
        scaled_ref[way] = scaled
        square = square + squares
    square_ref[...] = jnp.broadcast_to(square, square_ref.shape)
    for way in range(ways):
        for copy, buf, out in (
            (copies[2 * way], gate_buf, gate_ref),
            (copies[2 * way + 1], up_buf, up_ref),
        ):
            copy.wait()
            product = jnp.dot(scaled_ref[way], buf[way], preferred_element_type=f32)
            out[...] = product if way == 0 else out[...] + product


def gate_up_half(part, core, rows, gains, w_gate, w_up):
    ways, all_rows, quarter = rows.shape
    hidden = w_gate.shape[1]
    return pl.pallas_call(
        functools.partial(gate_up_kernel, core),
        out_shape=(
            jax.ShapeDtypeStruct((all_rows, hidden), f32),
            jax.ShapeDtypeStruct((all_rows, hidden), f32),
            jax.ShapeDtypeStruct((all_rows, 128), f32),
        ),
        in_specs=[smem, vmem, vmem, hbm, hbm],
        out_specs=(vmem, vmem, vmem),
        scratch_shapes=[
            pltpu.VMEM((ways, quarter, hidden), bf16),
            pltpu.VMEM((ways, quarter, hidden), bf16),
            pltpu.VMEM(rows.shape, bf16),
            pltpu.SemaphoreType.DMA((2, ways)),
        ],
        compiler_params=pltpu.CompilerParams(vmem_limit_bytes=40 << 20),
        cost_estimate=pl.CostEstimate(
            flops=4 * rows.size * hidden,
            bytes_accessed=4 * ways * quarter * hidden + 8 * all_rows * hidden,
            transcendentals=0,
        ),
        name="gate_up_half",
    )(part.reshape(1), rows, gains, w_gate, w_up)


def down_copies(part, core, ways, quarter, down_hbm, down_buf, sems):
    copies = []
    for way in range(ways):
        at = pl.multiple_of((part ^ (way * CORES + core)) * quarter, quarter)
        copies.append(
            pltpu.make_async_copy(down_hbm.at[:, pl.ds(at, quarter)], down_buf.at[way], sems.at[way])
        )
    return copies


def rest_kernel(
    width, part_ref, rows_ref, gain_ref, old_gate_ref, old_up_ref, square_ref, gate_hbm, up_hbm, down_hbm,
    activation_ref, term_ref, gate_buf, up_buf, down_buf, scaled_ref, gate_ref, up_ref, sems, down_sems,
):
    ways, _, quarter = rows_ref.shape
    part = part_ref[0]
    copies = gate_up_copies(part, 1, ways, quarter, gate_hbm, up_hbm, gate_buf, up_buf, sems)
    later = down_copies(part, 1, ways, quarter, down_hbm, down_buf, down_sems)
    start_all(copies + later)
    square = square_ref[:, :1]
    for way in range(ways):
        scaled, squares = scaled_rows(part, 1, way, rows_ref, gain_ref)
        scaled_ref[way] = scaled
        square = square + squares
    factor = lax.rsqrt(square * (1.0 / width) + norm_eps)
    for way in range(ways):
        for copy, buf, old, out in (
            (copies[2 * way], gate_buf, old_gate_ref, gate_ref),
            (copies[2 * way + 1], up_buf, old_up_ref, up_ref),
        ):
            copy.wait()
            product = jnp.dot(scaled_ref[way], buf[way], preferred_element_type=f32)
            out[...] = (old if way == 0 else out)[...] + product
    gate = gate_ref[...] * factor
    up = up_ref[...] * factor
    activation_ref[...] = (gate / (1.0 + jnp.exp(-gate)) * up).astype(bf16)
    for way in range(ways):
        later[way].wait()
        product = jnp.dot(activation_ref[...], down_buf[way], preferred_element_type=f32)
        term_ref[way] = product.astype(bf16)


def gate_up_rest(part, rows, gains, w_gate, w_up, w_down, sums, width):
    ways, all_rows, quarter = rows.shape
    hidden = w_gate.shape[1]
    return pl.pallas_call(
        functools.partial(rest_kernel, width),
        out_shape=(
            jax.ShapeDtypeStruct((all_rows, hidden), bf16),
            jax.ShapeDtypeStruct((ways, all_rows, quarter), bf16),
        ),
        in_specs=[smem, vmem, vmem, vmem, vmem, vmem, hbm, hbm, hbm],
        out_specs=(vmem, vmem),
        scratch_shapes=[
            pltpu.VMEM((ways, quarter, hidden), bf16),
            pltpu.VMEM((ways, quarter, hidden), bf16),
            pltpu.VMEM((ways, hidden, quarter), bf16),
            pltpu.VMEM(rows.shape, bf16),
            pltpu.VMEM((all_rows, hidden), f32),
            pltpu.VMEM((all_rows, hidden), f32),
            pltpu.SemaphoreType.DMA((2, ways)),
            pltpu.SemaphoreType.DMA((ways,)),
        ],
        compiler_params=pltpu.CompilerParams(vmem_limit_bytes=40 << 20),
        cost_estimate=pl.CostEstimate(
            flops=6 * rows.size * hidden, bytes_accessed=6 * ways * quarter * hidden, transcendentals=0
        ),
        name="gate_up_rest",
    )(part.reshape(1), rows, gains, *sums, w_gate, w_up, w_down)


def down_kernel(part_ref, activation_ref, down_hbm, term_ref, down_buf, sems):
    ways, _, quarter = term_ref.shape
    copies = down_copies(part_ref[0], 0, ways, quarter, down_hbm, down_buf, sems)
    start_all(copies)
    for way in range(ways):
        copies[way].wait()
        product = jnp.dot(activation_ref[...], down_buf[way], preferred_element_type=f32)
        term_ref[way] = product.astype(bf16)


def down_half(part, activation, w_down, ways):
    all_rows, hidden = activation.shape
    quarter = w_down.shape[1] // (ways * CORES)
    return pl.pallas_call(
        down_kernel,
        out_shape=jax.ShapeDtypeStruct((ways, all_rows, quarter), bf16),
        in_specs=[smem, vmem, hbm],
        out_specs=vmem,
        scratch_shapes=[
            pltpu.VMEM((ways, hidden, quarter), bf16),
            pltpu.SemaphoreType.DMA((ways,)),
        ],
        compiler_params=pltpu.CompilerParams(vmem_limit_bytes=48 << 20),
        cost_estimate=pl.CostEstimate(
            flops=w_down.size * all_rows, bytes_accessed=w_down.size, transcendentals=0
        ),
        name="down_half",
    )(part.reshape(1), activation, w_down)


def sum_kernel(ways, across, own_ref, other_ref, *out_refs):
    all_rows, columns = own_ref.shape[1:]
    half = out_refs[0].shape[1]
    outs = iter(out_refs)
    height = all_rows // 2
    for row in (height, 0):
        for way in range(ways):
            at = (way, slice(row, row + height), slice(0, half))
            next(outs)[...] = (own_ref[at].astype(f32) + other_ref[at].astype(f32)).astype(bf16)
        step = height // across
        for k in range(across):
            out = next(outs)
            for way in range(ways):
                at = (way, slice(row + k * step, row + (k + 1) * step), slice(half, columns))
                out[way] = (own_ref[at].astype(f32) + other_ref[at].astype(f32)).astype(bf16)


def sum_terms(own, other, across, half):
    ways, all_rows, columns = own.shape
    height = all_rows // 2
    group = [jax.ShapeDtypeStruct((height, half), bf16)] * ways
    group = group + [jax.ShapeDtypeStruct((ways, height // across, columns - half), bf16)] * across
    outs = pl.pallas_call(
        functools.partial(sum_kernel, ways, across),
        out_shape=group + group,
        in_specs=[vmem, vmem],
        out_specs=[vmem] * (2 * len(group)),
        compiler_params=pltpu.CompilerParams(vmem_limit_bytes=8 << 20),
        cost_estimate=pl.CostEstimate(flops=own.size, bytes_accessed=6 * own.size, transcendentals=0),
        name="sum_terms",
    )(own, other)
    count = len(group)
    return [(part[:ways], part[ways:]) for part in (outs[:count], outs[count:])]


def local(
    token_inputs,
    attn_gain,
    w_query,
    key_projection,
    value_projection,
    w_output,
    mlp_gain,
    w_gate,
    w_up,
    w_down,
    key_cache,
    paged_value_cache,
    cache_lengths,
    page_request,
    page_number,
    request_slot,
):
    steps, row_count, width = token_inputs.shape
    seq, tp = lax.axis_size("seq"), lax.axis_size("tp")
    deep, across = split_axis(seq)
    ways, cores = tp // CORES, CORES
    page_count, kv_local, page_size, head_dim = key_cache.shape
    heads_per_group = w_query.shape[1] // (kv_local * head_dim)
    rows = steps * row_count
    pairs = row_count * kv_local
    me, part = lax.axis_index("seq"), lax.axis_index("tp")
    quarter = width // tp

    page_live = page_request >= 0
    request_ids = jnp.arange(request_slot.shape[0], dtype=jnp.int32)
    is_request = request_ids[None, :] == page_request[:, None]
    page_row = jnp.sum(jnp.where(is_request, request_slot[None, :], 0), axis=1)
    page_length = jnp.sum(jnp.where(is_request, cache_lengths[None, :], 0), axis=1)
    valid = jnp.where(page_live, jnp.clip(page_length - page_number * page_size, 0, page_size), 0)
    mask = (page_row // row_count) ^ me
    slots = ((mask % across) * deep + mask // across) * row_count + page_row % row_count

    query, normalized, cosine, sine = project_queries(
        me, request_slot, cache_lengths, token_inputs, attn_gain, w_query, kv_local, head_dim
    )
    shared = [query] + [swap(query, "seq", across * k) for k in range(1, deep)]
    shared = jnp.concatenate(shared, axis=0)
    queries = [shared] + [swap(shared, "seq", k) for k in range(1, across)]
    queries = jnp.concatenate(queries, axis=0)

    normalized, shared = lax.optimization_barrier((normalized, shared))
    fresh_keys, fresh_values = project_fresh(
        normalized, cosine, sine, key_projection, value_projection, kv_local, head_dim
    )

    packed = attend_pages(
        queries,
        fresh_keys,
        fresh_values,
        key_cache,
        paged_value_cache,
        slots,
        valid,
        seq,
    )
    sides = [packed[:deep]] + [swap(packed[k * deep : (k + 1) * deep], "seq", k) for k in range(1, across)]
    merged = merge_parts(sides)
    layers = [merged[:1]] + [swap(merged[k : k + 1], "seq", across * k) for k in range(1, deep)]
    own_input = lax.dynamic_slice_in_dim(token_inputs.reshape(rows, width), part * quarter, quarter, 1)
    own_term, terms = project_out(part, layers, own_input, w_output, tp, kv_local)
    total = own_term
    for slot in range(1, tp):
        total = total + swap(terms[slot - 1], "tp", slot).astype(f32)
    own_attended = total.astype(bf16)

    half = (quarter + 255) // 256 * 128
    count = deep // 2

    def along_x(value):
        return [value] + [swap(value, "seq", k) for k in range(1, across)]

    def along_y(value):
        return [value] + [swap(value, "tp", CORES * k) for k in range(1, ways)]

    def spread_first(group):
        first, second = group[:, :half], group[:, half:]
        return along_x(first), along_y(second)

    def spread_second(first, second):
        return along_y(jnp.concatenate(first, axis=0)) + along_x(jnp.stack(second))

    far = [swap(own_attended, "seq", across * k) for k in range(count, deep)]
    near = [own_attended] + [swap(own_attended, "seq", across * k) for k in range(1, count)]
    near = spread_first(jnp.concatenate(near, axis=0))
    near, far = lax.optimization_barrier((near, far))
    near = spread_second(*near)
    far = spread_second(*spread_first(jnp.concatenate(far, axis=0)))
    both = join_groups(near, far, ways)
    other = swap(both, "tp", 1)
    all_rows = both.shape[1]

    def assemble(pieces, height):
        whole = jnp.zeros((height, width), bf16)
        for slot, piece in enumerate(pieces):
            whole = lax.dynamic_update_slice_in_dim(whole, piece, (part ^ slot) * quarter, 1)
        return whole

    gains = mlp_gain.reshape(tp, 1, quarter)
    sums = gate_up_half(part, 0, both, gains, w_gate, w_up)
    activation, other_terms = gate_up_rest(part, other, gains, w_gate, w_up, w_down, sums, width)
    received = swap(other_terms, "tp", 1)
    own_terms = down_half(part, activation, w_down, ways)
    far, near = sum_terms(own_terms, received, across, half)
    own_pieces = [piece[k, :rows] for k in range(ways) for piece in (both, other)]
    attended = assemble(own_pieces, rows).reshape(steps, row_count, width)

    def add(first, others):
        value = first.astype(f32)
        for one in others:
            value = value + one.astype(f32)
        return value

    def collect_group(first, second):
        first = add(first[0], [swap(first[k], "tp", CORES * k) for k in range(1, ways)]).astype(bf16)
        second = add(second[0], [swap(second[k], "seq", k) for k in range(1, across)]).astype(bf16)
        first = first.reshape(across, -1, half)
        first = add(first[0], [swap(first[k], "seq", k) for k in range(1, across)]).astype(bf16)
        second = add(second[0], [swap(second[k], "tp", CORES * k) for k in range(1, ways)]).astype(bf16)
        return jnp.concatenate([first, second], axis=1).reshape(-1, rows, quarter)

    far = collect_group(*far)
    near = collect_group(*near)
    far = [swap(far[k], "seq", across * (count + k)) for k in range(deep - count)]
    near = [near[0]] + [swap(near[k], "seq", across * k) for k in range(1, count)]
    mlp_result = add(near[0], near[1:] + far)
    own_out = (own_attended.astype(f32) + mlp_result).astype(bf16)
    pieces = [own_out] + [swap(own_out, "tp", slot) for slot in range(1, tp)]
    layer_out = assemble(pieces, rows).reshape(steps, row_count, width)
    return attended, layer_out


def solution(mesh):
    in_specs = (
        P(None, "seq", None),
        P(),
        P(None, "tp"),
        P(None, "tp"),
        P(None, "tp"),
        P("tp", None),
        P(),
        P(None, ("seq", "tp")),
        P(None, ("seq", "tp")),
        P(("seq", "tp"), None),
        P("seq", "tp", None, None),
        P("seq", "tp", None, None),
        P(),
        P("seq"),
        P("seq"),
        P(),
    )
    out_specs = (P(None, "seq", None), P(None, "seq", None))
    return jax.shard_map(local, mesh=mesh, in_specs=in_specs, out_specs=out_specs, check_vma=False)
```

```python
import functools

import jax
import jax.numpy as jnp
from jax import lax
from jax.experimental import pallas as pl
from jax.experimental.pallas import tpu as pltpu
from jax.sharding import PartitionSpec as P

STEPS = 4
CORES = 2

rope_theta = 100000000.0
norm_eps = 1e-05
masked_low = -1e30
f32 = jnp.float32
bf16 = jnp.bfloat16


def split_axis(size):
    fast = 1
    while fast * fast * 4 <= size:
        fast *= 2
    return size // fast, fast


def swap(value, axis, mask):
    size = lax.axis_size(axis)
    return lax.ppermute(value, axis, [(i, i ^ mask) for i in range(size)])


def cross(value, x_first, k):
    seq, tp = lax.axis_size("seq"), lax.axis_size("tp")
    pairs = []
    for s in range(seq):
        for t in range(tp):
            along_x = (t % CORES == 0) == x_first
            partner = (s ^ k) * tp + t if along_x else s * tp + (t ^ (CORES * k))
            pairs.append((s * tp + t, partner))
    return lax.ppermute(value, ("seq", "tp"), pairs)


def dot_t(a, b):
    return lax.dot_general(a, b, (((1,), (1,)), ((), ())), preferred_element_type=f32)


def round_trip(value):
    return value.astype(bf16).astype(f32)


def encode_stats(top, total, pairs):
    pieces = []
    rest = top
    for _ in range(3):
        piece = round_trip(rest)
        pieces.append(piece)
        rest = rest - piece
    rest = total
    for _ in range(2):
        piece = round_trip(rest)
        pieces.append(piece)
        rest = rest - piece
    tile = pieces[0]
    for i in range(1, 5):
        tile = tile + pltpu.roll(pieces[i], i * pairs, 1)
    return tile.astype(bf16)


def decode_stats(tile, pairs):
    values = tile.astype(f32)
    lanes = values.shape[1]
    shifted = [values] + [pltpu.roll(values, lanes - i * pairs, 1) for i in range(1, 5)]
    top = shifted[0] + shifted[1] + shifted[2]
    total = shifted[3] + shifted[4]
    return top, total


def softmax_parts(scores, live, scale):
    scores = [jnp.where(keep, score * scale, masked_low) for score, keep in zip(scores, live)]
    tops = [jnp.max(score, axis=1, keepdims=True) for score in scores]
    weights = [jnp.where(keep, jnp.exp(score - top), 0.0) for score, top, keep in zip(scores, tops, live)]
    totals = [jnp.sum(weight, axis=1, keepdims=True) for weight in weights]
    return tops, totals, [weight.astype(bf16) for weight in weights]


def pages_kernel(block_pages, piece_count, near_count, slot_ref, valid_ref, *refs):
    pieces = refs[:piece_count]
    key_buf, value_buf, _ = refs[piece_count : piece_count + 3]
    outs = refs[piece_count + 3 : -4]
    query_ref, top_ref, total_ref, acc_ref = refs[-4:]
    page_count, kv_local, page_size, head_dim = key_buf.shape
    blocks = page_count // block_pages
    pairs = outs[0].shape[1] - 1
    deep = pieces[0].shape[0] // pairs
    rows = query_ref.shape[1]
    scale = head_dim ** (-0.5)

    top_ref[...] = jnp.full(top_ref.shape, masked_low, f32)
    total_ref[...] = jnp.zeros(total_ref.shape, f32)
    acc_ref[...] = jnp.zeros(acc_ref.shape, f32)
    for i, piece in enumerate(pieces):
        query_ref[i * deep * pairs : (i + 1) * deep * pairs] = piece[...]
    lane = lax.broadcasted_iota(jnp.int32, (rows, page_size), 1)

    @pl.loop(0, blocks)
    def _(block):
        pages = [block * block_pages + i for i in range(block_pages)]
        places = [(page, head) for page in pages for head in range(kv_local)]
        at = [slot_ref[page] * kv_local + head for page, head in places]
        live = [lane < valid_ref[page] for page, _ in places]
        scores = [dot_t(query_ref[i], key_buf[page, head]) for i, (page, head) in zip(at, places)]
        tops, totals, weights = softmax_parts(scores, live, scale)
        accs = [
            jnp.dot(weight, value_buf[page, head], preferred_element_type=f32)
            for weight, (page, head) in zip(weights, places)
        ]
        for i, top, total, acc in zip(at, tops, totals, accs):
            old_top = top_ref[i]
            new_top = jnp.maximum(old_top, top)
            old_factor = jnp.exp(old_top - new_top)
            factor = jnp.exp(top - new_top)
            top_ref[i] = new_top
            total_ref[i] = total_ref[i] * old_factor + total * factor
            acc_ref[i] = acc_ref[i] * old_factor + acc * factor

    out_lane = lax.broadcasted_iota(jnp.int32, (rows, head_dim), 1)
    for number, out_ref in enumerate(outs):
        start = number % piece_count * deep + (near_count if number >= piece_count else 0)

        @pl.loop(0, out_ref.shape[0])
        def _(group):
            tops = jnp.zeros((rows, head_dim), f32)
            totals = jnp.zeros((rows, head_dim), f32)
            for i in range(pairs):
                at = (start + group) * pairs + i
                out_ref[group, i] = acc_ref[at].astype(bf16)
                tops = jnp.where(out_lane == i, top_ref[at], tops)
                totals = jnp.where(out_lane == i, total_ref[at], totals)
            out_ref[group, pairs] = encode_stats(tops, totals, pairs)


def attend_pages(pieces, key_cache, value_cache, slots, valid, near_count, pairs, after):
    height, rows, head_dim = pieces[0].shape
    deep = height // pairs
    page_count, kv_local, page_size, _ = key_cache.shape
    block_pages = 6
    while page_count % block_pages:
        block_pages -= 1
    count = height * len(pieces)
    outs = pl.pallas_call(
        functools.partial(pages_kernel, block_pages, len(pieces), near_count),
        out_shape=[
            jax.ShapeDtypeStruct((layers, pairs + 1, rows, head_dim), bf16)
            for layers in (near_count, deep - near_count)
            for _ in pieces
        ],
        in_specs=[smem, smem] + [vmem] * (len(pieces) + 2) + [hbm],
        out_specs=[vmem] * (2 * len(pieces)),
        scratch_shapes=[
            pltpu.VMEM((count, rows, head_dim), bf16),
            pltpu.VMEM((count, rows, head_dim), f32),
            pltpu.VMEM((count, rows, head_dim), f32),
            pltpu.VMEM((count, rows, head_dim), f32),
        ],
        compiler_params=pltpu.CompilerParams(vmem_limit_bytes=14 << 20),
        cost_estimate=pl.CostEstimate(
            flops=4 * rows * page_count * kv_local * page_size * head_dim,
            bytes_accessed=4 * page_count * kv_local * page_size * head_dim,
            transcendentals=0,
        ),
        name="attend_pages",
    )(slots, valid, *pieces, key_cache, value_cache, after)
    return outs[: len(pieces)], outs[len(pieces) :]


def merge_tile(parts, group, pairs):
    stats = [decode_stats(part[group, pairs], pairs) for part in parts]
    top = functools.reduce(jnp.maximum, [s[0] for s in stats])
    factors = [jnp.exp(s[0] - top) for s in stats]
    total = functools.reduce(jnp.add, [s[1] * f for s, f in zip(stats, factors)])
    return top, total, factors


def merge_pair(parts, factors, group, i):
    return functools.reduce(
        jnp.add, [part[group, i].astype(f32) * f[:, i : i + 1] for part, f in zip(parts, factors)]
    )


def merge_kernel(count, *refs):
    parts, outs = refs[:count], refs[count:]
    _, tiles, rows, head_dim = parts[0].shape
    pairs = tiles - 1
    used = lax.broadcasted_iota(jnp.int32, (rows, head_dim), 1) < pairs
    for group, out_ref in enumerate(outs):
        top, total, factors = merge_tile(parts, group, pairs)
        for i in range(pairs):
            out_ref[0, i] = merge_pair(parts, factors, group, i).astype(bf16)
        out_ref[0, pairs] = encode_stats(jnp.where(used, top, 0.0), jnp.where(used, total, 0.0), pairs)


vmem = pl.BlockSpec(memory_space=pltpu.VMEM)
smem = pl.BlockSpec(memory_space=pltpu.SMEM)
hbm = pl.BlockSpec(memory_space=pl.ANY)


def merge_parts(parts):
    groups, *tile = parts[0].shape
    return pl.pallas_call(
        functools.partial(merge_kernel, len(parts)),
        out_shape=[jax.ShapeDtypeStruct((1, *tile), bf16)] * groups,
        in_specs=[vmem] * len(parts),
        out_specs=[vmem] * groups,
        compiler_params=pltpu.CompilerParams(vmem_limit_bytes=8 << 20),
        name="merge_parts",
    )(*parts)


def columns_of(ref, index, size):
    return ref[:, pl.ds(pl.multiple_of(index * size, size), size)]


def rows_of(ref, index, size):
    return ref[pl.ds(pl.multiple_of(index * size, size), size), :]


def start_all(copies):
    for copy in copies:
        copy.start()


def query_kernel(
    kv_local, me_ref, slots_ref, lengths_ref, input_ref, gain_ref, weight_hbm,
    query_ref, normalized_ref, cosine_ref, sine_ref, weight_buf, total_ref, tile_ref, sems,
):
    steps, row_count, width = input_ref.shape
    head_dim = cosine_ref.shape[1]
    heads = weight_buf.shape[1] // head_dim
    group = heads // kv_local
    chunks = sems.shape[0]
    depth = width // chunks
    copies = []
    for chunk in range(chunks):
        at = pl.ds(chunk * depth, depth)
        copies.append(pltpu.make_async_copy(weight_hbm.at[at], weight_buf.at[at], sems.at[chunk]))
    start_all(copies)

    gain = gain_ref[...]
    for step in range(0, steps, 2):
        pair = []
        for at in (step, step + 1):
            floats = input_ref[at].astype(f32)
            mean = jnp.mean(floats * floats, axis=1, keepdims=True)
            pair.append(floats * lax.rsqrt(mean + norm_eps) * gain)
        normalized_ref[step * row_count : (step + 2) * row_count] = jnp.concatenate(pair, axis=0).astype(bf16)

    requests = slots_ref.shape[1]
    own = me_ref[0] * row_count + lax.broadcasted_iota(jnp.int32, (row_count, requests), 0)
    length = jnp.sum(jnp.where(slots_ref[...] == own, lengths_ref[...], 0), axis=1, keepdims=True)
    half = head_dim // 2
    lane = lax.broadcasted_iota(jnp.int32, (row_count, head_dim), 1)
    exponent = jnp.where(lane < half, lane, lane - half).astype(f32) * (2.0 / head_dim)
    inverse_freq = rope_theta ** (-exponent)
    for step in range(steps):
        angles = (length + step).astype(f32) * inverse_freq
        sine = jnp.sin(angles)
        cosine_ref[step * row_count : (step + 1) * row_count] = jnp.cos(angles)
        sine_ref[step * row_count : (step + 1) * row_count] = jnp.where(lane < half, -sine, sine)

    for chunk, copy in enumerate(copies):
        copy.wait()
        at = slice(chunk * depth, (chunk + 1) * depth)
        product = jnp.dot(normalized_ref[:, at], weight_buf[at], preferred_element_type=f32)
        total_ref[...] = product if chunk == 0 else total_ref[...] + product

    cosine, sine = cosine_ref[...], sine_ref[...]
    tile_rows = steps * group
    for head in range(heads):
        value = total_ref[:, head * head_dim : (head + 1) * head_dim]
        value = value * cosine + pltpu.roll(value, half, 1) * sine
        for step in range(steps):
            first = head // group * tile_rows + step * group + head % group
            tile_ref[pl.ds(first, row_count, stride=kv_local * tile_rows), :] = value[
                step * row_count : (step + 1) * row_count
            ]
    query_ref[...] = tile_ref[...].reshape(query_ref.shape).astype(bf16)


def project_queries(me, request_slot, cache_lengths, token_inputs, gain, weight, kv_local, head_dim):
    steps, row_count, width = token_inputs.shape
    rows = steps * row_count
    columns = weight.shape[1]
    tile_rows = columns // (kv_local * head_dim) * steps
    pairs = row_count * kv_local
    chunks = 4
    return pl.pallas_call(
        functools.partial(query_kernel, kv_local),
        out_shape=(
            jax.ShapeDtypeStruct((pairs, tile_rows, head_dim), bf16),
            jax.ShapeDtypeStruct((rows, width), bf16),
            jax.ShapeDtypeStruct((rows, head_dim), f32),
            jax.ShapeDtypeStruct((rows, head_dim), f32),
        ),
        in_specs=[smem, vmem, vmem, vmem, vmem, hbm],
        out_specs=(vmem, vmem, vmem, vmem),
        scratch_shapes=[
            pltpu.VMEM((width, columns), bf16),
            pltpu.VMEM((rows, columns), f32),
            pltpu.VMEM((pairs * tile_rows, head_dim), f32),
            pltpu.SemaphoreType.DMA((chunks,)),
        ],
        compiler_params=pltpu.CompilerParams(vmem_limit_bytes=52 << 20),
        cost_estimate=pl.CostEstimate(
            flops=2 * rows * width * columns, bytes_accessed=2 * width * columns, transcendentals=0
        ),
        name="project_queries",
    )(
        me.reshape(1),
        request_slot.reshape(1, -1),
        cache_lengths.reshape(1, -1),
        token_inputs,
        gain.reshape(1, width),
        weight,
    )


def recent_kernel(
    kv_local, normalized_ref, cosine_ref, sine_ref, query_ref, key_hbm, value_hbm,
    out_ref, key_buf, value_buf, key_tile, value_tile, sems,
):
    rows, width = normalized_ref.shape
    head_dim = cosine_ref.shape[1]
    row_count = rows // STEPS
    pairs, tile_rows, _ = query_ref.shape
    pads = key_tile.shape[0] // pairs
    copies = [
        pltpu.make_async_copy(key_hbm, key_buf, sems.at[0]),
        pltpu.make_async_copy(value_hbm, value_buf, sems.at[1]),
    ]
    start_all(copies)
    key_tile[...] = jnp.zeros(key_tile.shape, f32)
    value_tile[...] = jnp.zeros(value_tile.shape, f32)
    cosine, sine = cosine_ref[...], sine_ref[...]
    for copy, buf, tile in ((copies[0], key_buf, key_tile), (copies[1], value_buf, value_tile)):
        copy.wait()
        product = jnp.dot(normalized_ref[...], buf[...], preferred_element_type=f32)
        for head in range(kv_local):
            value = product[:, head * head_dim : (head + 1) * head_dim]
            if buf is key_buf:
                value = value * cosine + pltpu.roll(value, head_dim // 2, 1) * sine
            for step in range(STEPS):
                tile[pl.ds(head * pads + step, row_count, stride=kv_local * pads), :] = value[
                    step * row_count : (step + 1) * row_count
                ]
    keys = key_tile[...].reshape(pairs, pads, head_dim).astype(bf16)
    values = value_tile[...].reshape(pairs, pads, head_dim).astype(bf16)
    row_step = lax.broadcasted_iota(jnp.int32, (tile_rows, pads), 0) // (tile_rows // STEPS)
    column = lax.broadcasted_iota(jnp.int32, (tile_rows, pads), 1)
    scores = [dot_t(query_ref[i], keys[i]) for i in range(pairs)]
    tops, totals, weights = softmax_parts(scores, [column <= row_step] * pairs, head_dim ** (-0.5))
    accs = [jnp.dot(weights[i], values[i], preferred_element_type=f32) for i in range(pairs)]
    lane = lax.broadcasted_iota(jnp.int32, (tile_rows, head_dim), 1)
    all_tops = jnp.zeros((tile_rows, head_dim), f32)
    all_totals = jnp.zeros((tile_rows, head_dim), f32)
    for i in range(pairs):
        out_ref[0, i] = accs[i].astype(bf16)
        all_tops = jnp.where(lane == i, tops[i], all_tops)
        all_totals = jnp.where(lane == i, totals[i], all_totals)
    out_ref[0, pairs] = encode_stats(all_tops, all_totals, pairs)


def recent_part(normalized, cosine, sine, query, key_projection, value_projection, kv_local, head_dim):
    rows, width = normalized.shape
    pairs, tile_rows, _ = query.shape
    pads = 16
    columns = key_projection.shape[1]
    return pl.pallas_call(
        functools.partial(recent_kernel, kv_local),
        out_shape=jax.ShapeDtypeStruct((1, pairs + 1, tile_rows, head_dim), bf16),
        in_specs=[vmem, vmem, vmem, vmem, hbm, hbm],
        out_specs=vmem,
        scratch_shapes=[
            pltpu.VMEM((width, columns), bf16),
            pltpu.VMEM((width, columns), bf16),
            pltpu.VMEM((pairs * pads, head_dim), f32),
            pltpu.VMEM((pairs * pads, head_dim), f32),
            pltpu.SemaphoreType.DMA((2,)),
        ],
        compiler_params=pltpu.CompilerParams(vmem_limit_bytes=50 << 20),
        cost_estimate=pl.CostEstimate(
            flops=4 * rows * width * columns, bytes_accessed=4 * width * columns, transcendentals=0
        ),
        name="recent_part",
    )(normalized, cosine, sine, query, key_projection, value_projection)


def out_kernel(
    count, kv_local, part_ref, input_ref, weight_hbm, *refs
):
    parts = refs[:count]
    own_ref, term_ref, weight_buf, tile_ref, attention_ref, sems = refs[count:]
    tp = sems.shape[0]
    quarter = own_ref.shape[1]
    part = part_ref[0]
    copies = []
    for slot in range(tp):
        at = pl.multiple_of((part ^ slot) * quarter, quarter)
        copies.append(
            pltpu.make_async_copy(
                weight_hbm.at[:, pl.ds(at, quarter)], weight_buf.at[slot], sems.at[slot]
            )
        )
    order = list(range(1, tp)) + [0]
    start_all([copies[slot] for slot in order])

    _, tiles, tile_rows, head_dim = parts[0].shape
    pairs = tiles - 1
    row_count = pairs // kv_local
    group = tile_rows // STEPS
    _, total, factors = merge_tile(parts, 0, pairs)
    inverse = 1.0 / total
    factors = [f * inverse for f in factors]
    for i in range(pairs):
        acc = merge_pair(parts, factors, 0, i)
        request, head = i // kv_local, i % kv_local
        for row in range(tile_rows):
            step, member = row // group, row % group
            column = (head * group + member) * head_dim
            at = step * row_count + request
            tile_ref[at : at + 1, column : column + head_dim] = acc[row : row + 1]
    attention_ref[...] = tile_ref[...].astype(bf16)
    for slot in order:
        copies[slot].wait()
        product = jnp.dot(attention_ref[...], weight_buf[slot], preferred_element_type=f32)
        if slot == 0:
            own_ref[...] = input_ref[...].astype(f32) + product
        else:
            term_ref[slot - 1] = product.astype(bf16)


def project_out(part, parts, own_input, weight, tp, kv_local):
    rows, quarter = own_input.shape
    depth = weight.shape[0]
    return pl.pallas_call(
        functools.partial(out_kernel, len(parts), kv_local),
        out_shape=(
            jax.ShapeDtypeStruct((rows, quarter), f32),
            jax.ShapeDtypeStruct((tp - 1, rows, quarter), bf16),
        ),
        in_specs=[smem, vmem, hbm] + [vmem] * len(parts),
        out_specs=(vmem, vmem),
        scratch_shapes=[
            pltpu.VMEM((tp, depth, quarter), bf16),
            pltpu.VMEM((rows, depth), f32),
            pltpu.VMEM((rows, depth), bf16),
            pltpu.SemaphoreType.DMA((tp,)),
        ],
        compiler_params=pltpu.CompilerParams(vmem_limit_bytes=50 << 20),
        cost_estimate=pl.CostEstimate(
            flops=2 * rows * weight.size, bytes_accessed=2 * weight.size, transcendentals=0
        ),
        name="project_out",
    )(part.reshape(1), own_input, weight, *parts)


def places(part, count):
    core = part % CORES
    for first in range(count):
        for second in range(count):
            way = jnp.where(core == 0, second, first)
            column = jnp.where(core == 0, first, second)
            yield first, second, way, column


def places(part, count):
    core = part % CORES
    for first in range(count):
        for second in range(count):
            way = jnp.where(core == 0, second, first)
            column = jnp.where(core == 0, first, second)
            yield first, second, way, column


def join_kernel(ways, near_count, *refs):
    out_ref = refs[-1]
    half = refs[0].shape[1]
    row = 0
    for group in range(2):
        pieces = refs[group * near_count : (group + 1) * near_count]
        height = pieces[0].shape[0]
        for way in range(ways):
            out_ref[way, row : row + height, :half] = pieces[way][...]
        at = row
        for piece in pieces[ways:]:
            out_ref[:, at : at + piece.shape[1], half:] = piece[...]
            at += piece.shape[1]
        row += height


def join_groups(near, far, ways):
    pieces = near + far
    columns = pieces[0].shape[1] + pieces[ways].shape[2]
    all_rows = near[0].shape[0] + far[0].shape[0]
    return pl.pallas_call(
        functools.partial(join_kernel, ways, len(near)),
        out_shape=jax.ShapeDtypeStruct((ways, all_rows, columns), bf16),
        in_specs=[vmem] * len(pieces),
        out_specs=vmem,
        compiler_params=pltpu.CompilerParams(vmem_limit_bytes=8 << 20),
        cost_estimate=pl.CostEstimate(
            flops=0, bytes_accessed=4 * ways * all_rows * columns, transcendentals=0
        ),
        name="join_groups",
    )(*pieces)


def gate_up_copies(part, core, ways, quarter, gate_hbm, up_hbm, gate_buf, up_buf, sems):
    copies = []
    for way in range(ways):
        at = pl.multiple_of((part ^ (way * CORES + core)) * quarter, quarter)
        copies.append(
            pltpu.make_async_copy(gate_hbm.at[pl.ds(at, quarter)], gate_buf.at[way], sems.at[0, way])
        )
        copies.append(pltpu.make_async_copy(up_hbm.at[pl.ds(at, quarter)], up_buf.at[way], sems.at[1, way]))
    return copies


def scaled_rows(part, core, way, rows_ref, gain_ref):
    floats = rows_ref[way].astype(f32)
    squares = jnp.sum(floats * floats, axis=1, keepdims=True)
    return (floats * gain_ref[part ^ (way * CORES + core)]).astype(bf16), squares


def gate_up_kernel(
    core, part_ref, rows_ref, gain_ref, gate_hbm, up_hbm, gate_ref, up_ref, square_ref,
    gate_buf, up_buf, scaled_ref, sems,
):
    ways, _, quarter = rows_ref.shape
    part = part_ref[0]
    copies = gate_up_copies(part, core, ways, quarter, gate_hbm, up_hbm, gate_buf, up_buf, sems)
    start_all(copies)
    square = 0.0
    for way in range(ways):
        scaled, squares = scaled_rows(part, core, way, rows_ref, gain_ref)
        scaled_ref[way] = scaled
        square = square + squares
    square_ref[...] = jnp.broadcast_to(square, square_ref.shape)
    for way in range(ways):
        for copy, buf, out in (
            (copies[2 * way], gate_buf, gate_ref),
            (copies[2 * way + 1], up_buf, up_ref),
        ):
            copy.wait()
            product = jnp.dot(scaled_ref[way], buf[way], preferred_element_type=f32)
            out[...] = product if way == 0 else out[...] + product


def gate_up_half(part, core, rows, gains, w_gate, w_up):
    ways, all_rows, quarter = rows.shape
    hidden = w_gate.shape[1]
    return pl.pallas_call(
        functools.partial(gate_up_kernel, core),
        out_shape=(
            jax.ShapeDtypeStruct((all_rows, hidden), f32),
            jax.ShapeDtypeStruct((all_rows, hidden), f32),
            jax.ShapeDtypeStruct((all_rows, 128), f32),
        ),
        in_specs=[smem, vmem, vmem, hbm, hbm],
        out_specs=(vmem, vmem, vmem),
        scratch_shapes=[
            pltpu.VMEM((ways, quarter, hidden), bf16),
            pltpu.VMEM((ways, quarter, hidden), bf16),
            pltpu.VMEM(rows.shape, bf16),
            pltpu.SemaphoreType.DMA((2, ways)),
        ],
        compiler_params=pltpu.CompilerParams(vmem_limit_bytes=46 << 20),
        cost_estimate=pl.CostEstimate(
            flops=4 * rows.size * hidden,
            bytes_accessed=4 * ways * quarter * hidden + 8 * all_rows * hidden,
            transcendentals=0,
        ),
        name="gate_up_half",
    )(part.reshape(1), rows, gains, w_gate, w_up)


def down_copies(part, core, ways, quarter, down_hbm, down_buf, sems):
    copies = []
    for way in range(ways):
        at = pl.multiple_of((part ^ (way * CORES + core)) * quarter, quarter)
        copies.append(
            pltpu.make_async_copy(down_hbm.at[:, pl.ds(at, quarter)], down_buf.at[way], sems.at[way])
        )
    return copies


def rest_kernel(
    width, part_ref, rows_ref, gain_ref, old_gate_ref, old_up_ref, square_ref, gate_hbm, up_hbm, down_hbm,
    activation_ref, term_ref, gate_buf, up_buf, down_buf, scaled_ref, gate_ref, up_ref, sems, down_sems,
):
    ways, _, quarter = rows_ref.shape
    part = part_ref[0]
    copies = gate_up_copies(part, 1, ways, quarter, gate_hbm, up_hbm, gate_buf, up_buf, sems)
    later = down_copies(part, 1, ways, quarter, down_hbm, down_buf, down_sems)
    start_all(copies + later)
    square = square_ref[:, :1]
    for way in range(ways):
        scaled, squares = scaled_rows(part, 1, way, rows_ref, gain_ref)
        scaled_ref[way] = scaled
        square = square + squares
    factor = lax.rsqrt(square * (1.0 / width) + norm_eps)
    for way in range(ways):
        for copy, buf, old, out in (
            (copies[2 * way], gate_buf, old_gate_ref, gate_ref),
            (copies[2 * way + 1], up_buf, old_up_ref, up_ref),
        ):
            copy.wait()
            product = jnp.dot(scaled_ref[way], buf[way], preferred_element_type=f32)
            out[...] = (old if way == 0 else out)[...] + product
    gate = gate_ref[...] * factor
    up = up_ref[...] * factor
    activation_ref[...] = (gate / (1.0 + jnp.exp(-gate)) * up).astype(bf16)
    for way in range(ways):
        later[way].wait()
        product = jnp.dot(activation_ref[...], down_buf[way], preferred_element_type=f32)
        term_ref[way] = product.astype(bf16)


def gate_up_rest(part, rows, gains, w_gate, w_up, w_down, sums, width):
    ways, all_rows, quarter = rows.shape
    hidden = w_gate.shape[1]
    return pl.pallas_call(
        functools.partial(rest_kernel, width),
        out_shape=(
            jax.ShapeDtypeStruct((all_rows, hidden), bf16),
            jax.ShapeDtypeStruct((ways, all_rows, quarter), bf16),
        ),
        in_specs=[smem, vmem, vmem, vmem, vmem, vmem, hbm, hbm, hbm],
        out_specs=(vmem, vmem),
        scratch_shapes=[
            pltpu.VMEM((ways, quarter, hidden), bf16),
            pltpu.VMEM((ways, quarter, hidden), bf16),
            pltpu.VMEM((ways, hidden, quarter), bf16),
            pltpu.VMEM(rows.shape, bf16),
            pltpu.VMEM((all_rows, hidden), f32),
            pltpu.VMEM((all_rows, hidden), f32),
            pltpu.SemaphoreType.DMA((2, ways)),
            pltpu.SemaphoreType.DMA((ways,)),
        ],
        compiler_params=pltpu.CompilerParams(vmem_limit_bytes=40 << 20),
        cost_estimate=pl.CostEstimate(
            flops=6 * rows.size * hidden, bytes_accessed=6 * ways * quarter * hidden, transcendentals=0
        ),
        name="gate_up_rest",
    )(part.reshape(1), rows, gains, *sums, w_gate, w_up, w_down)


def down_kernel(part_ref, activation_ref, down_hbm, term_ref, down_buf, sems):
    ways, _, quarter = term_ref.shape
    copies = down_copies(part_ref[0], 0, ways, quarter, down_hbm, down_buf, sems)
    start_all(copies)
    for way in range(ways):
        copies[way].wait()
        product = jnp.dot(activation_ref[...], down_buf[way], preferred_element_type=f32)
        term_ref[way] = product.astype(bf16)


def down_half(part, activation, w_down, ways):
    all_rows, hidden = activation.shape
    quarter = w_down.shape[1] // (ways * CORES)
    return pl.pallas_call(
        down_kernel,
        out_shape=jax.ShapeDtypeStruct((ways, all_rows, quarter), bf16),
        in_specs=[smem, vmem, hbm],
        out_specs=vmem,
        scratch_shapes=[
            pltpu.VMEM((ways, hidden, quarter), bf16),
            pltpu.SemaphoreType.DMA((ways,)),
        ],
        compiler_params=pltpu.CompilerParams(vmem_limit_bytes=48 << 20),
        cost_estimate=pl.CostEstimate(
            flops=w_down.size * all_rows, bytes_accessed=w_down.size, transcendentals=0
        ),
        name="down_half",
    )(part.reshape(1), activation, w_down)


def sum_kernel(part_ref, own_ref, other_ref, *out_refs):
    count, all_rows, _ = own_ref.shape
    height = all_rows // 2
    step = height // count
    for group, row in enumerate((height, 0)):
        outs = out_refs[group * count : (group + 1) * count]
        for second, first, way, column in places(part_ref[0], count):
            at = pl.ds(pl.multiple_of(row + column * step, 16), step)
            total = own_ref[way, at, :].astype(f32) + other_ref[way, at, :].astype(f32)
            outs[first][second * step : (second + 1) * step, :] = total.astype(bf16)


def sum_terms(part, own, other):
    count, all_rows, columns = own.shape
    outs = pl.pallas_call(
        sum_kernel,
        out_shape=[jax.ShapeDtypeStruct((all_rows // 2, columns), bf16)] * (2 * count),
        in_specs=[smem, vmem, vmem],
        out_specs=[vmem] * (2 * count),
        compiler_params=pltpu.CompilerParams(vmem_limit_bytes=8 << 20),
        cost_estimate=pl.CostEstimate(flops=own.size, bytes_accessed=6 * own.size, transcendentals=0),
        name="sum_terms",
    )(part.reshape(1), own, other)
    return outs[:count], outs[count:]


def assemble_kernel(part_ref, *refs):
    out_ref = refs[-1]
    height = out_ref.shape[0]
    if len(refs[0].shape) == 3:
        pieces = [ref.at[way] for way in range(refs[0].shape[0]) for ref in refs[:-1]]
    else:
        pieces = refs[:-1]
    quarter = pieces[0].shape[1]
    for slot, piece in enumerate(pieces):
        at = pl.multiple_of((part_ref[0] ^ slot) * quarter, quarter)
        out_ref[:, pl.ds(at, quarter)] = piece[:height, :]


def assemble(part, height, pieces):
    shares = sum(piece.shape[0] if piece.ndim == 3 else 1 for piece in pieces)
    return pl.pallas_call(
        assemble_kernel,
        out_shape=jax.ShapeDtypeStruct((height, shares * pieces[0].shape[-1]), bf16),
        in_specs=[smem] + [vmem] * len(pieces),
        out_specs=vmem,
        compiler_params=pltpu.CompilerParams(vmem_limit_bytes=8 << 20),
        name="assemble",
    )(part.reshape(1), *pieces)


def local(
    token_inputs,
    attn_gain,
    w_query,
    key_projection,
    value_projection,
    w_output,
    mlp_gain,
    w_gate,
    w_up,
    w_down,
    key_cache,
    paged_value_cache,
    cache_lengths,
    page_request,
    page_number,
    request_slot,
):
    steps, row_count, width = token_inputs.shape
    seq, tp = lax.axis_size("seq"), lax.axis_size("tp")
    deep, across = split_axis(seq)
    ways, cores = tp // CORES, CORES
    page_count, kv_local, page_size, head_dim = key_cache.shape
    heads_per_group = w_query.shape[1] // (kv_local * head_dim)
    rows = steps * row_count
    pairs = row_count * kv_local
    me, part = lax.axis_index("seq"), lax.axis_index("tp")
    quarter = width // tp

    page_live = page_request >= 0
    request_ids = jnp.arange(request_slot.shape[0], dtype=jnp.int32)
    is_request = request_ids[None, :] == page_request[:, None]
    page_row = jnp.sum(jnp.where(is_request, request_slot[None, :], 0), axis=1)
    page_length = jnp.sum(jnp.where(is_request, cache_lengths[None, :], 0), axis=1)
    valid = jnp.where(page_live, jnp.clip(page_length - page_number * page_size, 0, page_size), 0)
    mask = (page_row // row_count) ^ me
    count = deep // 2
    slots = mask % across * deep + mask // across
    slots = slots * row_count + page_row % row_count

    query, normalized, cosine, sine = project_queries(
        me, request_slot, cache_lengths, token_inputs, attn_gain, w_query, kv_local, head_dim
    )
    near = [query] + [swap(query, "seq", across * k) for k in range(1, count)]
    far = [swap(query, "seq", across * k) for k in range(count, deep)]
    shared = jnp.concatenate(near + far, axis=0)
    queries = [shared] + [swap(shared, "seq", k) for k in range(1, across)]
    normalized, shared = lax.optimization_barrier((normalized, shared))
    recent = recent_part(
        normalized, cosine, sine, query, key_projection, value_projection, kv_local, head_dim
    )
    near_parts, far_parts = attend_pages(queries, key_cache, paged_value_cache, slots, valid, count, pairs, recent)

    def merge_x(parts):
        return merge_parts([parts[0]] + [swap(parts[k], "seq", k) for k in range(1, across)])

    far_parts = merge_x(far_parts)
    layers = [swap(far_parts[k], "seq", across * (count + k)) for k in range(deep - count)]
    near_parts = merge_x(near_parts)
    layers = layers + [near_parts[0]] + [swap(near_parts[k], "seq", across * k) for k in range(1, count)]
    layers.append(recent)
    own_input = lax.dynamic_slice_in_dim(token_inputs.reshape(rows, width), part * quarter, quarter, 1)
    own_term, terms = project_out(part, layers, own_input, w_output, tp, kv_local)
    total = own_term
    for slot in range(1, tp):
        total = total + swap(terms[slot - 1], "tp", slot).astype(f32)
    own_attended = total.astype(bf16)

    half = (quarter + 255) // 256 * 128
    def along_x(value):
        return [value] + [swap(value, "seq", k) for k in range(1, across)]

    def along_y(value):
        return [value] + [swap(value, "tp", CORES * k) for k in range(1, ways)]

    def spread_first(group):
        first, second = group[:, :half], group[:, half:]
        return along_x(first), along_y(second)

    def spread_second(first, second):
        return along_y(jnp.concatenate(first, axis=0)) + along_x(jnp.stack(second))

    far = [swap(own_attended, "seq", across * k) for k in range(count, deep)]
    near = [own_attended] + [swap(own_attended, "seq", across * k) for k in range(1, count)]
    near = spread_first(jnp.concatenate(near, axis=0))
    near, far = lax.optimization_barrier((near, far))
    near = spread_second(*near)
    far = spread_second(*spread_first(jnp.concatenate(far, axis=0)))
    both = join_groups(near, far, ways)
    other = swap(both, "tp", 1)
    all_rows = both.shape[1]

    gains = mlp_gain.reshape(tp, 1, quarter)
    sums = gate_up_half(part, 0, both, gains, w_gate, w_up)
    activation, other_terms = gate_up_rest(part, other, gains, w_gate, w_up, w_down, sums, width)
    received = swap(other_terms, "tp", 1)
    own_terms = down_half(part, activation, w_down, ways)
    far, near = sum_terms(part, own_terms, received)
    attended = assemble(part, rows, [both, other]).reshape(steps, row_count, width)

    def add(first, others):
        value = first.astype(f32)
        for one in others:
            value = value + one.astype(f32)
        return value

    def collect_group(pieces):
        total = add(pieces[0], [cross(pieces[k], False, k) for k in range(1, across)]).astype(bf16)
        total = total.reshape(across, -1, quarter)
        total = add(total[0], [cross(total[k], True, k) for k in range(1, across)]).astype(bf16)
        return total.reshape(-1, rows, quarter)

    far = collect_group(far)
    near = collect_group(near)
    far = [swap(far[k], "seq", across * (count + k)) for k in range(deep - count)]
    near = [near[0]] + [swap(near[k], "seq", across * k) for k in range(1, count)]
    mlp_result = add(near[0], near[1:] + far)
    own_out = (own_attended.astype(f32) + mlp_result).astype(bf16)
    pieces = [own_out] + [swap(own_out, "tp", slot) for slot in range(1, tp)]
    layer_out = assemble(part, rows, pieces).reshape(steps, row_count, width)
    return attended, layer_out


def solution(mesh):
    in_specs = (
        P(None, "seq", None),
        P(),
        P(None, "tp"),
        P(None, "tp"),
        P(None, "tp"),
        P("tp", None),
        P(),
        P(None, ("seq", "tp")),
        P(None, ("seq", "tp")),
        P(("seq", "tp"), None),
        P("seq", "tp", None, None),
        P("seq", "tp", None, None),
        P(),
        P("seq"),
        P("seq"),
        P(),
    )
    out_specs = (P(None, "seq", None), P(None, "seq", None))
    return jax.shard_map(local, mesh=mesh, in_specs=in_specs, out_specs=out_specs, check_vma=False)
```

```python
import functools

import jax
import jax.numpy as jnp
from jax import lax
from jax.experimental import pallas as pl
from jax.experimental.pallas import tpu as pltpu
from jax.sharding import PartitionSpec as P

STEPS = 4
CORES = 2

rope_theta = 100000000.0
norm_eps = 1e-05
masked_low = -1e30
f32 = jnp.float32
bf16 = jnp.bfloat16


def split_axis(size):
    fast = 1
    while fast * fast * 4 <= size:
        fast *= 2
    return size // fast, fast


def swap(value, axis, mask):
    size = lax.axis_size(axis)
    return lax.ppermute(value, axis, [(i, i ^ mask) for i in range(size)])


def cross(value, x_first, k):
    seq, tp = lax.axis_size("seq"), lax.axis_size("tp")
    pairs = []
    for s in range(seq):
        for t in range(tp):
            along_x = (t % CORES == 0) == x_first
            partner = (s ^ k) * tp + t if along_x else s * tp + (t ^ (CORES * k))
            pairs.append((s * tp + t, partner))
    return lax.ppermute(value, ("seq", "tp"), pairs)


def dot_t(a, b):
    return lax.dot_general(a, b, (((1,), (1,)), ((), ())), preferred_element_type=f32)


def round_trip(value):
    return value.astype(bf16).astype(f32)


def encode_stats(top, total, pairs):
    pieces = []
    rest = top
    for _ in range(3):
        piece = round_trip(rest)
        pieces.append(piece)
        rest = rest - piece
    rest = total
    for _ in range(2):
        piece = round_trip(rest)
        pieces.append(piece)
        rest = rest - piece
    tile = pieces[0]
    for i in range(1, 5):
        tile = tile + pltpu.roll(pieces[i], i * pairs, 1)
    return tile.astype(bf16)


def decode_stats(tile, pairs):
    values = tile.astype(f32)
    lanes = values.shape[1]
    shifted = [values] + [pltpu.roll(values, lanes - i * pairs, 1) for i in range(1, 5)]
    top = shifted[0] + shifted[1] + shifted[2]
    total = shifted[3] + shifted[4]
    return top, total


def softmax_parts(scores, live, scale):
    scores = [jnp.where(keep, score * scale, masked_low) for score, keep in zip(scores, live)]
    tops = [jnp.max(score, axis=1, keepdims=True) for score in scores]
    weights = [jnp.where(keep, jnp.exp(score - top), 0.0) for score, top, keep in zip(scores, tops, live)]
    totals = [jnp.sum(weight, axis=1, keepdims=True) for weight in weights]
    return tops, totals, [weight.astype(bf16) for weight in weights]


def pages_kernel(block_pages, piece_count, near_count, slot_ref, valid_ref, *refs):
    pieces = refs[:piece_count]
    key_buf, value_buf, _ = refs[piece_count : piece_count + 3]
    outs = refs[piece_count + 3 : -4]
    query_ref, top_ref, total_ref, acc_ref = refs[-4:]
    page_count, kv_local, page_size, head_dim = key_buf.shape
    blocks = page_count // block_pages
    pairs = outs[0].shape[1] - 1
    deep = pieces[0].shape[0] // pairs
    rows = query_ref.shape[1]
    scale = head_dim ** (-0.5)

    top_ref[...] = jnp.full(top_ref.shape, masked_low, f32)
    total_ref[...] = jnp.zeros(total_ref.shape, f32)
    acc_ref[...] = jnp.zeros(acc_ref.shape, f32)
    for i, piece in enumerate(pieces):
        query_ref[i * deep * pairs : (i + 1) * deep * pairs] = piece[...]
    lane = lax.broadcasted_iota(jnp.int32, (rows, page_size), 1)

    @pl.loop(0, blocks)
    def _(block):
        pages = [block * block_pages + i for i in range(block_pages)]
        places = [(page, head) for page in pages for head in range(kv_local)]
        at = [slot_ref[page] * kv_local + head for page, head in places]
        live = [lane < valid_ref[page] for page, _ in places]
        scores = [dot_t(query_ref[i], key_buf[page, head]) for i, (page, head) in zip(at, places)]
        tops, totals, weights = softmax_parts(scores, live, scale)
        accs = [
            jnp.dot(weight, value_buf[page, head], preferred_element_type=f32)
            for weight, (page, head) in zip(weights, places)
        ]
        for i, top, total, acc in zip(at, tops, totals, accs):
            old_top = top_ref[i]
            new_top = jnp.maximum(old_top, top)
            old_factor = jnp.exp(old_top - new_top)
            factor = jnp.exp(top - new_top)
            top_ref[i] = new_top
            total_ref[i] = total_ref[i] * old_factor + total * factor
            acc_ref[i] = acc_ref[i] * old_factor + acc * factor

    out_lane = lax.broadcasted_iota(jnp.int32, (rows, head_dim), 1)
    for number, out_ref in enumerate(outs):
        start = number % piece_count * deep + (near_count if number >= piece_count else 0)

        @pl.loop(0, out_ref.shape[0])
        def _(group):
            tops = jnp.zeros((rows, head_dim), f32)
            totals = jnp.zeros((rows, head_dim), f32)
            for i in range(pairs):
                at = (start + group) * pairs + i
                out_ref[group, i] = acc_ref[at].astype(bf16)
                tops = jnp.where(out_lane == i, top_ref[at], tops)
                totals = jnp.where(out_lane == i, total_ref[at], totals)
            out_ref[group, pairs] = encode_stats(tops, totals, pairs)


def attend_pages(pieces, key_cache, value_cache, slots, valid, near_count, pairs, after):
    height, rows, head_dim = pieces[0].shape
    deep = height // pairs
    page_count, kv_local, page_size, _ = key_cache.shape
    block_pages = 6
    while page_count % block_pages:
        block_pages -= 1
    count = height * len(pieces)
    outs = pl.pallas_call(
        functools.partial(pages_kernel, block_pages, len(pieces), near_count),
        out_shape=[
            jax.ShapeDtypeStruct((layers, pairs + 1, rows, head_dim), bf16)
            for layers in (near_count, deep - near_count)
            for _ in pieces
        ],
        in_specs=[smem, smem] + [vmem] * (len(pieces) + 2) + [hbm],
        out_specs=[vmem] * (2 * len(pieces)),
        scratch_shapes=[
            pltpu.VMEM((count, rows, head_dim), bf16),
            pltpu.VMEM((count, rows, head_dim), f32),
            pltpu.VMEM((count, rows, head_dim), f32),
            pltpu.VMEM((count, rows, head_dim), f32),
        ],
        compiler_params=pltpu.CompilerParams(vmem_limit_bytes=14 << 20),
        cost_estimate=pl.CostEstimate(
            flops=4 * rows * page_count * kv_local * page_size * head_dim,
            bytes_accessed=4 * page_count * kv_local * page_size * head_dim,
            transcendentals=0,
        ),
        name="attend_pages",
    )(slots, valid, *pieces, key_cache, value_cache, after)
    return outs[: len(pieces)], outs[len(pieces) :]


def merge_tile(parts, group, pairs):
    stats = [decode_stats(part[group, pairs], pairs) for part in parts]
    top = functools.reduce(jnp.maximum, [s[0] for s in stats])
    factors = [jnp.exp(s[0] - top) for s in stats]
    total = functools.reduce(jnp.add, [s[1] * f for s, f in zip(stats, factors)])
    return top, total, factors


def merge_pair(parts, factors, group, i):
    return functools.reduce(
        jnp.add, [part[group, i].astype(f32) * f[:, i : i + 1] for part, f in zip(parts, factors)]
    )


def merge_kernel(count, *refs):
    parts, outs = refs[:count], refs[count:]
    _, tiles, rows, head_dim = parts[0].shape
    pairs = tiles - 1
    used = lax.broadcasted_iota(jnp.int32, (rows, head_dim), 1) < pairs
    for group, out_ref in enumerate(outs):
        top, total, factors = merge_tile(parts, group, pairs)
        for i in range(pairs):
            out_ref[0, i] = merge_pair(parts, factors, group, i).astype(bf16)
        out_ref[0, pairs] = encode_stats(jnp.where(used, top, 0.0), jnp.where(used, total, 0.0), pairs)


vmem = pl.BlockSpec(memory_space=pltpu.VMEM)
smem = pl.BlockSpec(memory_space=pltpu.SMEM)
hbm = pl.BlockSpec(memory_space=pl.ANY)


def merge_parts(parts):
    groups, *tile = parts[0].shape
    return pl.pallas_call(
        functools.partial(merge_kernel, len(parts)),
        out_shape=[jax.ShapeDtypeStruct((1, *tile), bf16)] * groups,
        in_specs=[vmem] * len(parts),
        out_specs=[vmem] * groups,
        compiler_params=pltpu.CompilerParams(vmem_limit_bytes=8 << 20),
        name="merge_parts",
    )(*parts)


def columns_of(ref, index, size):
    return ref[:, pl.ds(pl.multiple_of(index * size, size), size)]


def rows_of(ref, index, size):
    return ref[pl.ds(pl.multiple_of(index * size, size), size), :]


def start_all(copies):
    for copy in copies:
        copy.start()


def load_kernel(slots, by_rows, part_ref, source_ref, out_ref, sems):
    size = out_ref.shape[1] if by_rows else out_ref.shape[2]
    copies = []
    for i, slot in enumerate(slots):
        at = pl.ds(pl.multiple_of((part_ref[0] ^ slot) * size, size), size)
        source = source_ref.at[at] if by_rows else source_ref.at[:, at]
        copies.append(pltpu.make_async_copy(source, out_ref.at[i], sems.at[i]))
    start_all(copies)
    for copy in copies:
        copy.wait()


def load(part, source, slots, size, by_rows, limit):
    rows, columns = source.shape
    block = (size, columns) if by_rows else (rows, size)
    return pl.pallas_call(
        functools.partial(load_kernel, slots, by_rows),
        out_shape=jax.ShapeDtypeStruct((len(slots), *block), bf16),
        in_specs=[smem, hbm],
        out_specs=vmem,
        scratch_shapes=[pltpu.SemaphoreType.DMA((len(slots),))],
        compiler_params=pltpu.CompilerParams(vmem_limit_bytes=limit << 20),
        cost_estimate=pl.CostEstimate(
            flops=0, bytes_accessed=2 * len(slots) * block[0] * block[1], transcendentals=0
        ),
        name="load",
    )(part.reshape(1), source)


def query_kernel(
    kv_local, me_ref, slots_hbm, lengths_hbm, input_hbm, gain_hbm, weight_hbm,
    query_ref, normalized_ref, rotary_ref,
    slots_ref, lengths_ref, input_ref, gain_ref, weight_buf, total_ref, tile_ref, small_sems, sems,
):
    steps, row_count, width = input_ref.shape
    head_dim = rotary_ref.shape[2]
    cosine_ref, sine_ref = rotary_ref.at[0], rotary_ref.at[1]
    small = [
        pltpu.make_async_copy(source, target, small_sems.at[i])
        for i, (source, target) in enumerate(
            (
                (input_hbm, input_ref),
                (gain_hbm, gain_ref),
                (slots_hbm, slots_ref),
                (lengths_hbm, lengths_ref),
            )
        )
    ]
    start_all(small)
    heads = weight_buf.shape[1] // head_dim
    group = heads // kv_local
    chunks = sems.shape[0]
    depth = width // chunks
    copies = []
    for chunk in range(chunks):
        at = pl.ds(chunk * depth, depth)
        copies.append(pltpu.make_async_copy(weight_hbm.at[at], weight_buf.at[at], sems.at[chunk]))
    start_all(copies)

    for copy in small:
        copy.wait()
    gain = gain_ref[...]
    for step in range(0, steps, 2):
        pair = []
        for at in (step, step + 1):
            floats = input_ref[at].astype(f32)
            mean = jnp.mean(floats * floats, axis=1, keepdims=True)
            pair.append(floats * lax.rsqrt(mean + norm_eps) * gain)
        normalized_ref[step * row_count : (step + 2) * row_count] = jnp.concatenate(pair, axis=0).astype(bf16)

    requests = slots_ref.shape[1]
    own = me_ref[0] * row_count + lax.broadcasted_iota(jnp.int32, (row_count, requests), 0)
    length = jnp.sum(jnp.where(slots_ref[...] == own, lengths_ref[...], 0), axis=1, keepdims=True)
    half = head_dim // 2
    lane = lax.broadcasted_iota(jnp.int32, (row_count, head_dim), 1)
    exponent = jnp.where(lane < half, lane, lane - half).astype(f32) * (2.0 / head_dim)
    inverse_freq = rope_theta ** (-exponent)
    for step in range(steps):
        angles = (length + step).astype(f32) * inverse_freq
        sine = jnp.sin(angles)
        cosine_ref[step * row_count : (step + 1) * row_count] = jnp.cos(angles)
        sine_ref[step * row_count : (step + 1) * row_count] = jnp.where(lane < half, -sine, sine)

    for chunk, copy in enumerate(copies):
        copy.wait()
        at = slice(chunk * depth, (chunk + 1) * depth)
        product = jnp.dot(normalized_ref[:, at], weight_buf[at], preferred_element_type=f32)
        total_ref[...] = product if chunk == 0 else total_ref[...] + product

    cosine, sine = cosine_ref[...], sine_ref[...]
    tile_rows = steps * group
    for head in range(heads):
        value = total_ref[:, head * head_dim : (head + 1) * head_dim]
        value = value * cosine + pltpu.roll(value, half, 1) * sine
        for step in range(steps):
            first = head // group * tile_rows + step * group + head % group
            tile_ref[pl.ds(first, row_count, stride=kv_local * tile_rows), :] = value[
                step * row_count : (step + 1) * row_count
            ]
    query_ref[...] = tile_ref[...].reshape(query_ref.shape).astype(bf16)


def project_queries(me, request_slot, cache_lengths, token_inputs, gain, weight, kv_local, head_dim):
    steps, row_count, width = token_inputs.shape
    rows = steps * row_count
    columns = weight.shape[1]
    tile_rows = columns // (kv_local * head_dim) * steps
    pairs = row_count * kv_local
    chunks = 4
    return pl.pallas_call(
        functools.partial(query_kernel, kv_local),
        out_shape=(
            jax.ShapeDtypeStruct((pairs, tile_rows, head_dim), bf16),
            jax.ShapeDtypeStruct((rows, width), bf16),
            jax.ShapeDtypeStruct((2, rows, head_dim), f32),
        ),
        in_specs=[smem] + [hbm] * 5,
        out_specs=(vmem, vmem, vmem),
        scratch_shapes=[
            pltpu.VMEM((1, request_slot.shape[0]), jnp.int32),
            pltpu.VMEM((1, request_slot.shape[0]), jnp.int32),
            pltpu.VMEM(token_inputs.shape, bf16),
            pltpu.VMEM((1, width), f32),
            pltpu.VMEM((width, columns), bf16),
            pltpu.VMEM((rows, columns), f32),
            pltpu.VMEM((pairs * tile_rows, head_dim), f32),
            pltpu.SemaphoreType.DMA((4,)),
            pltpu.SemaphoreType.DMA((chunks,)),
        ],
        compiler_params=pltpu.CompilerParams(vmem_limit_bytes=54 << 20),
        cost_estimate=pl.CostEstimate(
            flops=2 * rows * width * columns, bytes_accessed=2 * width * columns, transcendentals=0
        ),
        name="project_queries",
    )(
        me.reshape(1),
        request_slot.reshape(1, -1),
        cache_lengths.reshape(1, -1),
        token_inputs,
        gain.reshape(1, width),
        weight,
    )


def recent_kernel(
    kv_local, pairs, normalized_ref, rotary_ref, query_ref, key_hbm, value_hbm,
    out_ref, key_buf, value_buf, key_tile, value_tile, sems,
):
    rows, width = normalized_ref.shape
    head_dim = rotary_ref.shape[2]
    row_count = rows // STEPS
    tile_rows = query_ref.shape[1]
    pads = key_tile.shape[0] // pairs
    copies = [
        pltpu.make_async_copy(key_hbm, key_buf, sems.at[0]),
        pltpu.make_async_copy(value_hbm, value_buf, sems.at[1]),
    ]
    start_all(copies)
    key_tile[...] = jnp.zeros(key_tile.shape, f32)
    value_tile[...] = jnp.zeros(value_tile.shape, f32)
    cosine, sine = rotary_ref[0], rotary_ref[1]
    for copy, buf, tile in ((copies[0], key_buf, key_tile), (copies[1], value_buf, value_tile)):
        copy.wait()
        product = jnp.dot(normalized_ref[...], buf[...], preferred_element_type=f32)
        for head in range(kv_local):
            value = product[:, head * head_dim : (head + 1) * head_dim]
            if buf is key_buf:
                value = value * cosine + pltpu.roll(value, head_dim // 2, 1) * sine
            for step in range(STEPS):
                tile[pl.ds(head * pads + step, row_count, stride=kv_local * pads), :] = value[
                    step * row_count : (step + 1) * row_count
                ]
    keys = key_tile[...].reshape(pairs, pads, head_dim).astype(bf16)
    values = value_tile[...].reshape(pairs, pads, head_dim).astype(bf16)
    row_step = lax.broadcasted_iota(jnp.int32, (tile_rows, pads), 0) // (tile_rows // STEPS)
    column = lax.broadcasted_iota(jnp.int32, (tile_rows, pads), 1)
    scores = [dot_t(query_ref[i], keys[i]) for i in range(pairs)]
    tops, totals, weights = softmax_parts(scores, [column <= row_step] * pairs, head_dim ** (-0.5))
    accs = [jnp.dot(weights[i], values[i], preferred_element_type=f32) for i in range(pairs)]
    lane = lax.broadcasted_iota(jnp.int32, (tile_rows, head_dim), 1)
    all_tops = jnp.zeros((tile_rows, head_dim), f32)
    all_totals = jnp.zeros((tile_rows, head_dim), f32)
    for i in range(pairs):
        out_ref[0, i] = accs[i].astype(bf16)
        all_tops = jnp.where(lane == i, tops[i], all_tops)
        all_totals = jnp.where(lane == i, totals[i], all_totals)
    out_ref[0, pairs] = encode_stats(all_tops, all_totals, pairs)


def recent_part(normalized, rotary, queries, key_projection, value_projection, pairs, kv_local):
    rows, width = normalized.shape
    _, tile_rows, head_dim = queries.shape
    pads = 16
    columns = key_projection.shape[1]
    return pl.pallas_call(
        functools.partial(recent_kernel, kv_local, pairs),
        out_shape=jax.ShapeDtypeStruct((1, pairs + 1, tile_rows, head_dim), bf16),
        in_specs=[vmem, vmem, vmem, hbm, hbm],
        out_specs=vmem,
        scratch_shapes=[
            pltpu.VMEM((width, columns), bf16),
            pltpu.VMEM((width, columns), bf16),
            pltpu.VMEM((pairs * pads, head_dim), f32),
            pltpu.VMEM((pairs * pads, head_dim), f32),
            pltpu.SemaphoreType.DMA((2,)),
        ],
        compiler_params=pltpu.CompilerParams(vmem_limit_bytes=53 << 20),
        cost_estimate=pl.CostEstimate(
            flops=4 * rows * width * columns, bytes_accessed=4 * width * columns, transcendentals=0
        ),
        name="recent_part",
    )(normalized, rotary, queries, key_projection, value_projection)


def out_kernel(
    count, kv_local, part_ref, input_ref, weight_hbm, *refs
):
    parts = refs[:count]
    own_ref, term_ref, weight_buf, tile_ref, attention_ref, sems = refs[count:]
    tp = sems.shape[0]
    quarter = own_ref.shape[1]
    part = part_ref[0]
    copies = []
    for slot in range(tp):
        at = pl.multiple_of((part ^ slot) * quarter, quarter)
        copies.append(
            pltpu.make_async_copy(
                weight_hbm.at[:, pl.ds(at, quarter)], weight_buf.at[slot], sems.at[slot]
            )
        )
    order = list(range(1, tp)) + [0]
    start_all([copies[slot] for slot in order])

    _, tiles, tile_rows, head_dim = parts[0].shape
    pairs = tiles - 1
    row_count = pairs // kv_local
    group = tile_rows // STEPS
    _, total, factors = merge_tile(parts, 0, pairs)
    inverse = 1.0 / total
    factors = [f * inverse for f in factors]
    for i in range(pairs):
        acc = merge_pair(parts, factors, 0, i)
        request, head = i // kv_local, i % kv_local
        for row in range(tile_rows):
            step, member = row // group, row % group
            column = (head * group + member) * head_dim
            at = step * row_count + request
            tile_ref[at : at + 1, column : column + head_dim] = acc[row : row + 1]
    attention_ref[...] = tile_ref[...].astype(bf16)
    for slot in order:
        copies[slot].wait()
        product = jnp.dot(attention_ref[...], weight_buf[slot], preferred_element_type=f32)
        if slot == 0:
            own_ref[...] = input_ref[...].astype(f32) + product
        else:
            term_ref[slot - 1] = product.astype(bf16)


def project_out(part, parts, own_input, weight, tp, kv_local):
    rows, quarter = own_input.shape
    depth = weight.shape[0]
    return pl.pallas_call(
        functools.partial(out_kernel, len(parts), kv_local),
        out_shape=(
            jax.ShapeDtypeStruct((rows, quarter), f32),
            jax.ShapeDtypeStruct((tp - 1, rows, quarter), bf16),
        ),
        in_specs=[smem, vmem, hbm] + [vmem] * len(parts),
        out_specs=(vmem, vmem),
        scratch_shapes=[
            pltpu.VMEM((tp, depth, quarter), bf16),
            pltpu.VMEM((rows, depth), f32),
            pltpu.VMEM((rows, depth), bf16),
            pltpu.SemaphoreType.DMA((tp,)),
        ],
        compiler_params=pltpu.CompilerParams(vmem_limit_bytes=50 << 20),
        cost_estimate=pl.CostEstimate(
            flops=2 * rows * weight.size, bytes_accessed=2 * weight.size, transcendentals=0
        ),
        name="project_out",
    )(part.reshape(1), own_input, weight, *parts)


def places(part, count):
    core = part % CORES
    for first in range(count):
        for second in range(count):
            way = jnp.where(core == 0, second, first)
            column = jnp.where(core == 0, first, second)
            yield first, second, way, column


def places(part, count):
    core = part % CORES
    for first in range(count):
        for second in range(count):
            way = jnp.where(core == 0, second, first)
            column = jnp.where(core == 0, first, second)
            yield first, second, way, column


def join_kernel(ways, near_count, *refs):
    out_ref = refs[-1]
    half = refs[0].shape[1]
    row = 0
    for group in range(2):
        pieces = refs[group * near_count : (group + 1) * near_count]
        height = pieces[0].shape[0]
        for way in range(ways):
            out_ref[way, row : row + height, :half] = pieces[way][...]
        at = row
        for piece in pieces[ways:]:
            out_ref[:, at : at + piece.shape[1], half:] = piece[...]
            at += piece.shape[1]
        row += height


def join_groups(near, far, ways):
    pieces = near + far
    columns = pieces[0].shape[1] + pieces[ways].shape[2]
    all_rows = near[0].shape[0] + far[0].shape[0]
    return pl.pallas_call(
        functools.partial(join_kernel, ways, len(near)),
        out_shape=jax.ShapeDtypeStruct((ways, all_rows, columns), bf16),
        in_specs=[vmem] * len(pieces),
        out_specs=vmem,
        compiler_params=pltpu.CompilerParams(vmem_limit_bytes=8 << 20),
        cost_estimate=pl.CostEstimate(
            flops=0, bytes_accessed=4 * ways * all_rows * columns, transcendentals=0
        ),
        name="join_groups",
    )(*pieces)


def gate_up_copies(part, core, ways, quarter, gate_hbm, up_hbm, gate_buf, up_buf, sems):
    copies = []
    for way in range(ways):
        at = pl.multiple_of((part ^ (way * CORES + core)) * quarter, quarter)
        copies.append(
            pltpu.make_async_copy(gate_hbm.at[pl.ds(at, quarter)], gate_buf.at[way], sems.at[0, way])
        )
        copies.append(pltpu.make_async_copy(up_hbm.at[pl.ds(at, quarter)], up_buf.at[way], sems.at[1, way]))
    return copies


def scaled_rows(part, core, way, rows_ref, gain_ref):
    floats = rows_ref[way].astype(f32)
    squares = jnp.sum(floats * floats, axis=1, keepdims=True)
    return (floats * gain_ref[part ^ (way * CORES + core)]).astype(bf16), squares


def gate_up_kernel(
    core, part_ref, rows_ref, gain_ref, gate_hbm, up_hbm, gate_ref, up_ref, square_ref,
    gate_buf, up_buf, scaled_ref, sems,
):
    ways, _, quarter = rows_ref.shape
    part = part_ref[0]
    copies = gate_up_copies(part, core, ways, quarter, gate_hbm, up_hbm, gate_buf, up_buf, sems)
    start_all(copies)
    square = 0.0
    for way in range(ways):
        scaled, squares = scaled_rows(part, core, way, rows_ref, gain_ref)
        scaled_ref[way] = scaled
        square = square + squares
    square_ref[...] = jnp.broadcast_to(square, square_ref.shape)
    for way in range(ways):
        for copy, buf, out in (
            (copies[2 * way], gate_buf, gate_ref),
            (copies[2 * way + 1], up_buf, up_ref),
        ):
            copy.wait()
            product = jnp.dot(scaled_ref[way], buf[way], preferred_element_type=f32)
            out[...] = product if way == 0 else out[...] + product


def gate_up_half(part, core, rows, gains, w_gate, w_up):
    ways, all_rows, quarter = rows.shape
    hidden = w_gate.shape[1]
    return pl.pallas_call(
        functools.partial(gate_up_kernel, core),
        out_shape=(
            jax.ShapeDtypeStruct((all_rows, hidden), f32),
            jax.ShapeDtypeStruct((all_rows, hidden), f32),
            jax.ShapeDtypeStruct((all_rows, 128), f32),
        ),
        in_specs=[smem, vmem, vmem, hbm, hbm],
        out_specs=(vmem, vmem, vmem),
        scratch_shapes=[
            pltpu.VMEM((ways, quarter, hidden), bf16),
            pltpu.VMEM((ways, quarter, hidden), bf16),
            pltpu.VMEM(rows.shape, bf16),
            pltpu.SemaphoreType.DMA((2, ways)),
        ],
        compiler_params=pltpu.CompilerParams(vmem_limit_bytes=46 << 20),
        cost_estimate=pl.CostEstimate(
            flops=4 * rows.size * hidden,
            bytes_accessed=4 * ways * quarter * hidden + 8 * all_rows * hidden,
            transcendentals=0,
        ),
        name="gate_up_half",
    )(part.reshape(1), rows, gains, w_gate, w_up)


def down_copies(part, core, ways, quarter, down_hbm, down_buf, sems):
    copies = []
    for way in range(ways):
        at = pl.multiple_of((part ^ (way * CORES + core)) * quarter, quarter)
        copies.append(
            pltpu.make_async_copy(down_hbm.at[:, pl.ds(at, quarter)], down_buf.at[way], sems.at[way])
        )
    return copies


def rest_kernel(
    width, part_ref, rows_ref, gain_ref, old_gate_ref, old_up_ref, square_ref, gate_hbm, up_hbm, down_hbm,
    activation_ref, term_ref, gate_buf, up_buf, down_buf, scaled_ref, gate_ref, up_ref, sems, down_sems,
):
    ways, _, quarter = rows_ref.shape
    part = part_ref[0]
    copies = gate_up_copies(part, 1, ways, quarter, gate_hbm, up_hbm, gate_buf, up_buf, sems)
    later = down_copies(part, 1, ways, quarter, down_hbm, down_buf, down_sems)
    start_all(copies + later)
    square = square_ref[:, :1]
    for way in range(ways):
        scaled, squares = scaled_rows(part, 1, way, rows_ref, gain_ref)
        scaled_ref[way] = scaled
        square = square + squares
    factor = lax.rsqrt(square * (1.0 / width) + norm_eps)
    for way in range(ways):
        for copy, buf, old, out in (
            (copies[2 * way], gate_buf, old_gate_ref, gate_ref),
            (copies[2 * way + 1], up_buf, old_up_ref, up_ref),
        ):
            copy.wait()
            product = jnp.dot(scaled_ref[way], buf[way], preferred_element_type=f32)
            out[...] = (old if way == 0 else out)[...] + product
    gate = gate_ref[...] * factor
    up = up_ref[...] * factor
    activation_ref[...] = (gate / (1.0 + jnp.exp(-gate)) * up).astype(bf16)
    for way in range(ways):
        later[way].wait()
        product = jnp.dot(activation_ref[...], down_buf[way], preferred_element_type=f32)
        term_ref[way] = product.astype(bf16)


def gate_up_rest(part, rows, gains, w_gate, w_up, w_down, sums, width):
    ways, all_rows, quarter = rows.shape
    hidden = w_gate.shape[1]
    return pl.pallas_call(
        functools.partial(rest_kernel, width),
        out_shape=(
            jax.ShapeDtypeStruct((all_rows, hidden), bf16),
            jax.ShapeDtypeStruct((ways, all_rows, quarter), bf16),
        ),
        in_specs=[smem, vmem, vmem, vmem, vmem, vmem, hbm, hbm, hbm],
        out_specs=(vmem, vmem),
        scratch_shapes=[
            pltpu.VMEM((ways, quarter, hidden), bf16),
            pltpu.VMEM((ways, quarter, hidden), bf16),
            pltpu.VMEM((ways, hidden, quarter), bf16),
            pltpu.VMEM(rows.shape, bf16),
            pltpu.VMEM((all_rows, hidden), f32),
            pltpu.VMEM((all_rows, hidden), f32),
            pltpu.SemaphoreType.DMA((2, ways)),
            pltpu.SemaphoreType.DMA((ways,)),
        ],
        compiler_params=pltpu.CompilerParams(vmem_limit_bytes=40 << 20),
        cost_estimate=pl.CostEstimate(
            flops=6 * rows.size * hidden, bytes_accessed=6 * ways * quarter * hidden, transcendentals=0
        ),
        name="gate_up_rest",
    )(part.reshape(1), rows, gains, *sums, w_gate, w_up, w_down)


def down_kernel(part_ref, activation_ref, down_hbm, term_ref, down_buf, sems):
    ways, _, quarter = term_ref.shape
    copies = down_copies(part_ref[0], 0, ways, quarter, down_hbm, down_buf, sems)
    start_all(copies)
    for way in range(ways):
        copies[way].wait()
        product = jnp.dot(activation_ref[...], down_buf[way], preferred_element_type=f32)
        term_ref[way] = product.astype(bf16)


def down_half(part, activation, w_down, ways):
    all_rows, hidden = activation.shape
    quarter = w_down.shape[1] // (ways * CORES)
    return pl.pallas_call(
        down_kernel,
        out_shape=jax.ShapeDtypeStruct((ways, all_rows, quarter), bf16),
        in_specs=[smem, vmem, hbm],
        out_specs=vmem,
        scratch_shapes=[
            pltpu.VMEM((ways, hidden, quarter), bf16),
            pltpu.SemaphoreType.DMA((ways,)),
        ],
        compiler_params=pltpu.CompilerParams(vmem_limit_bytes=48 << 20),
        cost_estimate=pl.CostEstimate(
            flops=w_down.size * all_rows, bytes_accessed=w_down.size, transcendentals=0
        ),
        name="down_half",
    )(part.reshape(1), activation, w_down)


def sum_kernel(part_ref, own_ref, other_ref, *out_refs):
    count, all_rows, _ = own_ref.shape
    height = all_rows // 2
    step = height // count
    for group, row in enumerate((height, 0)):
        outs = out_refs[group * count : (group + 1) * count]
        for second, first, way, column in places(part_ref[0], count):
            at = pl.ds(pl.multiple_of(row + column * step, 16), step)
            total = own_ref[way, at, :].astype(f32) + other_ref[way, at, :].astype(f32)
            outs[first][second * step : (second + 1) * step, :] = total.astype(bf16)


def sum_terms(part, own, other):
    count, all_rows, columns = own.shape
    outs = pl.pallas_call(
        sum_kernel,
        out_shape=[jax.ShapeDtypeStruct((all_rows // 2, columns), bf16)] * (2 * count),
        in_specs=[smem, vmem, vmem],
        out_specs=[vmem] * (2 * count),
        compiler_params=pltpu.CompilerParams(vmem_limit_bytes=8 << 20),
        cost_estimate=pl.CostEstimate(flops=own.size, bytes_accessed=6 * own.size, transcendentals=0),
        name="sum_terms",
    )(part.reshape(1), own, other)
    return outs[:count], outs[count:]


def stack_kernel(*refs):
    at = 0
    for ref in refs[:-1]:
        refs[-1][at : at + ref.shape[0]] = ref[...]
        at += ref.shape[0]


def stack_rows(pieces, weight):
    height = sum(piece.shape[0] for piece in pieces)
    return pl.pallas_call(
        stack_kernel,
        out_shape=jax.ShapeDtypeStruct((height, *pieces[0].shape[1:]), bf16),
        in_specs=[vmem] * len(pieces),
        out_specs=vmem,
        compiler_params=pltpu.CompilerParams(vmem_limit_bytes=8 << 20),
        cost_estimate=pl.CostEstimate(flops=0, bytes_accessed=weight << 20, transcendentals=0),
        name="stack_rows",
    )(*pieces)


def total_kernel(*refs):
    total = refs[0][...].astype(f32)
    for ref in refs[1:-1]:
        total = total + ref[...].astype(f32)
    refs[-1][...] = total


def total_of(pieces, weight):
    return pl.pallas_call(
        total_kernel,
        out_shape=jax.ShapeDtypeStruct(pieces[0].shape, f32),
        in_specs=[vmem] * len(pieces),
        out_specs=vmem,
        compiler_params=pltpu.CompilerParams(vmem_limit_bytes=8 << 20),
        cost_estimate=pl.CostEstimate(flops=0, bytes_accessed=weight << 20, transcendentals=0),
        name="total_of",
    )(*pieces)


def assemble_kernel(part_ref, *refs):
    out_ref = refs[-1]
    height = out_ref.shape[0]
    if len(refs[0].shape) == 3:
        pieces = [ref.at[way] for way in range(refs[0].shape[0]) for ref in refs[:-1]]
    else:
        pieces = refs[:-1]
    quarter = pieces[0].shape[1]
    for slot, piece in enumerate(pieces):
        at = pl.multiple_of((part_ref[0] ^ slot) * quarter, quarter)
        out_ref[:, pl.ds(at, quarter)] = piece[:height, :]


def assemble(part, height, pieces):
    shares = sum(piece.shape[0] if piece.ndim == 3 else 1 for piece in pieces)
    return pl.pallas_call(
        assemble_kernel,
        out_shape=jax.ShapeDtypeStruct((height, shares * pieces[0].shape[-1]), bf16),
        in_specs=[smem] + [vmem] * len(pieces),
        out_specs=vmem,
        compiler_params=pltpu.CompilerParams(vmem_limit_bytes=8 << 20),
        name="assemble",
    )(part.reshape(1), *pieces)


def local(
    token_inputs,
    attn_gain,
    w_query,
    key_projection,
    value_projection,
    w_output,
    mlp_gain,
    w_gate,
    w_up,
    w_down,
    key_cache,
    paged_value_cache,
    cache_lengths,
    page_request,
    page_number,
    request_slot,
):
    steps, row_count, width = token_inputs.shape
    seq, tp = lax.axis_size("seq"), lax.axis_size("tp")
    deep, across = split_axis(seq)
    ways, cores = tp // CORES, CORES
    page_count, kv_local, page_size, head_dim = key_cache.shape
    heads_per_group = w_query.shape[1] // (kv_local * head_dim)
    rows = steps * row_count
    pairs = row_count * kv_local
    me, part = lax.axis_index("seq"), lax.axis_index("tp")
    quarter = width // tp

    page_live = page_request >= 0
    request_ids = jnp.arange(request_slot.shape[0], dtype=jnp.int32)
    is_request = request_ids[None, :] == page_request[:, None]
    page_row = jnp.sum(jnp.where(is_request, request_slot[None, :], 0), axis=1)
    page_length = jnp.sum(jnp.where(is_request, cache_lengths[None, :], 0), axis=1)
    valid = jnp.where(page_live, jnp.clip(page_length - page_number * page_size, 0, page_size), 0)
    mask = (page_row // row_count) ^ me
    count = deep // 2
    slots = mask % across * deep + mask // across
    slots = slots * row_count + page_row % row_count

    query, normalized, rotary = project_queries(
        me, request_slot, cache_lengths, token_inputs, attn_gain, w_query, kv_local, head_dim
    )
    near = [query] + [swap(query, "seq", across * k) for k in range(1, count)]
    far = [swap(query, "seq", across * k) for k in range(count, deep)]
    shared = jnp.concatenate(near + far, axis=0)
    queries = [shared] + [swap(shared, "seq", k) for k in range(1, across)]
    recent = recent_part(normalized, rotary, shared, key_projection, value_projection, pairs, kv_local)
    near_parts, far_parts = attend_pages(queries, key_cache, paged_value_cache, slots, valid, count, pairs, recent)

    def merge_x(parts):
        return merge_parts([parts[0]] + [swap(parts[k], "seq", k) for k in range(1, across)])

    far_parts = merge_x(far_parts)
    layers = [swap(far_parts[k], "seq", across * (count + k)) for k in range(deep - count)]
    near_parts = merge_x(near_parts)
    layers = layers + [near_parts[0]] + [swap(near_parts[k], "seq", across * k) for k in range(1, count)]
    layers.append(recent)
    own_input = lax.dynamic_slice_in_dim(token_inputs.reshape(rows, width), part * quarter, quarter, 1)
    own_term, terms = project_out(part, layers, own_input, w_output, tp, kv_local)
    total = own_term
    for slot in range(1, tp):
        total = total + swap(terms[slot - 1], "tp", slot).astype(f32)
    own_attended = total.astype(bf16)

    half = (quarter + 255) // 256 * 128
    def along_x(value):
        return [value] + [swap(value, "seq", k) for k in range(1, across)]

    def along_y(value):
        return [value] + [swap(value, "tp", CORES * k) for k in range(1, ways)]

    def spread_first(group):
        first, second = group[:, :half], group[:, half:]
        return along_x(first), along_y(second)

    def spread_second(first, second):
        return along_y(jnp.concatenate(first, axis=0)) + along_x(jnp.stack(second))

    far = [swap(own_attended, "seq", across * k) for k in range(count, deep)]
    near = [own_attended] + [swap(own_attended, "seq", across * k) for k in range(1, count)]
    near = spread_first(jnp.concatenate(near, axis=0))
    near, far = lax.optimization_barrier((near, far))
    near = spread_second(*near)
    far = spread_second(*spread_first(jnp.concatenate(far, axis=0)))
    both = join_groups(near, far, ways)
    other = swap(both, "tp", 1)
    all_rows = both.shape[1]

    gains = mlp_gain.reshape(tp, 1, quarter)
    sums = gate_up_half(part, 0, both, gains, w_gate, w_up)
    activation, other_terms = gate_up_rest(part, other, gains, w_gate, w_up, w_down, sums, width)
    received = swap(other_terms, "tp", 1)
    own_terms = down_half(part, activation, w_down, ways)
    far, near = sum_terms(part, own_terms, received)
    attended = assemble(part, rows, [both, other]).reshape(steps, row_count, width)

    def add(first, others):
        value = first.astype(f32)
        for one in others:
            value = value + one.astype(f32)
        return value

    def collect_group(pieces):
        total = add(pieces[0], [cross(pieces[k], False, k) for k in range(1, across)]).astype(bf16)
        total = total.reshape(across, -1, quarter)
        total = add(total[0], [cross(total[k], True, k) for k in range(1, across)]).astype(bf16)
        return total.reshape(-1, rows, quarter)

    far = collect_group(far)
    near = collect_group(near)
    far = [swap(far[k], "seq", across * (count + k)) for k in range(deep - count)]
    near = [near[0]] + [swap(near[k], "seq", across * k) for k in range(1, count)]
    mlp_result = add(near[0], near[1:] + [total_of(far, 40)])
    own_out = (own_attended.astype(f32) + mlp_result).astype(bf16)
    pieces = [own_out] + [swap(own_out, "tp", slot) for slot in range(1, tp)]
    layer_out = assemble(part, rows, pieces).reshape(steps, row_count, width)
    return attended, layer_out


def solution(mesh):
    in_specs = (
        P(None, "seq", None),
        P(),
        P(None, "tp"),
        P(None, "tp"),
        P(None, "tp"),
        P("tp", None),
        P(),
        P(None, ("seq", "tp")),
        P(None, ("seq", "tp")),
        P(("seq", "tp"), None),
        P("seq", "tp", None, None),
        P("seq", "tp", None, None),
        P(),
        P("seq"),
        P("seq"),
        P(),
    )
    out_specs = (P(None, "seq", None), P(None, "seq", None))
    return jax.shard_map(local, mesh=mesh, in_specs=in_specs, out_specs=out_specs, check_vma=False)
```

```python
import functools

import jax
import jax.numpy as jnp
from jax import lax
from jax.experimental import pallas as pl
from jax.experimental.pallas import tpu as pltpu
from jax.sharding import PartitionSpec as P

STEPS = 4
CORES = 2

rope_theta = 100000000.0
norm_eps = 1e-05
masked_low = -1e30
f32 = jnp.float32
bf16 = jnp.bfloat16


def split_axis(size):
    fast = 1
    while fast * fast * 4 <= size:
        fast *= 2
    return size // fast, fast


def swap(value, axis, mask):
    size = lax.axis_size(axis)
    return lax.ppermute(value, axis, [(i, i ^ mask) for i in range(size)])


def cross(value, x_first, k):
    seq, tp = lax.axis_size("seq"), lax.axis_size("tp")
    pairs = []
    for s in range(seq):
        for t in range(tp):
            along_x = (t % CORES == 0) == x_first
            partner = (s ^ k) * tp + t if along_x else s * tp + (t ^ (CORES * k))
            pairs.append((s * tp + t, partner))
    return lax.ppermute(value, ("seq", "tp"), pairs)


def dot_t(a, b):
    return lax.dot_general(a, b, (((1,), (1,)), ((), ())), preferred_element_type=f32)


def round_trip(value):
    return value.astype(bf16).astype(f32)


def encode_stats(top, total, pairs):
    pieces = []
    rest = top
    for _ in range(3):
        piece = round_trip(rest)
        pieces.append(piece)
        rest = rest - piece
    rest = total
    for _ in range(2):
        piece = round_trip(rest)
        pieces.append(piece)
        rest = rest - piece
    tile = pieces[0]
    for i in range(1, 5):
        tile = tile + pltpu.roll(pieces[i], i * pairs, 1)
    return tile.astype(bf16)


def decode_stats(tile, pairs):
    values = tile.astype(f32)
    lanes = values.shape[1]
    shifted = [values] + [pltpu.roll(values, lanes - i * pairs, 1) for i in range(1, 5)]
    top = shifted[0] + shifted[1] + shifted[2]
    total = shifted[3] + shifted[4]
    return top, total


def softmax_parts(scores, live, scale):
    scores = [jnp.where(keep, score * scale, masked_low) for score, keep in zip(scores, live)]
    tops = [jnp.max(score, axis=1, keepdims=True) for score in scores]
    weights = [jnp.where(keep, jnp.exp(score - top), 0.0) for score, top, keep in zip(scores, tops, live)]
    totals = [jnp.sum(weight, axis=1, keepdims=True) for weight in weights]
    return tops, totals, [weight.astype(bf16) for weight in weights]


def pages_kernel(block_pages, piece_count, near_count, slot_ref, valid_ref, *refs):
    pieces = refs[:piece_count]
    key_buf, value_buf, _ = refs[piece_count : piece_count + 3]
    outs = refs[piece_count + 3 : -4]
    query_ref, top_ref, total_ref, acc_ref = refs[-4:]
    page_count, kv_local, page_size, head_dim = key_buf.shape
    blocks = page_count // block_pages
    pairs = outs[0].shape[1] - 1
    deep = pieces[0].shape[0] // pairs
    rows = query_ref.shape[1]
    scale = head_dim ** (-0.5)

    top_ref[...] = jnp.full(top_ref.shape, masked_low, f32)
    total_ref[...] = jnp.zeros(total_ref.shape, f32)
    acc_ref[...] = jnp.zeros(acc_ref.shape, f32)
    for i, piece in enumerate(pieces):
        query_ref[i * deep * pairs : (i + 1) * deep * pairs] = piece[...]
    lane = lax.broadcasted_iota(jnp.int32, (rows, page_size), 1)

    @pl.loop(0, blocks)
    def _(block):
        pages = [block * block_pages + i for i in range(block_pages)]
        places = [(page, head) for page in pages for head in range(kv_local)]
        at = [slot_ref[page] * kv_local + head for page, head in places]
        live = [lane < valid_ref[page] for page, _ in places]
        scores = [dot_t(query_ref[i], key_buf[page, head]) for i, (page, head) in zip(at, places)]
        tops, totals, weights = softmax_parts(scores, live, scale)
        accs = [
            jnp.dot(weight, value_buf[page, head], preferred_element_type=f32)
            for weight, (page, head) in zip(weights, places)
        ]
        for i, top, total, acc in zip(at, tops, totals, accs):
            old_top = top_ref[i]
            new_top = jnp.maximum(old_top, top)
            old_factor = jnp.exp(old_top - new_top)
            factor = jnp.exp(top - new_top)
            top_ref[i] = new_top
            total_ref[i] = total_ref[i] * old_factor + total * factor
            acc_ref[i] = acc_ref[i] * old_factor + acc * factor

    out_lane = lax.broadcasted_iota(jnp.int32, (rows, head_dim), 1)
    for number, out_ref in enumerate(outs):
        start = number % piece_count * deep + (near_count if number >= piece_count else 0)

        @pl.loop(0, out_ref.shape[0])
        def _(group):
            tops = jnp.zeros((rows, head_dim), f32)
            totals = jnp.zeros((rows, head_dim), f32)
            for i in range(pairs):
                at = (start + group) * pairs + i
                out_ref[group, i] = acc_ref[at].astype(bf16)
                tops = jnp.where(out_lane == i, top_ref[at], tops)
                totals = jnp.where(out_lane == i, total_ref[at], totals)
            out_ref[group, pairs] = encode_stats(tops, totals, pairs)


def attend_pages(pieces, key_cache, value_cache, slots, valid, near_count, pairs, after):
    height, rows, head_dim = pieces[0].shape
    deep = height // pairs
    page_count, kv_local, page_size, _ = key_cache.shape
    block_pages = 6
    while page_count % block_pages:
        block_pages -= 1
    count = height * len(pieces)
    outs = pl.pallas_call(
        functools.partial(pages_kernel, block_pages, len(pieces), near_count),
        out_shape=[
            jax.ShapeDtypeStruct((layers, pairs + 1, rows, head_dim), bf16)
            for layers in (near_count, deep - near_count)
            for _ in pieces
        ],
        in_specs=[smem, smem] + [vmem] * (len(pieces) + 2) + [hbm],
        out_specs=[vmem] * (2 * len(pieces)),
        scratch_shapes=[
            pltpu.VMEM((count, rows, head_dim), bf16),
            pltpu.VMEM((count, rows, head_dim), f32),
            pltpu.VMEM((count, rows, head_dim), f32),
            pltpu.VMEM((count, rows, head_dim), f32),
        ],
        compiler_params=pltpu.CompilerParams(vmem_limit_bytes=14 << 20),
        cost_estimate=pl.CostEstimate(
            flops=4 * rows * page_count * kv_local * page_size * head_dim,
            bytes_accessed=4 * page_count * kv_local * page_size * head_dim,
            transcendentals=0,
        ),
        name="attend_pages",
    )(slots, valid, *pieces, key_cache, value_cache, after)
    return outs[: len(pieces)], outs[len(pieces) :]


def merge_tile(parts, group, pairs):
    stats = [decode_stats(part[group, pairs], pairs) for part in parts]
    top = functools.reduce(jnp.maximum, [s[0] for s in stats])
    factors = [jnp.exp(s[0] - top) for s in stats]
    total = functools.reduce(jnp.add, [s[1] * f for s, f in zip(stats, factors)])
    return top, total, factors


def merge_pair(parts, factors, group, i):
    return functools.reduce(
        jnp.add, [part[group, i].astype(f32) * f[:, i : i + 1] for part, f in zip(parts, factors)]
    )


def merge_kernel(count, *refs):
    parts, outs = refs[:count], refs[count:]
    _, tiles, rows, head_dim = parts[0].shape
    pairs = tiles - 1
    used = lax.broadcasted_iota(jnp.int32, (rows, head_dim), 1) < pairs
    for group, out_ref in enumerate(outs):
        top, total, factors = merge_tile(parts, group, pairs)
        for i in range(pairs):
            out_ref[0, i] = merge_pair(parts, factors, group, i).astype(bf16)
        out_ref[0, pairs] = encode_stats(jnp.where(used, top, 0.0), jnp.where(used, total, 0.0), pairs)


vmem = pl.BlockSpec(memory_space=pltpu.VMEM)
smem = pl.BlockSpec(memory_space=pltpu.SMEM)
hbm = pl.BlockSpec(memory_space=pl.ANY)


def merge_parts(parts):
    groups, *tile = parts[0].shape
    return pl.pallas_call(
        functools.partial(merge_kernel, len(parts)),
        out_shape=[jax.ShapeDtypeStruct((1, *tile), bf16)] * groups,
        in_specs=[vmem] * len(parts),
        out_specs=[vmem] * groups,
        compiler_params=pltpu.CompilerParams(vmem_limit_bytes=8 << 20),
        name="merge_parts",
    )(*parts)


def columns_of(ref, index, size):
    return ref[:, pl.ds(pl.multiple_of(index * size, size), size)]


def rows_of(ref, index, size):
    return ref[pl.ds(pl.multiple_of(index * size, size), size), :]


def start_all(copies):
    for copy in copies:
        copy.start()


def load_kernel(slots, part_ref, first_ref, second_ref, first_out, second_out, sems):
    size = first_out.shape[1]
    copies = []
    for number, (source, out) in enumerate(((first_ref, first_out), (second_ref, second_out))):
        for i, slot in enumerate(slots):
            at = pl.ds(pl.multiple_of((part_ref[0] ^ slot) * size, size), size)
            copies.append(pltpu.make_async_copy(source.at[at], out.at[i], sems.at[number, i]))
    start_all(copies)
    for copy in copies:
        copy.wait()


def load(part, first, second, slots, size):
    columns = first.shape[1]
    shape = jax.ShapeDtypeStruct((len(slots), size, columns), bf16)
    return pl.pallas_call(
        functools.partial(load_kernel, slots),
        out_shape=(shape, shape),
        in_specs=[smem, hbm, hbm],
        out_specs=(vmem, vmem),
        scratch_shapes=[pltpu.SemaphoreType.DMA((2, len(slots)))],
        compiler_params=pltpu.CompilerParams(vmem_limit_bytes=34 << 20),
        cost_estimate=pl.CostEstimate(
            flops=0, bytes_accessed=4 * len(slots) * size * columns, transcendentals=0
        ),
        name="load",
    )(part.reshape(1), first, second)


def query_kernel(
    kv_local, me_ref, slots_hbm, lengths_hbm, input_hbm, gain_hbm, weight_hbm,
    query_ref, normalized_ref, rotary_ref,
    slots_ref, lengths_ref, input_ref, gain_ref, weight_buf, total_ref, tile_ref, small_sems, sems,
):
    steps, row_count, width = input_ref.shape
    head_dim = rotary_ref.shape[2]
    cosine_ref, sine_ref = rotary_ref.at[0], rotary_ref.at[1]
    small = [
        pltpu.make_async_copy(source, target, small_sems.at[i])
        for i, (source, target) in enumerate(
            (
                (input_hbm, input_ref),
                (gain_hbm, gain_ref),
                (slots_hbm, slots_ref),
                (lengths_hbm, lengths_ref),
            )
        )
    ]
    start_all(small)
    heads = weight_buf.shape[1] // head_dim
    group = heads // kv_local
    chunks = sems.shape[0]
    depth = width // chunks
    copies = []
    for chunk in range(chunks):
        at = pl.ds(chunk * depth, depth)
        copies.append(pltpu.make_async_copy(weight_hbm.at[at], weight_buf.at[at], sems.at[chunk]))
    start_all(copies)

    for copy in small:
        copy.wait()
    gain = gain_ref[...]
    for step in range(0, steps, 2):
        pair = []
        for at in (step, step + 1):
            floats = input_ref[at].astype(f32)
            mean = jnp.mean(floats * floats, axis=1, keepdims=True)
            pair.append(floats * lax.rsqrt(mean + norm_eps) * gain)
        normalized_ref[step * row_count : (step + 2) * row_count] = jnp.concatenate(pair, axis=0).astype(bf16)

    requests = slots_ref.shape[1]
    own = me_ref[0] * row_count + lax.broadcasted_iota(jnp.int32, (row_count, requests), 0)
    length = jnp.sum(jnp.where(slots_ref[...] == own, lengths_ref[...], 0), axis=1, keepdims=True)
    half = head_dim // 2
    lane = lax.broadcasted_iota(jnp.int32, (row_count, head_dim), 1)
    exponent = jnp.where(lane < half, lane, lane - half).astype(f32) * (2.0 / head_dim)
    inverse_freq = rope_theta ** (-exponent)
    for step in range(steps):
        angles = (length + step).astype(f32) * inverse_freq
        sine = jnp.sin(angles)
        cosine_ref[step * row_count : (step + 1) * row_count] = jnp.cos(angles)
        sine_ref[step * row_count : (step + 1) * row_count] = jnp.where(lane < half, -sine, sine)

    for chunk, copy in enumerate(copies):
        copy.wait()
        at = slice(chunk * depth, (chunk + 1) * depth)
        product = jnp.dot(normalized_ref[:, at], weight_buf[at], preferred_element_type=f32)
        total_ref[...] = product if chunk == 0 else total_ref[...] + product

    cosine, sine = cosine_ref[...], sine_ref[...]
    tile_rows = steps * group
    for head in range(heads):
        value = total_ref[:, head * head_dim : (head + 1) * head_dim]
        value = value * cosine + pltpu.roll(value, half, 1) * sine
        for step in range(steps):
            first = head // group * tile_rows + step * group + head % group
            tile_ref[pl.ds(first, row_count, stride=kv_local * tile_rows), :] = value[
                step * row_count : (step + 1) * row_count
            ]
    query_ref[...] = tile_ref[...].reshape(query_ref.shape).astype(bf16)


def project_queries(me, request_slot, cache_lengths, token_inputs, gain, weight, kv_local, head_dim):
    steps, row_count, width = token_inputs.shape
    rows = steps * row_count
    columns = weight.shape[1]
    tile_rows = columns // (kv_local * head_dim) * steps
    pairs = row_count * kv_local
    chunks = 4
    return pl.pallas_call(
        functools.partial(query_kernel, kv_local),
        out_shape=(
            jax.ShapeDtypeStruct((pairs, tile_rows, head_dim), bf16),
            jax.ShapeDtypeStruct((rows, width), bf16),
            jax.ShapeDtypeStruct((2, rows, head_dim), f32),
        ),
        in_specs=[smem] + [hbm] * 5,
        out_specs=(vmem, vmem, vmem),
        scratch_shapes=[
            pltpu.VMEM((1, request_slot.shape[0]), jnp.int32),
            pltpu.VMEM((1, request_slot.shape[0]), jnp.int32),
            pltpu.VMEM(token_inputs.shape, bf16),
            pltpu.VMEM((1, width), f32),
            pltpu.VMEM((width, columns), bf16),
            pltpu.VMEM((rows, columns), f32),
            pltpu.VMEM((pairs * tile_rows, head_dim), f32),
            pltpu.SemaphoreType.DMA((4,)),
            pltpu.SemaphoreType.DMA((chunks,)),
        ],
        compiler_params=pltpu.CompilerParams(vmem_limit_bytes=54 << 20),
        cost_estimate=pl.CostEstimate(
            flops=2 * rows * width * columns, bytes_accessed=2 * width * columns, transcendentals=0
        ),
        name="project_queries",
    )(
        me.reshape(1),
        request_slot.reshape(1, -1),
        cache_lengths.reshape(1, -1),
        token_inputs,
        gain.reshape(1, width),
        weight,
    )


def recent_kernel(
    kv_local, pairs, normalized_ref, rotary_ref, query_ref, key_hbm, value_hbm,
    out_ref, key_buf, value_buf, key_tile, value_tile, sems,
):
    rows, width = normalized_ref.shape
    head_dim = rotary_ref.shape[2]
    row_count = rows // STEPS
    tile_rows = query_ref.shape[1]
    pads = key_tile.shape[0] // pairs
    copies = [
        pltpu.make_async_copy(key_hbm, key_buf, sems.at[0]),
        pltpu.make_async_copy(value_hbm, value_buf, sems.at[1]),
    ]
    start_all(copies)
    key_tile[...] = jnp.zeros(key_tile.shape, f32)
    value_tile[...] = jnp.zeros(value_tile.shape, f32)
    cosine, sine = rotary_ref[0], rotary_ref[1]
    for copy, buf, tile in ((copies[0], key_buf, key_tile), (copies[1], value_buf, value_tile)):
        copy.wait()
        product = jnp.dot(normalized_ref[...], buf[...], preferred_element_type=f32)
        for head in range(kv_local):
            value = product[:, head * head_dim : (head + 1) * head_dim]
            if buf is key_buf:
                value = value * cosine + pltpu.roll(value, head_dim // 2, 1) * sine
            for step in range(STEPS):
                tile[pl.ds(head * pads + step, row_count, stride=kv_local * pads), :] = value[
                    step * row_count : (step + 1) * row_count
                ]
    keys = key_tile[...].reshape(pairs, pads, head_dim).astype(bf16)
    values = value_tile[...].reshape(pairs, pads, head_dim).astype(bf16)
    row_step = lax.broadcasted_iota(jnp.int32, (tile_rows, pads), 0) // (tile_rows // STEPS)
    column = lax.broadcasted_iota(jnp.int32, (tile_rows, pads), 1)
    scores = [dot_t(query_ref[i], keys[i]) for i in range(pairs)]
    tops, totals, weights = softmax_parts(scores, [column <= row_step] * pairs, head_dim ** (-0.5))
    accs = [jnp.dot(weights[i], values[i], preferred_element_type=f32) for i in range(pairs)]
    lane = lax.broadcasted_iota(jnp.int32, (tile_rows, head_dim), 1)
    all_tops = jnp.zeros((tile_rows, head_dim), f32)
    all_totals = jnp.zeros((tile_rows, head_dim), f32)
    for i in range(pairs):
        out_ref[0, i] = accs[i].astype(bf16)
        all_tops = jnp.where(lane == i, tops[i], all_tops)
        all_totals = jnp.where(lane == i, totals[i], all_totals)
    out_ref[0, pairs] = encode_stats(all_tops, all_totals, pairs)


def recent_part(normalized, rotary, queries, key_projection, value_projection, pairs, kv_local):
    rows, width = normalized.shape
    _, tile_rows, head_dim = queries.shape
    pads = 16
    columns = key_projection.shape[1]
    return pl.pallas_call(
        functools.partial(recent_kernel, kv_local, pairs),
        out_shape=jax.ShapeDtypeStruct((1, pairs + 1, tile_rows, head_dim), bf16),
        in_specs=[vmem, vmem, vmem, hbm, hbm],
        out_specs=vmem,
        scratch_shapes=[
            pltpu.VMEM((width, columns), bf16),
            pltpu.VMEM((width, columns), bf16),
            pltpu.VMEM((pairs * pads, head_dim), f32),
            pltpu.VMEM((pairs * pads, head_dim), f32),
            pltpu.SemaphoreType.DMA((2,)),
        ],
        compiler_params=pltpu.CompilerParams(vmem_limit_bytes=53 << 20),
        cost_estimate=pl.CostEstimate(
            flops=4 * rows * width * columns, bytes_accessed=4 * width * columns, transcendentals=0
        ),
        name="recent_part",
    )(normalized, rotary, queries, key_projection, value_projection)


def out_kernel(
    count, kv_local, part_ref, input_ref, weight_hbm, *refs
):
    parts = refs[:count]
    own_ref, term_ref, weight_buf, tile_ref, attention_ref, sems = refs[count:]
    tp = sems.shape[0]
    quarter = own_ref.shape[1]
    part = part_ref[0]
    copies = []
    for slot in range(tp):
        at = pl.multiple_of((part ^ slot) * quarter, quarter)
        copies.append(
            pltpu.make_async_copy(
                weight_hbm.at[:, pl.ds(at, quarter)], weight_buf.at[slot], sems.at[slot]
            )
        )
    order = list(range(1, tp)) + [0]
    start_all([copies[slot] for slot in order])

    _, tiles, tile_rows, head_dim = parts[0].shape
    pairs = tiles - 1
    row_count = pairs // kv_local
    group = tile_rows // STEPS
    _, total, factors = merge_tile(parts, 0, pairs)
    inverse = 1.0 / total
    factors = [f * inverse for f in factors]
    for i in range(pairs):
        acc = merge_pair(parts, factors, 0, i)
        request, head = i // kv_local, i % kv_local
        for row in range(tile_rows):
            step, member = row // group, row % group
            column = (head * group + member) * head_dim
            at = step * row_count + request
            tile_ref[at : at + 1, column : column + head_dim] = acc[row : row + 1]
    attention_ref[...] = tile_ref[...].astype(bf16)
    for slot in order:
        copies[slot].wait()
        product = jnp.dot(attention_ref[...], weight_buf[slot], preferred_element_type=f32)
        if slot == 0:
            own_ref[...] = input_ref[...].astype(f32) + product
        else:
            term_ref[slot - 1] = product.astype(bf16)


def project_out(part, parts, own_input, weight, tp, kv_local):
    rows, quarter = own_input.shape
    depth = weight.shape[0]
    return pl.pallas_call(
        functools.partial(out_kernel, len(parts), kv_local),
        out_shape=(
            jax.ShapeDtypeStruct((rows, quarter), f32),
            jax.ShapeDtypeStruct((tp - 1, rows, quarter), bf16),
        ),
        in_specs=[smem, vmem, hbm] + [vmem] * len(parts),
        out_specs=(vmem, vmem),
        scratch_shapes=[
            pltpu.VMEM((tp, depth, quarter), bf16),
            pltpu.VMEM((rows, depth), f32),
            pltpu.VMEM((rows, depth), bf16),
            pltpu.SemaphoreType.DMA((tp,)),
        ],
        compiler_params=pltpu.CompilerParams(vmem_limit_bytes=50 << 20),
        cost_estimate=pl.CostEstimate(
            flops=2 * rows * weight.size, bytes_accessed=2 * weight.size, transcendentals=0
        ),
        name="project_out",
    )(part.reshape(1), own_input, weight, *parts)


def places(part, count):
    core = part % CORES
    for first in range(count):
        for second in range(count):
            way = jnp.where(core == 0, second, first)
            column = jnp.where(core == 0, first, second)
            yield first, second, way, column


def places(part, count):
    core = part % CORES
    for first in range(count):
        for second in range(count):
            way = jnp.where(core == 0, second, first)
            column = jnp.where(core == 0, first, second)
            yield first, second, way, column


def join_kernel(ways, near_count, *refs):
    *refs, _, out_ref = refs
    half = refs[0].shape[1]
    row = 0
    for group in range(2):
        pieces = refs[group * near_count : (group + 1) * near_count]
        height = pieces[0].shape[0]
        for way in range(ways):
            out_ref[way, row : row + height, :half] = pieces[way][...]
        at = row
        for piece in pieces[ways:]:
            out_ref[:, at : at + piece.shape[1], half:] = piece[...]
            at += piece.shape[1]
        row += height


def join_groups(near, far, ways, after):
    pieces = near + far
    columns = pieces[0].shape[1] + pieces[ways].shape[2]
    all_rows = near[0].shape[0] + far[0].shape[0]
    return pl.pallas_call(
        functools.partial(join_kernel, ways, len(near)),
        out_shape=jax.ShapeDtypeStruct((ways, all_rows, columns), bf16),
        in_specs=[vmem] * len(pieces) + [hbm],
        out_specs=vmem,
        compiler_params=pltpu.CompilerParams(vmem_limit_bytes=8 << 20),
        cost_estimate=pl.CostEstimate(
            flops=0, bytes_accessed=4 * ways * all_rows * columns, transcendentals=0
        ),
        name="join_groups",
    )(*pieces, after)


def row_copies(part, core, hbm_ref, buf, sems):
    ways, size = buf.shape[:2]
    copies = []
    for way in range(ways):
        at = pl.ds(pl.multiple_of((part ^ (way * CORES + core)) * size, size), size)
        copies.append(pltpu.make_async_copy(hbm_ref.at[at], buf.at[way], sems.at[way]))
    return copies


def scaled_rows(part, core, way, rows_ref, gain_ref):
    floats = rows_ref[way].astype(f32)
    squares = jnp.sum(floats * floats, axis=1, keepdims=True)
    return (floats * gain_ref[part ^ (way * CORES + core)]).astype(bf16), squares


def gate_up_kernel(
    part_ref, rows_ref, gain_ref, gate_in, up_in, gate_hbm, gate_ref, up_ref, square_ref, next_ref,
    scaled_ref, next_sems,
):
    ways = rows_ref.shape[0]
    part = part_ref[0]
    later = row_copies(part, 1, gate_hbm, next_ref, next_sems)
    start_all(later)
    square = 0.0
    for way in range(ways):
        scaled, squares = scaled_rows(part, 0, way, rows_ref, gain_ref)
        scaled_ref[way] = scaled
        square = square + squares
    square_ref[...] = jnp.broadcast_to(square, square_ref.shape)
    for way in range(ways):
        product = jnp.dot(scaled_ref[way], gate_in[way], preferred_element_type=f32)
        gate_ref[...] = product if way == 0 else gate_ref[...] + product
    for way in range(ways):
        product = jnp.dot(scaled_ref[way], up_in[way], preferred_element_type=f32)
        up_ref[...] = product if way == 0 else up_ref[...] + product
    for copy in later:
        copy.wait()


def gate_up_half(part, rows, gains, gate_first, up_first, w_gate):
    ways, all_rows, quarter = rows.shape
    hidden = w_gate.shape[1]
    return pl.pallas_call(
        gate_up_kernel,
        out_shape=(
            jax.ShapeDtypeStruct((all_rows, hidden), f32),
            jax.ShapeDtypeStruct((all_rows, hidden), f32),
            jax.ShapeDtypeStruct((all_rows, 128), f32),
            jax.ShapeDtypeStruct((ways, quarter, hidden), bf16),
        ),
        in_specs=[smem, vmem, vmem, vmem, vmem, hbm],
        out_specs=(vmem, vmem, vmem, vmem),
        scratch_shapes=[
            pltpu.VMEM(rows.shape, bf16),
            pltpu.SemaphoreType.DMA((ways,)),
        ],
        compiler_params=pltpu.CompilerParams(vmem_limit_bytes=34 << 20),
        cost_estimate=pl.CostEstimate(
            flops=4 * rows.size * hidden,
            bytes_accessed=4 * ways * quarter * hidden + 8 * all_rows * hidden,
            transcendentals=0,
        ),
        name="gate_up_half",
    )(part.reshape(1), rows, gains, gate_first, up_first, w_gate)


def down_copies(part, core, ways, quarter, down_hbm, down_buf, sems):
    copies = []
    for way in range(ways):
        at = pl.multiple_of((part ^ (way * CORES + core)) * quarter, quarter)
        copies.append(
            pltpu.make_async_copy(down_hbm.at[:, pl.ds(at, quarter)], down_buf.at[way], sems.at[way])
        )
    return copies


def rest_kernel(
    width, part_ref, rows_ref, gain_ref, old_gate_ref, old_up_ref, square_ref, gate_buf, up_hbm, down_hbm,
    activation_ref, term_ref, up_buf, down_buf, scaled_ref, gate_ref, up_ref, sems, down_sems,
):
    ways, _, quarter = rows_ref.shape
    part = part_ref[0]
    copies = row_copies(part, 1, up_hbm, up_buf, sems)
    later = down_copies(part, 1, ways, quarter, down_hbm, down_buf, down_sems)
    start_all(copies + later)
    square = square_ref[:, :1]
    for way in range(ways):
        scaled, squares = scaled_rows(part, 1, way, rows_ref, gain_ref)
        scaled_ref[way] = scaled
        square = square + squares
    factor = lax.rsqrt(square * (1.0 / width) + norm_eps)
    for way in range(ways):
        product = jnp.dot(scaled_ref[way], gate_buf[way], preferred_element_type=f32)
        gate_ref[...] = (old_gate_ref if way == 0 else gate_ref)[...] + product
    for way in range(ways):
        copies[way].wait()
        product = jnp.dot(scaled_ref[way], up_buf[way], preferred_element_type=f32)
        up_ref[...] = (old_up_ref if way == 0 else up_ref)[...] + product
    gate = gate_ref[...] * factor
    up = up_ref[...] * factor
    activation_ref[...] = (gate / (1.0 + jnp.exp(-gate)) * up).astype(bf16)
    for way in range(ways):
        later[way].wait()
        product = jnp.dot(activation_ref[...], down_buf[way], preferred_element_type=f32)
        term_ref[way] = product.astype(bf16)


def gate_up_rest(part, rows, gains, w_up, w_down, sums, width):
    ways, all_rows, quarter = rows.shape
    hidden = w_up.shape[1]
    return pl.pallas_call(
        functools.partial(rest_kernel, width),
        out_shape=(
            jax.ShapeDtypeStruct((all_rows, hidden), bf16),
            jax.ShapeDtypeStruct((ways, all_rows, quarter), bf16),
        ),
        in_specs=[smem] + [vmem] * 6 + [hbm, hbm],
        out_specs=(vmem, vmem),
        scratch_shapes=[
            pltpu.VMEM((ways, quarter, hidden), bf16),
            pltpu.VMEM((ways, hidden, quarter), bf16),
            pltpu.VMEM(rows.shape, bf16),
            pltpu.VMEM((all_rows, hidden), f32),
            pltpu.VMEM((all_rows, hidden), f32),
            pltpu.SemaphoreType.DMA((ways,)),
            pltpu.SemaphoreType.DMA((ways,)),
        ],
        compiler_params=pltpu.CompilerParams(vmem_limit_bytes=36 << 20),
        cost_estimate=pl.CostEstimate(
            flops=6 * rows.size * hidden, bytes_accessed=6 * ways * quarter * hidden, transcendentals=0
        ),
        name="gate_up_rest",
    )(part.reshape(1), rows, gains, *sums, w_up, w_down)


def down_kernel(part_ref, activation_ref, down_hbm, term_ref, down_buf, sems):
    ways, _, quarter = term_ref.shape
    copies = down_copies(part_ref[0], 0, ways, quarter, down_hbm, down_buf, sems)
    start_all(copies)
    for way in range(ways):
        copies[way].wait()
        product = jnp.dot(activation_ref[...], down_buf[way], preferred_element_type=f32)
        term_ref[way] = product.astype(bf16)


def down_half(part, activation, w_down, ways):
    all_rows, hidden = activation.shape
    quarter = w_down.shape[1] // (ways * CORES)
    return pl.pallas_call(
        down_kernel,
        out_shape=jax.ShapeDtypeStruct((ways, all_rows, quarter), bf16),
        in_specs=[smem, vmem, hbm],
        out_specs=vmem,
        scratch_shapes=[
            pltpu.VMEM((ways, hidden, quarter), bf16),
            pltpu.SemaphoreType.DMA((ways,)),
        ],
        compiler_params=pltpu.CompilerParams(vmem_limit_bytes=48 << 20),
        cost_estimate=pl.CostEstimate(
            flops=w_down.size * all_rows, bytes_accessed=w_down.size, transcendentals=0
        ),
        name="down_half",
    )(part.reshape(1), activation, w_down)


def sum_kernel(part_ref, own_ref, other_ref, *out_refs):
    count, all_rows, _ = own_ref.shape
    height = all_rows // 2
    step = height // count
    for group, row in enumerate((height, 0)):
        outs = out_refs[group * count : (group + 1) * count]
        for second, first, way, column in places(part_ref[0], count):
            at = pl.ds(pl.multiple_of(row + column * step, 16), step)
            total = own_ref[way, at, :].astype(f32) + other_ref[way, at, :].astype(f32)
            outs[first][second * step : (second + 1) * step, :] = total.astype(bf16)


def sum_terms(part, own, other):
    count, all_rows, columns = own.shape
    outs = pl.pallas_call(
        sum_kernel,
        out_shape=[jax.ShapeDtypeStruct((all_rows // 2, columns), bf16)] * (2 * count),
        in_specs=[smem, vmem, vmem],
        out_specs=[vmem] * (2 * count),
        compiler_params=pltpu.CompilerParams(vmem_limit_bytes=8 << 20),
        cost_estimate=pl.CostEstimate(flops=own.size, bytes_accessed=6 * own.size, transcendentals=0),
        name="sum_terms",
    )(part.reshape(1), own, other)
    return outs[:count], outs[count:]


def stack_kernel(*refs):
    at = 0
    for ref in refs[:-1]:
        refs[-1][at : at + ref.shape[0]] = ref[...]
        at += ref.shape[0]


def stack_rows(pieces, weight):
    height = sum(piece.shape[0] for piece in pieces)
    return pl.pallas_call(
        stack_kernel,
        out_shape=jax.ShapeDtypeStruct((height, *pieces[0].shape[1:]), bf16),
        in_specs=[vmem] * len(pieces),
        out_specs=vmem,
        compiler_params=pltpu.CompilerParams(vmem_limit_bytes=8 << 20),
        cost_estimate=pl.CostEstimate(flops=0, bytes_accessed=weight << 20, transcendentals=0),
        name="stack_rows",
    )(*pieces)


def total_kernel(*refs):
    total = refs[0][...].astype(f32)
    for ref in refs[1:-1]:
        total = total + ref[...].astype(f32)
    refs[-1][...] = total


def total_of(pieces, weight):
    return pl.pallas_call(
        total_kernel,
        out_shape=jax.ShapeDtypeStruct(pieces[0].shape, f32),
        in_specs=[vmem] * len(pieces),
        out_specs=vmem,
        compiler_params=pltpu.CompilerParams(vmem_limit_bytes=8 << 20),
        cost_estimate=pl.CostEstimate(flops=0, bytes_accessed=weight << 20, transcendentals=0),
        name="total_of",
    )(*pieces)


def assemble_kernel(part_ref, *refs):
    out_ref = refs[-1]
    height = out_ref.shape[0]
    if len(refs[0].shape) == 3:
        pieces = [ref.at[way] for way in range(refs[0].shape[0]) for ref in refs[:-1]]
    else:
        pieces = refs[:-1]
    quarter = pieces[0].shape[1]
    for slot, piece in enumerate(pieces):
        at = pl.multiple_of((part_ref[0] ^ slot) * quarter, quarter)
        out_ref[:, pl.ds(at, quarter)] = piece[:height, :]


def assemble(part, height, pieces):
    shares = sum(piece.shape[0] if piece.ndim == 3 else 1 for piece in pieces)
    return pl.pallas_call(
        assemble_kernel,
        out_shape=jax.ShapeDtypeStruct((height, shares * pieces[0].shape[-1]), bf16),
        in_specs=[smem] + [vmem] * len(pieces),
        out_specs=vmem,
        compiler_params=pltpu.CompilerParams(vmem_limit_bytes=8 << 20),
        name="assemble",
    )(part.reshape(1), *pieces)


def local(
    token_inputs,
    attn_gain,
    w_query,
    key_projection,
    value_projection,
    w_output,
    mlp_gain,
    w_gate,
    w_up,
    w_down,
    key_cache,
    paged_value_cache,
    cache_lengths,
    page_request,
    page_number,
    request_slot,
):
    steps, row_count, width = token_inputs.shape
    seq, tp = lax.axis_size("seq"), lax.axis_size("tp")
    deep, across = split_axis(seq)
    ways, cores = tp // CORES, CORES
    page_count, kv_local, page_size, head_dim = key_cache.shape
    heads_per_group = w_query.shape[1] // (kv_local * head_dim)
    rows = steps * row_count
    pairs = row_count * kv_local
    me, part = lax.axis_index("seq"), lax.axis_index("tp")
    quarter = width // tp

    page_live = page_request >= 0
    request_ids = jnp.arange(request_slot.shape[0], dtype=jnp.int32)
    is_request = request_ids[None, :] == page_request[:, None]
    page_row = jnp.sum(jnp.where(is_request, request_slot[None, :], 0), axis=1)
    page_length = jnp.sum(jnp.where(is_request, cache_lengths[None, :], 0), axis=1)
    valid = jnp.where(page_live, jnp.clip(page_length - page_number * page_size, 0, page_size), 0)
    mask = (page_row // row_count) ^ me
    count = deep // 2
    slots = mask % across * deep + mask // across
    slots = slots * row_count + page_row % row_count

    query, normalized, rotary = project_queries(
        me, request_slot, cache_lengths, token_inputs, attn_gain, w_query, kv_local, head_dim
    )
    near = [query] + [swap(query, "seq", across * k) for k in range(1, count)]
    far = [swap(query, "seq", across * k) for k in range(count, deep)]
    shared = jnp.concatenate(near + far, axis=0)
    queries = [shared] + [swap(shared, "seq", k) for k in range(1, across)]
    recent = recent_part(normalized, rotary, shared, key_projection, value_projection, pairs, kv_local)
    near_parts, far_parts = attend_pages(queries, key_cache, paged_value_cache, slots, valid, count, pairs, recent)

    def merge_x(parts):
        return merge_parts([parts[0]] + [swap(parts[k], "seq", k) for k in range(1, across)])

    far_parts = merge_x(far_parts)
    layers = [swap(far_parts[k], "seq", across * (count + k)) for k in range(deep - count)]
    near_parts = merge_x(near_parts)
    layers = layers + [near_parts[0]] + [swap(near_parts[k], "seq", across * k) for k in range(1, count)]
    layers.append(recent)
    own_input = lax.dynamic_slice_in_dim(token_inputs.reshape(rows, width), part * quarter, quarter, 1)
    own_term, terms = project_out(part, layers, own_input, w_output, tp, kv_local)
    same = [own_term] + [terms[CORES * k - 1] for k in range(1, ways)]
    across_cores = jnp.stack([terms[CORES * k] for k in range(ways)])
    arrived = swap(across_cores, "tp", 1)
    sums = [same[k].astype(f32) + arrived[k].astype(f32) for k in range(ways)]
    total = sums[0]
    for k in range(1, ways):
        total = total + swap(sums[k].astype(bf16), "tp", CORES * k).astype(f32)
    own_attended = total.astype(bf16)

    half = (quarter + 255) // 256 * 128
    def along_x(value):
        return [value] + [swap(value, "seq", k) for k in range(1, across)]

    def along_y(value):
        return [value] + [swap(value, "tp", CORES * k) for k in range(1, ways)]

    def spread_first(group):
        first, second = group[:, :half], group[:, half:]
        return along_x(first), along_y(second)

    def spread_second(first, second):
        return along_y(jnp.concatenate(first, axis=0)) + along_x(jnp.stack(second))

    far = [swap(own_attended, "seq", across * k) for k in range(count, deep)]
    near = [own_attended] + [swap(own_attended, "seq", across * k) for k in range(1, count)]
    near = spread_first(jnp.concatenate(near, axis=0))
    near, far = lax.optimization_barrier((near, far))
    near = spread_second(*near)
    far = spread_second(*spread_first(jnp.concatenate(far, axis=0)))
    gate_first, up_first = load(part, w_gate, w_up, tuple(range(0, tp, CORES)), quarter)
    both = join_groups(near, far, ways, gate_first)
    other = swap(both, "tp", 1)
    all_rows = both.shape[1]

    gains = mlp_gain.reshape(tp, 1, quarter)
    sums = gate_up_half(part, both, gains, gate_first, up_first, w_gate)
    activation, other_terms = gate_up_rest(part, other, gains, w_up, w_down, sums, width)
    received = swap(other_terms, "tp", 1)
    own_terms = down_half(part, activation, w_down, ways)
    far, near = sum_terms(part, own_terms, received)
    attended = assemble(part, rows, [both, other]).reshape(steps, row_count, width)

    def add(first, others):
        value = first.astype(f32)
        for one in others:
            value = value + one.astype(f32)
        return value

    def collect_group(pieces):
        total = add(pieces[0], [cross(pieces[k], False, k) for k in range(1, across)]).astype(bf16)
        total = total.reshape(across, -1, quarter)
        total = add(total[0], [cross(total[k], True, k) for k in range(1, across)]).astype(bf16)
        return total.reshape(-1, rows, quarter)

    far = collect_group(far)
    near = collect_group(near)
    far = [swap(far[k], "seq", across * (count + k)) for k in range(deep - count)]
    near = [near[0]] + [swap(near[k], "seq", across * k) for k in range(1, count)]
    mlp_result = add(near[0], near[1:] + [total_of(far, 40)])
    own_out = (own_attended.astype(f32) + mlp_result).astype(bf16)
    along = jnp.stack([own_out] + [swap(own_out, "tp", CORES * k) for k in range(1, ways)])
    beside = swap(along, "tp", 1)
    pieces = [along, beside]
    layer_out = assemble(part, rows, pieces).reshape(steps, row_count, width)
    return attended, layer_out


def solution(mesh):
    in_specs = (
        P(None, "seq", None),
        P(),
        P(None, "tp"),
        P(None, "tp"),
        P(None, "tp"),
        P("tp", None),
        P(),
        P(None, ("seq", "tp")),
        P(None, ("seq", "tp")),
        P(("seq", "tp"), None),
        P("seq", "tp", None, None),
        P("seq", "tp", None, None),
        P(),
        P("seq"),
        P("seq"),
        P(),
    )
    out_specs = (P(None, "seq", None), P(None, "seq", None))
    return jax.shard_map(local, mesh=mesh, in_specs=in_specs, out_specs=out_specs, check_vma=False)
```

```python
import functools

import jax
import jax.numpy as jnp
from jax import lax
from jax.experimental import pallas as pl
from jax.experimental.pallas import tpu as pltpu
from jax.sharding import PartitionSpec as P

STEPS = 4
CORES = 2

rope_theta = 100000000.0
norm_eps = 1e-05
masked_low = -1e30
f32 = jnp.float32
bf16 = jnp.bfloat16


def split_axis(size):
    fast = 1
    while fast * fast * 4 <= size:
        fast *= 2
    return size // fast, fast


def swap(value, axis, mask):
    size = lax.axis_size(axis)
    return lax.ppermute(value, axis, [(i, i ^ mask) for i in range(size)])


def cross(value, x_first, k):
    seq, tp = lax.axis_size("seq"), lax.axis_size("tp")
    pairs = []
    for s in range(seq):
        for t in range(tp):
            along_x = (t % CORES == 0) == x_first
            partner = (s ^ k) * tp + t if along_x else s * tp + (t ^ (CORES * k))
            pairs.append((s * tp + t, partner))
    return lax.ppermute(value, ("seq", "tp"), pairs)


def dot_t(a, b):
    return lax.dot_general(a, b, (((1,), (1,)), ((), ())), preferred_element_type=f32)


def round_trip(value):
    return value.astype(bf16).astype(f32)


def encode_stats(top, total, pairs):
    pieces = []
    rest = top
    for _ in range(3):
        piece = round_trip(rest)
        pieces.append(piece)
        rest = rest - piece
    rest = total
    for _ in range(2):
        piece = round_trip(rest)
        pieces.append(piece)
        rest = rest - piece
    tile = pieces[0]
    for i in range(1, 5):
        tile = tile + pltpu.roll(pieces[i], i * pairs, 1)
    return tile.astype(bf16)


def decode_stats(tile, pairs):
    values = tile.astype(f32)
    lanes = values.shape[1]
    shifted = [values] + [pltpu.roll(values, lanes - i * pairs, 1) for i in range(1, 5)]
    top = shifted[0] + shifted[1] + shifted[2]
    total = shifted[3] + shifted[4]
    return top, total


def softmax_parts(scores, live, scale):
    scores = [jnp.where(keep, score * scale, masked_low) for score, keep in zip(scores, live)]
    tops = [jnp.max(score, axis=1, keepdims=True) for score in scores]
    weights = [jnp.where(keep, jnp.exp(score - top), 0.0) for score, top, keep in zip(scores, tops, live)]
    totals = [jnp.sum(weight, axis=1, keepdims=True) for weight in weights]
    return tops, totals, [weight.astype(bf16) for weight in weights]


def pages_kernel(block_pages, piece_count, near_count, slot_ref, valid_ref, *refs):
    pieces = refs[:piece_count]
    key_buf, value_buf, _ = refs[piece_count : piece_count + 3]
    outs = refs[piece_count + 3 : -4]
    query_ref, top_ref, total_ref, acc_ref = refs[-4:]
    page_count, kv_local, page_size, head_dim = key_buf.shape
    blocks = page_count // block_pages
    pairs = outs[0].shape[1] - 1
    deep = pieces[0].shape[0] // pairs
    rows = query_ref.shape[1]
    scale = head_dim ** (-0.5)

    top_ref[...] = jnp.full(top_ref.shape, masked_low, f32)
    total_ref[...] = jnp.zeros(total_ref.shape, f32)
    acc_ref[...] = jnp.zeros(acc_ref.shape, f32)
    for i, piece in enumerate(pieces):
        query_ref[i * deep * pairs : (i + 1) * deep * pairs] = piece[...]
    lane = lax.broadcasted_iota(jnp.int32, (rows, page_size), 1)

    @pl.loop(0, blocks)
    def _(block):
        pages = [block * block_pages + i for i in range(block_pages)]
        places = [(page, head) for page in pages for head in range(kv_local)]
        at = [slot_ref[page] * kv_local + head for page, head in places]
        live = [lane < valid_ref[page] for page, _ in places]
        scores = [dot_t(query_ref[i], key_buf[page, head]) for i, (page, head) in zip(at, places)]
        tops, totals, weights = softmax_parts(scores, live, scale)
        accs = [
            jnp.dot(weight, value_buf[page, head], preferred_element_type=f32)
            for weight, (page, head) in zip(weights, places)
        ]
        for i, top, total, acc in zip(at, tops, totals, accs):
            old_top = top_ref[i]
            new_top = jnp.maximum(old_top, top)
            old_factor = jnp.exp(old_top - new_top)
            factor = jnp.exp(top - new_top)
            top_ref[i] = new_top
            total_ref[i] = total_ref[i] * old_factor + total * factor
            acc_ref[i] = acc_ref[i] * old_factor + acc * factor

    out_lane = lax.broadcasted_iota(jnp.int32, (rows, head_dim), 1)
    for number, out_ref in enumerate(outs):
        start = number % piece_count * deep + (near_count if number >= piece_count else 0)

        @pl.loop(0, out_ref.shape[0])
        def _(group):
            tops = jnp.zeros((rows, head_dim), f32)
            totals = jnp.zeros((rows, head_dim), f32)
            for i in range(pairs):
                at = (start + group) * pairs + i
                out_ref[group, i] = acc_ref[at].astype(bf16)
                tops = jnp.where(out_lane == i, top_ref[at], tops)
                totals = jnp.where(out_lane == i, total_ref[at], totals)
            out_ref[group, pairs] = encode_stats(tops, totals, pairs)


def attend_pages(pieces, key_cache, value_cache, slots, valid, near_count, pairs, after):
    height, rows, head_dim = pieces[0].shape
    deep = height // pairs
    page_count, kv_local, page_size, _ = key_cache.shape
    block_pages = 9
    while page_count % block_pages:
        block_pages -= 1
    count = height * len(pieces)
    outs = pl.pallas_call(
        functools.partial(pages_kernel, block_pages, len(pieces), near_count),
        out_shape=[
            jax.ShapeDtypeStruct((layers, pairs + 1, rows, head_dim), bf16)
            for layers in (near_count, deep - near_count)
            for _ in pieces
        ],
        in_specs=[smem, smem] + [vmem] * (len(pieces) + 2) + [hbm],
        out_specs=[vmem] * (2 * len(pieces)),
        scratch_shapes=[
            pltpu.VMEM((count, rows, head_dim), bf16),
            pltpu.VMEM((count, rows, head_dim), f32),
            pltpu.VMEM((count, rows, head_dim), f32),
            pltpu.VMEM((count, rows, head_dim), f32),
        ],
        compiler_params=pltpu.CompilerParams(vmem_limit_bytes=14 << 20),
        cost_estimate=pl.CostEstimate(
            flops=4 * rows * page_count * kv_local * page_size * head_dim,
            bytes_accessed=4 * page_count * kv_local * page_size * head_dim,
            transcendentals=0,
        ),
        name="attend_pages",
    )(slots, valid, *pieces, key_cache, value_cache, after)
    return outs[: len(pieces)], outs[len(pieces) :]


def merge_tile(parts, group, pairs):
    stats = [decode_stats(part[group, pairs], pairs) for part in parts]
    top = functools.reduce(jnp.maximum, [s[0] for s in stats])
    factors = [jnp.exp(s[0] - top) for s in stats]
    total = functools.reduce(jnp.add, [s[1] * f for s, f in zip(stats, factors)])
    return top, total, factors


def merge_pair(parts, factors, group, i):
    return functools.reduce(
        jnp.add, [part[group, i].astype(f32) * f[:, i : i + 1] for part, f in zip(parts, factors)]
    )


def merge_kernel(count, *refs):
    parts, outs = refs[:count], refs[count:]
    _, tiles, rows, head_dim = parts[0].shape
    pairs = tiles - 1
    used = lax.broadcasted_iota(jnp.int32, (rows, head_dim), 1) < pairs
    for group, out_ref in enumerate(outs):
        top, total, factors = merge_tile(parts, group, pairs)
        for i in range(pairs):
            out_ref[0, i] = merge_pair(parts, factors, group, i).astype(bf16)
        out_ref[0, pairs] = encode_stats(jnp.where(used, top, 0.0), jnp.where(used, total, 0.0), pairs)


vmem = pl.BlockSpec(memory_space=pltpu.VMEM)
smem = pl.BlockSpec(memory_space=pltpu.SMEM)
hbm = pl.BlockSpec(memory_space=pl.ANY)


def merge_parts(parts):
    groups, *tile = parts[0].shape
    return pl.pallas_call(
        functools.partial(merge_kernel, len(parts)),
        out_shape=[jax.ShapeDtypeStruct((1, *tile), bf16)] * groups,
        in_specs=[vmem] * len(parts),
        out_specs=[vmem] * groups,
        compiler_params=pltpu.CompilerParams(vmem_limit_bytes=8 << 20),
        name="merge_parts",
    )(*parts)


def columns_of(ref, index, size):
    return ref[:, pl.ds(pl.multiple_of(index * size, size), size)]


def rows_of(ref, index, size):
    return ref[pl.ds(pl.multiple_of(index * size, size), size), :]


def start_all(copies):
    for copy in copies:
        copy.start()


def load_kernel(slots, part_ref, first_ref, second_ref, first_out, second_out, sems):
    size = first_out.shape[1]
    copies = []
    for number, (source, out) in enumerate(((first_ref, first_out), (second_ref, second_out))):
        for i, slot in enumerate(slots):
            at = pl.ds(pl.multiple_of((part_ref[0] ^ slot) * size, size), size)
            copies.append(pltpu.make_async_copy(source.at[at], out.at[i], sems.at[number, i]))
    start_all(copies)
    for copy in copies:
        copy.wait()


def load(part, first, second, slots, size):
    columns = first.shape[1]
    shape = jax.ShapeDtypeStruct((len(slots), size, columns), bf16)
    return pl.pallas_call(
        functools.partial(load_kernel, slots),
        out_shape=(shape, shape),
        in_specs=[smem, hbm, hbm],
        out_specs=(vmem, vmem),
        scratch_shapes=[pltpu.SemaphoreType.DMA((2, len(slots)))],
        compiler_params=pltpu.CompilerParams(vmem_limit_bytes=34 << 20),
        cost_estimate=pl.CostEstimate(
            flops=0, bytes_accessed=4 * len(slots) * size * columns, transcendentals=0
        ),
        name="load",
    )(part.reshape(1), first, second)


def query_kernel(
    kv_local, me_ref, slots_hbm, lengths_hbm, input_hbm, gain_hbm, weight_hbm,
    query_ref, normalized_ref, rotary_ref,
    slots_ref, lengths_ref, input_ref, gain_ref, weight_buf, total_ref, tile_ref, small_sems, sems,
):
    steps, row_count, width = input_ref.shape
    head_dim = rotary_ref.shape[2]
    cosine_ref, sine_ref = rotary_ref.at[0], rotary_ref.at[1]
    small = [
        pltpu.make_async_copy(source, target, small_sems.at[i])
        for i, (source, target) in enumerate(
            (
                (input_hbm, input_ref),
                (gain_hbm, gain_ref),
                (slots_hbm, slots_ref),
                (lengths_hbm, lengths_ref),
            )
        )
    ]
    start_all(small)
    heads = weight_buf.shape[1] // head_dim
    group = heads // kv_local
    chunks = sems.shape[0]
    depth = width // chunks
    copies = []
    for chunk in range(chunks):
        at = pl.ds(chunk * depth, depth)
        copies.append(pltpu.make_async_copy(weight_hbm.at[at], weight_buf.at[at], sems.at[chunk]))
    start_all(copies)

    for copy in small:
        copy.wait()
    gain = gain_ref[...]
    for step in range(0, steps, 2):
        pair = []
        for at in (step, step + 1):
            floats = input_ref[at].astype(f32)
            mean = jnp.mean(floats * floats, axis=1, keepdims=True)
            pair.append(floats * lax.rsqrt(mean + norm_eps) * gain)
        normalized_ref[step * row_count : (step + 2) * row_count] = jnp.concatenate(pair, axis=0).astype(bf16)

    requests = slots_ref.shape[1]
    own = me_ref[0] * row_count + lax.broadcasted_iota(jnp.int32, (row_count, requests), 0)
    length = jnp.sum(jnp.where(slots_ref[...] == own, lengths_ref[...], 0), axis=1, keepdims=True)
    half = head_dim // 2
    lane = lax.broadcasted_iota(jnp.int32, (row_count, head_dim), 1)
    exponent = jnp.where(lane < half, lane, lane - half).astype(f32) * (2.0 / head_dim)
    inverse_freq = rope_theta ** (-exponent)
    for step in range(steps):
        angles = (length + step).astype(f32) * inverse_freq
        sine = jnp.sin(angles)
        cosine_ref[step * row_count : (step + 1) * row_count] = jnp.cos(angles)
        sine_ref[step * row_count : (step + 1) * row_count] = jnp.where(lane < half, -sine, sine)

    for chunk, copy in enumerate(copies):
        copy.wait()
        at = slice(chunk * depth, (chunk + 1) * depth)
        product = jnp.dot(normalized_ref[:, at], weight_buf[at], preferred_element_type=f32)
        total_ref[...] = product if chunk == 0 else total_ref[...] + product

    cosine, sine = cosine_ref[...], sine_ref[...]
    tile_rows = steps * group
    for head in range(heads):
        value = total_ref[:, head * head_dim : (head + 1) * head_dim]
        value = value * cosine + pltpu.roll(value, half, 1) * sine
        for step in range(steps):
            first = head // group * tile_rows + step * group + head % group
            tile_ref[pl.ds(first, row_count, stride=kv_local * tile_rows), :] = value[
                step * row_count : (step + 1) * row_count
            ]
    query_ref[...] = tile_ref[...].reshape(query_ref.shape).astype(bf16)


def project_queries(me, request_slot, cache_lengths, token_inputs, gain, weight, kv_local, head_dim):
    steps, row_count, width = token_inputs.shape
    rows = steps * row_count
    columns = weight.shape[1]
    tile_rows = columns // (kv_local * head_dim) * steps
    pairs = row_count * kv_local
    chunks = 4
    return pl.pallas_call(
        functools.partial(query_kernel, kv_local),
        out_shape=(
            jax.ShapeDtypeStruct((pairs, tile_rows, head_dim), bf16),
            jax.ShapeDtypeStruct((rows, width), bf16),
            jax.ShapeDtypeStruct((2, rows, head_dim), f32),
        ),
        in_specs=[smem] + [hbm] * 5,
        out_specs=(vmem, vmem, vmem),
        scratch_shapes=[
            pltpu.VMEM((1, request_slot.shape[0]), jnp.int32),
            pltpu.VMEM((1, request_slot.shape[0]), jnp.int32),
            pltpu.VMEM(token_inputs.shape, bf16),
            pltpu.VMEM((1, width), f32),
            pltpu.VMEM((width, columns), bf16),
            pltpu.VMEM((rows, columns), f32),
            pltpu.VMEM((pairs * tile_rows, head_dim), f32),
            pltpu.SemaphoreType.DMA((4,)),
            pltpu.SemaphoreType.DMA((chunks,)),
        ],
        compiler_params=pltpu.CompilerParams(vmem_limit_bytes=54 << 20),
        cost_estimate=pl.CostEstimate(
            flops=2 * rows * width * columns, bytes_accessed=2 * width * columns, transcendentals=0
        ),
        name="project_queries",
    )(
        me.reshape(1),
        request_slot.reshape(1, -1),
        cache_lengths.reshape(1, -1),
        token_inputs,
        gain.reshape(1, width),
        weight,
    )


def recent_kernel(
    kv_local, pairs, normalized_ref, rotary_ref, query_ref, key_hbm, value_hbm,
    out_ref, key_buf, value_buf, key_tile, value_tile, sems,
):
    rows, width = normalized_ref.shape
    head_dim = rotary_ref.shape[2]
    row_count = rows // STEPS
    tile_rows = query_ref.shape[1]
    pads = key_tile.shape[0] // pairs
    copies = [
        pltpu.make_async_copy(key_hbm, key_buf, sems.at[0]),
        pltpu.make_async_copy(value_hbm, value_buf, sems.at[1]),
    ]
    start_all(copies)
    key_tile[...] = jnp.zeros(key_tile.shape, f32)
    value_tile[...] = jnp.zeros(value_tile.shape, f32)
    cosine, sine = rotary_ref[0], rotary_ref[1]
    for copy, buf, tile in ((copies[0], key_buf, key_tile), (copies[1], value_buf, value_tile)):
        copy.wait()
        product = jnp.dot(normalized_ref[...], buf[...], preferred_element_type=f32)
        for head in range(kv_local):
            value = product[:, head * head_dim : (head + 1) * head_dim]
            if buf is key_buf:
                value = value * cosine + pltpu.roll(value, head_dim // 2, 1) * sine
            for step in range(STEPS):
                tile[pl.ds(head * pads + step, row_count, stride=kv_local * pads), :] = value[
                    step * row_count : (step + 1) * row_count
                ]
    keys = key_tile[...].reshape(pairs, pads, head_dim).astype(bf16)
    values = value_tile[...].reshape(pairs, pads, head_dim).astype(bf16)
    row_step = lax.broadcasted_iota(jnp.int32, (tile_rows, pads), 0) // (tile_rows // STEPS)
    column = lax.broadcasted_iota(jnp.int32, (tile_rows, pads), 1)
    scores = [dot_t(query_ref[i], keys[i]) for i in range(pairs)]
    tops, totals, weights = softmax_parts(scores, [column <= row_step] * pairs, head_dim ** (-0.5))
    accs = [jnp.dot(weights[i], values[i], preferred_element_type=f32) for i in range(pairs)]
    lane = lax.broadcasted_iota(jnp.int32, (tile_rows, head_dim), 1)
    all_tops = jnp.zeros((tile_rows, head_dim), f32)
    all_totals = jnp.zeros((tile_rows, head_dim), f32)
    for i in range(pairs):
        out_ref[0, i] = accs[i].astype(bf16)
        all_tops = jnp.where(lane == i, tops[i], all_tops)
        all_totals = jnp.where(lane == i, totals[i], all_totals)
    out_ref[0, pairs] = encode_stats(all_tops, all_totals, pairs)


def recent_part(normalized, rotary, queries, key_projection, value_projection, pairs, kv_local):
    rows, width = normalized.shape
    _, tile_rows, head_dim = queries.shape
    pads = 16
    columns = key_projection.shape[1]
    return pl.pallas_call(
        functools.partial(recent_kernel, kv_local, pairs),
        out_shape=jax.ShapeDtypeStruct((1, pairs + 1, tile_rows, head_dim), bf16),
        in_specs=[vmem, vmem, vmem, hbm, hbm],
        out_specs=vmem,
        scratch_shapes=[
            pltpu.VMEM((width, columns), bf16),
            pltpu.VMEM((width, columns), bf16),
            pltpu.VMEM((pairs * pads, head_dim), f32),
            pltpu.VMEM((pairs * pads, head_dim), f32),
            pltpu.SemaphoreType.DMA((2,)),
        ],
        compiler_params=pltpu.CompilerParams(vmem_limit_bytes=53 << 20),
        cost_estimate=pl.CostEstimate(
            flops=4 * rows * width * columns, bytes_accessed=4 * width * columns, transcendentals=0
        ),
        name="recent_part",
    )(normalized, rotary, queries, key_projection, value_projection)


def out_kernel(
    count, kv_local, part_ref, input_ref, weight_hbm, *refs
):
    parts = refs[:count]
    own_ref, term_ref, weight_buf, tile_ref, attention_ref, sems = refs[count:]
    tp = sems.shape[0]
    quarter = own_ref.shape[1]
    part = part_ref[0]
    copies = []
    for slot in range(tp):
        at = pl.multiple_of((part ^ slot) * quarter, quarter)
        copies.append(
            pltpu.make_async_copy(
                weight_hbm.at[:, pl.ds(at, quarter)], weight_buf.at[slot], sems.at[slot]
            )
        )
    order = list(range(1, tp)) + [0]
    start_all([copies[slot] for slot in order])

    _, tiles, tile_rows, head_dim = parts[0].shape
    pairs = tiles - 1
    row_count = pairs // kv_local
    group = tile_rows // STEPS
    _, total, factors = merge_tile(parts, 0, pairs)
    inverse = 1.0 / total
    factors = [f * inverse for f in factors]
    for i in range(pairs):
        acc = merge_pair(parts, factors, 0, i)
        request, head = i // kv_local, i % kv_local
        for row in range(tile_rows):
            step, member = row // group, row % group
            column = (head * group + member) * head_dim
            at = step * row_count + request
            tile_ref[at : at + 1, column : column + head_dim] = acc[row : row + 1]
    attention_ref[...] = tile_ref[...].astype(bf16)
    for slot in order:
        copies[slot].wait()
        product = jnp.dot(attention_ref[...], weight_buf[slot], preferred_element_type=f32)
        if slot == 0:
            own_ref[...] = input_ref[...].astype(f32) + product
        else:
            term_ref[slot - 1] = product.astype(bf16)


def project_out(part, parts, own_input, weight, tp, kv_local):
    rows, quarter = own_input.shape
    depth = weight.shape[0]
    return pl.pallas_call(
        functools.partial(out_kernel, len(parts), kv_local),
        out_shape=(
            jax.ShapeDtypeStruct((rows, quarter), f32),
            jax.ShapeDtypeStruct((tp - 1, rows, quarter), bf16),
        ),
        in_specs=[smem, vmem, hbm] + [vmem] * len(parts),
        out_specs=(vmem, vmem),
        scratch_shapes=[
            pltpu.VMEM((tp, depth, quarter), bf16),
            pltpu.VMEM((rows, depth), f32),
            pltpu.VMEM((rows, depth), bf16),
            pltpu.SemaphoreType.DMA((tp,)),
        ],
        compiler_params=pltpu.CompilerParams(vmem_limit_bytes=50 << 20),
        cost_estimate=pl.CostEstimate(
            flops=2 * rows * weight.size, bytes_accessed=2 * weight.size, transcendentals=0
        ),
        name="project_out",
    )(part.reshape(1), own_input, weight, *parts)


def places(part, count):
    core = part % CORES
    for first in range(count):
        for second in range(count):
            way = jnp.where(core == 0, second, first)
            column = jnp.where(core == 0, first, second)
            yield first, second, way, column


def places(part, count):
    core = part % CORES
    for first in range(count):
        for second in range(count):
            way = jnp.where(core == 0, second, first)
            column = jnp.where(core == 0, first, second)
            yield first, second, way, column


def join_kernel(ways, near_count, *refs):
    *refs, _, out_ref = refs
    half = refs[0].shape[1]
    row = 0
    for group in range(2):
        pieces = refs[group * near_count : (group + 1) * near_count]
        height = pieces[0].shape[0]
        for way in range(ways):
            out_ref[way, row : row + height, :half] = pieces[way][...]
        at = row
        for piece in pieces[ways:]:
            out_ref[:, at : at + piece.shape[1], half:] = piece[...]
            at += piece.shape[1]
        row += height


def join_groups(near, far, ways, after):
    pieces = near + far
    columns = pieces[0].shape[1] + pieces[ways].shape[2]
    all_rows = near[0].shape[0] + far[0].shape[0]
    return pl.pallas_call(
        functools.partial(join_kernel, ways, len(near)),
        out_shape=jax.ShapeDtypeStruct((ways, all_rows, columns), bf16),
        in_specs=[vmem] * len(pieces) + [hbm],
        out_specs=vmem,
        compiler_params=pltpu.CompilerParams(vmem_limit_bytes=8 << 20),
        cost_estimate=pl.CostEstimate(
            flops=0, bytes_accessed=4 * ways * all_rows * columns, transcendentals=0
        ),
        name="join_groups",
    )(*pieces, after)


def row_copies(part, core, hbm_ref, buf, sems):
    ways, size = buf.shape[:2]
    copies = []
    for way in range(ways):
        at = pl.ds(pl.multiple_of((part ^ (way * CORES + core)) * size, size), size)
        copies.append(pltpu.make_async_copy(hbm_ref.at[at], buf.at[way], sems.at[way]))
    return copies


def scaled_rows(part, core, way, rows_ref, gain_ref):
    floats = rows_ref[way].astype(f32)
    squares = jnp.sum(floats * floats, axis=1, keepdims=True)
    return (floats * gain_ref[part ^ (way * CORES + core)]).astype(bf16), squares


def gate_up_kernel(
    part_ref, rows_ref, gain_ref, gate_in, up_in, gate_hbm, gate_ref, up_ref, square_ref, next_ref,
    scaled_ref, next_sems,
):
    ways = rows_ref.shape[0]
    part = part_ref[0]
    later = row_copies(part, 1, gate_hbm, next_ref, next_sems)
    start_all(later)
    square = 0.0
    for way in range(ways):
        scaled, squares = scaled_rows(part, 0, way, rows_ref, gain_ref)
        scaled_ref[way] = scaled
        square = square + squares
    square_ref[...] = jnp.broadcast_to(square, square_ref.shape)
    for way in range(ways):
        product = jnp.dot(scaled_ref[way], gate_in[way], preferred_element_type=f32)
        gate_ref[...] = product if way == 0 else gate_ref[...] + product
    for way in range(ways):
        product = jnp.dot(scaled_ref[way], up_in[way], preferred_element_type=f32)
        up_ref[...] = product if way == 0 else up_ref[...] + product
    for copy in later:
        copy.wait()


def gate_up_half(part, rows, gains, gate_first, up_first, w_gate):
    ways, all_rows, quarter = rows.shape
    hidden = w_gate.shape[1]
    return pl.pallas_call(
        gate_up_kernel,
        out_shape=(
            jax.ShapeDtypeStruct((all_rows, hidden), f32),
            jax.ShapeDtypeStruct((all_rows, hidden), f32),
            jax.ShapeDtypeStruct((all_rows, 128), f32),
            jax.ShapeDtypeStruct((ways, quarter, hidden), bf16),
        ),
        in_specs=[smem, vmem, vmem, vmem, vmem, hbm],
        out_specs=(vmem, vmem, vmem, vmem),
        scratch_shapes=[
            pltpu.VMEM(rows.shape, bf16),
            pltpu.SemaphoreType.DMA((ways,)),
        ],
        compiler_params=pltpu.CompilerParams(vmem_limit_bytes=34 << 20),
        cost_estimate=pl.CostEstimate(
            flops=4 * rows.size * hidden,
            bytes_accessed=4 * ways * quarter * hidden + 8 * all_rows * hidden,
            transcendentals=0,
        ),
        name="gate_up_half",
    )(part.reshape(1), rows, gains, gate_first, up_first, w_gate)


def down_copies(part, core, ways, quarter, down_hbm, down_buf, sems):
    copies = []
    for way in range(ways):
        at = pl.multiple_of((part ^ (way * CORES + core)) * quarter, quarter)
        copies.append(
            pltpu.make_async_copy(down_hbm.at[:, pl.ds(at, quarter)], down_buf.at[way], sems.at[way])
        )
    return copies


def rest_kernel(
    width, part_ref, rows_ref, gain_ref, old_gate_ref, old_up_ref, square_ref, gate_buf, up_hbm, down_hbm,
    activation_ref, term_ref, up_buf, down_buf, scaled_ref, gate_ref, up_ref, sems, down_sems,
):
    ways, _, quarter = rows_ref.shape
    part = part_ref[0]
    copies = row_copies(part, 1, up_hbm, up_buf, sems)
    later = down_copies(part, 1, ways, quarter, down_hbm, down_buf, down_sems)
    start_all(copies + later)
    square = square_ref[:, :1]
    for way in range(ways):
        scaled, squares = scaled_rows(part, 1, way, rows_ref, gain_ref)
        scaled_ref[way] = scaled
        square = square + squares
    factor = lax.rsqrt(square * (1.0 / width) + norm_eps)
    for way in range(ways):
        product = jnp.dot(scaled_ref[way], gate_buf[way], preferred_element_type=f32)
        gate_ref[...] = (old_gate_ref if way == 0 else gate_ref)[...] + product
    for way in range(ways):
        copies[way].wait()
        product = jnp.dot(scaled_ref[way], up_buf[way], preferred_element_type=f32)
        up_ref[...] = (old_up_ref if way == 0 else up_ref)[...] + product
    gate = gate_ref[...] * factor
    up = up_ref[...] * factor
    activation_ref[...] = (gate / (1.0 + jnp.exp(-gate)) * up).astype(bf16)
    for way in range(ways):
        later[way].wait()
        product = jnp.dot(activation_ref[...], down_buf[way], preferred_element_type=f32)
        term_ref[way] = product.astype(bf16)


def gate_up_rest(part, rows, gains, w_up, w_down, sums, width):
    ways, all_rows, quarter = rows.shape
    hidden = w_up.shape[1]
    return pl.pallas_call(
        functools.partial(rest_kernel, width),
        out_shape=(
            jax.ShapeDtypeStruct((all_rows, hidden), bf16),
            jax.ShapeDtypeStruct((ways, all_rows, quarter), bf16),
        ),
        in_specs=[smem] + [vmem] * 6 + [hbm, hbm],
        out_specs=(vmem, vmem),
        scratch_shapes=[
            pltpu.VMEM((ways, quarter, hidden), bf16),
            pltpu.VMEM((ways, hidden, quarter), bf16),
            pltpu.VMEM(rows.shape, bf16),
            pltpu.VMEM((all_rows, hidden), f32),
            pltpu.VMEM((all_rows, hidden), f32),
            pltpu.SemaphoreType.DMA((ways,)),
            pltpu.SemaphoreType.DMA((ways,)),
        ],
        compiler_params=pltpu.CompilerParams(vmem_limit_bytes=36 << 20),
        cost_estimate=pl.CostEstimate(
            flops=6 * rows.size * hidden, bytes_accessed=6 * ways * quarter * hidden, transcendentals=0
        ),
        name="gate_up_rest",
    )(part.reshape(1), rows, gains, *sums, w_up, w_down)


def down_kernel(part_ref, activation_ref, down_hbm, term_ref, down_buf, sems):
    ways, _, quarter = term_ref.shape
    copies = down_copies(part_ref[0], 0, ways, quarter, down_hbm, down_buf, sems)
    start_all(copies)
    for way in range(ways):
        copies[way].wait()
        product = jnp.dot(activation_ref[...], down_buf[way], preferred_element_type=f32)
        term_ref[way] = product.astype(bf16)


def down_half(part, activation, w_down, ways):
    all_rows, hidden = activation.shape
    quarter = w_down.shape[1] // (ways * CORES)
    return pl.pallas_call(
        down_kernel,
        out_shape=jax.ShapeDtypeStruct((ways, all_rows, quarter), bf16),
        in_specs=[smem, vmem, hbm],
        out_specs=vmem,
        scratch_shapes=[
            pltpu.VMEM((ways, hidden, quarter), bf16),
            pltpu.SemaphoreType.DMA((ways,)),
        ],
        compiler_params=pltpu.CompilerParams(vmem_limit_bytes=48 << 20),
        cost_estimate=pl.CostEstimate(
            flops=w_down.size * all_rows, bytes_accessed=w_down.size, transcendentals=0
        ),
        name="down_half",
    )(part.reshape(1), activation, w_down)


def sum_kernel(part_ref, own_ref, other_ref, *out_refs):
    count, all_rows, _ = own_ref.shape
    height = all_rows // 2
    step = height // count
    for group, row in enumerate((height, 0)):
        outs = out_refs[group * count : (group + 1) * count]
        for second, first, way, column in places(part_ref[0], count):
            at = pl.ds(pl.multiple_of(row + column * step, 16), step)
            total = own_ref[way, at, :].astype(f32) + other_ref[way, at, :].astype(f32)
            outs[first][second * step : (second + 1) * step, :] = total.astype(bf16)


def sum_terms(part, own, other):
    count, all_rows, columns = own.shape
    outs = pl.pallas_call(
        sum_kernel,
        out_shape=[jax.ShapeDtypeStruct((all_rows // 2, columns), bf16)] * (2 * count),
        in_specs=[smem, vmem, vmem],
        out_specs=[vmem] * (2 * count),
        compiler_params=pltpu.CompilerParams(vmem_limit_bytes=8 << 20),
        cost_estimate=pl.CostEstimate(flops=own.size, bytes_accessed=6 * own.size, transcendentals=0),
        name="sum_terms",
    )(part.reshape(1), own, other)
    return outs[:count], outs[count:]


def stack_kernel(*refs):
    at = 0
    for ref in refs[:-1]:
        refs[-1][at : at + ref.shape[0]] = ref[...]
        at += ref.shape[0]


def stack_rows(pieces, weight):
    height = sum(piece.shape[0] for piece in pieces)
    return pl.pallas_call(
        stack_kernel,
        out_shape=jax.ShapeDtypeStruct((height, *pieces[0].shape[1:]), bf16),
        in_specs=[vmem] * len(pieces),
        out_specs=vmem,
        compiler_params=pltpu.CompilerParams(vmem_limit_bytes=8 << 20),
        cost_estimate=pl.CostEstimate(flops=0, bytes_accessed=weight << 20, transcendentals=0),
        name="stack_rows",
    )(*pieces)


def total_kernel(*refs):
    total = refs[0][...].astype(f32)
    for ref in refs[1:-1]:
        total = total + ref[...].astype(f32)
    refs[-1][...] = total


def total_of(pieces, weight):
    return pl.pallas_call(
        total_kernel,
        out_shape=jax.ShapeDtypeStruct(pieces[0].shape, f32),
        in_specs=[vmem] * len(pieces),
        out_specs=vmem,
        compiler_params=pltpu.CompilerParams(vmem_limit_bytes=8 << 20),
        cost_estimate=pl.CostEstimate(flops=0, bytes_accessed=weight << 20, transcendentals=0),
        name="total_of",
    )(*pieces)


def assemble_kernel(part_ref, *refs):
    out_ref = refs[-1]
    height = out_ref.shape[0]
    if len(refs[0].shape) == 3:
        pieces = [ref.at[way] for way in range(refs[0].shape[0]) for ref in refs[:-1]]
    else:
        pieces = refs[:-1]
    quarter = pieces[0].shape[1]
    for slot, piece in enumerate(pieces):
        at = pl.multiple_of((part_ref[0] ^ slot) * quarter, quarter)
        out_ref[:, pl.ds(at, quarter)] = piece[:height, :]


def assemble(part, height, pieces):
    shares = sum(piece.shape[0] if piece.ndim == 3 else 1 for piece in pieces)
    return pl.pallas_call(
        assemble_kernel,
        out_shape=jax.ShapeDtypeStruct((height, shares * pieces[0].shape[-1]), bf16),
        in_specs=[smem] + [vmem] * len(pieces),
        out_specs=vmem,
        compiler_params=pltpu.CompilerParams(vmem_limit_bytes=8 << 20),
        name="assemble",
    )(part.reshape(1), *pieces)


def local(
    token_inputs,
    attn_gain,
    w_query,
    key_projection,
    value_projection,
    w_output,
    mlp_gain,
    w_gate,
    w_up,
    w_down,
    key_cache,
    paged_value_cache,
    cache_lengths,
    page_request,
    page_number,
    request_slot,
):
    steps, row_count, width = token_inputs.shape
    seq, tp = lax.axis_size("seq"), lax.axis_size("tp")
    deep, across = split_axis(seq)
    ways, cores = tp // CORES, CORES
    page_count, kv_local, page_size, head_dim = key_cache.shape
    heads_per_group = w_query.shape[1] // (kv_local * head_dim)
    rows = steps * row_count
    pairs = row_count * kv_local
    me, part = lax.axis_index("seq"), lax.axis_index("tp")
    quarter = width // tp

    page_live = page_request >= 0
    request_ids = jnp.arange(request_slot.shape[0], dtype=jnp.int32)
    is_request = request_ids[None, :] == page_request[:, None]
    page_row = jnp.sum(jnp.where(is_request, request_slot[None, :], 0), axis=1)
    page_length = jnp.sum(jnp.where(is_request, cache_lengths[None, :], 0), axis=1)
    valid = jnp.where(page_live, jnp.clip(page_length - page_number * page_size, 0, page_size), 0)
    mask = (page_row // row_count) ^ me
    count = deep // 2
    slots = mask % across * deep + mask // across
    slots = slots * row_count + page_row % row_count

    query, normalized, rotary = project_queries(
        me, request_slot, cache_lengths, token_inputs, attn_gain, w_query, kv_local, head_dim
    )
    near = [query] + [swap(query, "seq", across * k) for k in range(1, count)]
    far = [swap(query, "seq", across * k) for k in range(count, deep)]
    shared = jnp.concatenate(near + far, axis=0)
    queries = [shared] + [swap(shared, "seq", k) for k in range(1, across)]
    recent = recent_part(normalized, rotary, shared, key_projection, value_projection, pairs, kv_local)
    near_parts, far_parts = attend_pages(queries, key_cache, paged_value_cache, slots, valid, count, pairs, recent)

    def merge_x(parts):
        return merge_parts([parts[0]] + [swap(parts[k], "seq", k) for k in range(1, across)])

    far_parts = merge_x(far_parts)
    layers = [swap(far_parts[k], "seq", across * (count + k)) for k in range(deep - count)]
    near_parts = merge_x(near_parts)
    layers = layers + [near_parts[0]] + [swap(near_parts[k], "seq", across * k) for k in range(1, count)]
    layers.append(recent)
    own_input = lax.dynamic_slice_in_dim(token_inputs.reshape(rows, width), part * quarter, quarter, 1)
    own_term, terms = project_out(part, layers, own_input, w_output, tp, kv_local)
    same = [own_term] + [terms[CORES * k - 1] for k in range(1, ways)]
    across_cores = jnp.stack([terms[CORES * k] for k in range(ways)])
    arrived = swap(across_cores, "tp", 1)
    sums = [same[k].astype(f32) + arrived[k].astype(f32) for k in range(ways)]
    total = sums[0]
    for k in range(1, ways):
        total = total + swap(sums[k].astype(bf16), "tp", CORES * k).astype(f32)
    own_attended = total.astype(bf16)

    half = (quarter + 255) // 256 * 128
    def along_x(value):
        return [value] + [swap(value, "seq", k) for k in range(1, across)]

    def along_y(value):
        return [value] + [swap(value, "tp", CORES * k) for k in range(1, ways)]

    def spread_first(group):
        first, second = group[:, :half], group[:, half:]
        return along_x(first), along_y(second)

    def spread_second(first, second):
        return along_y(jnp.concatenate(first, axis=0)) + along_x(jnp.stack(second))

    far = [swap(own_attended, "seq", across * k) for k in range(count, deep)]
    near = [own_attended] + [swap(own_attended, "seq", across * k) for k in range(1, count)]
    near = spread_first(jnp.concatenate(near, axis=0))
    near, far = lax.optimization_barrier((near, far))
    near = spread_second(*near)
    far = spread_second(*spread_first(jnp.concatenate(far, axis=0)))
    gate_first, up_first = load(part, w_gate, w_up, tuple(range(0, tp, CORES)), quarter)
    both = join_groups(near, far, ways, gate_first)
    other = swap(both, "tp", 1)
    all_rows = both.shape[1]

    gains = mlp_gain.reshape(tp, 1, quarter)
    sums = gate_up_half(part, both, gains, gate_first, up_first, w_gate)
    activation, other_terms = gate_up_rest(part, other, gains, w_up, w_down, sums, width)
    received = swap(other_terms, "tp", 1)
    own_terms = down_half(part, activation, w_down, ways)
    far, near = sum_terms(part, own_terms, received)
    attended = assemble(part, rows, [both, other]).reshape(steps, row_count, width)

    def add(first, others):
        value = first.astype(f32)
        for one in others:
            value = value + one.astype(f32)
        return value

    def collect_group(pieces):
        total = add(pieces[0], [cross(pieces[k], False, k) for k in range(1, across)]).astype(bf16)
        total = total.reshape(across, -1, quarter)
        total = add(total[0], [cross(total[k], True, k) for k in range(1, across)]).astype(bf16)
        return total.reshape(-1, rows, quarter)

    far = collect_group(far)
    near = collect_group(near)
    far = [swap(far[k], "seq", across * (count + k)) for k in range(deep - count)]
    near = [near[0]] + [swap(near[k], "seq", across * k) for k in range(1, count)]
    mlp_result = add(near[0], near[1:] + [total_of(far, 40)])
    own_out = (own_attended.astype(f32) + mlp_result).astype(bf16)
    along = jnp.stack([own_out] + [swap(own_out, "tp", CORES * k) for k in range(1, ways)])
    beside = swap(along, "tp", 1)
    pieces = [along, beside]
    layer_out = assemble(part, rows, pieces).reshape(steps, row_count, width)
    return attended, layer_out


def solution(mesh):
    in_specs = (
        P(None, "seq", None),
        P(),
        P(None, "tp"),
        P(None, "tp"),
        P(None, "tp"),
        P("tp", None),
        P(),
        P(None, ("seq", "tp")),
        P(None, ("seq", "tp")),
        P(("seq", "tp"), None),
        P("seq", "tp", None, None),
        P("seq", "tp", None, None),
        P(),
        P("seq"),
        P("seq"),
        P(),
    )
    out_specs = (P(None, "seq", None), P(None, "seq", None))
    return jax.shard_map(local, mesh=mesh, in_specs=in_specs, out_specs=out_specs, check_vma=False)
```
